512 devices in a mesh: dp: 8 (over x, core), seq: 64 (over y, z).
Axes of the slice: x: 4, y: 8, z: 8, core: 2. Of those that a mesh axis runs over, the one named last changes fastest.
Arguments:
- hidden: bfloat16 [8, 8192, 2048], P('dp', 'seq'), may hold values from -7 to 7
- cotangent: bfloat16 [8, 8192, 2048], P('dp', 'seq'), may hold values from -6 to 6
- picks: int32 [8, 8192], P('dp', 'seq'), may hold values from 0 to 1, as said below
- gain: float32 [2048], replicated, may hold values from 0.5 to 1.5
- router: float32 [2048], replicated, may hold values from -0.125 to 0.125
- w_query: bfloat16 [2048, 1024], P('seq'), may hold values from -2 to 2
- w_kv: bfloat16 [2048, 256], P('seq'), may hold values from -2 to 2
- w_out: bfloat16 [1024, 2048], P('seq'), may hold values from -0.1875 to 0.1875
Outputs:
- mixed: bfloat16 [8, 8192, 2048], P('dp', 'seq')
- input_grad: bfloat16 [8, 8192, 2048], P('dp', 'seq')
- kv_grad: float32 [2048, 256], P('seq')
- router_grad: float32 [2048], P('seq')
The draws below stay inside these ranges and needn't reach their ends.
Inputs may be any that keep to these rules, and one draw needn't show every extreme that they name: `picks`: every sequence has exactly 1024 picked tokens; each aligned block of 128 tokens has 0 to 32 of them, and in every sequence some block has exactly 32.
All inputs are finite; a program needn't handle non-finite values.
Results may differ from the reference program's by a relative error of at most 0.013.
The reference program's roundings to bfloat16 on the way count: a program that leaves them out, or rounds other values in their place, can miss the bound.
Values may be sent and summed in bfloat16 or wider, within the bound.
A program may use at most 64 MiB of HBM per device.

```python
import jax
import jax.numpy as jnp
from jax import lax

MODEL_WIDTH = 2048
QUERY_HEADS = 16
KEY_VALUE_HEADS = 2
HEAD_SIZE = 64
TOK_DEV = 128
CAP = 16
LEN = 8192
NSEQ = 8
N_SEQ = 64


def draw_picks(key, part):
    half_count = N_SEQ // 2
    most_picks = 2 * CAP
    key_low, key_pair, key_flip, key_order = jax.random.split(key, 4)
    lower = jax.random.randint(key_low, (NSEQ, half_count), 0, most_picks + 1)
    chosen_pair = jax.random.randint(key_pair, (NSEQ, 1), 0, half_count)
    pair_index = lax.broadcasted_iota(jnp.int32, (NSEQ, half_count), 1)
    lower = jnp.where(pair_index == chosen_pair, most_picks, lower)
    flipped = jax.random.randint(key_flip, (NSEQ, half_count), 0, 2)
    leading = jnp.where(flipped == 1, most_picks - lower, lower)
    counts = jnp.stack([leading, most_picks - leading], axis=2).reshape(NSEQ, N_SEQ)
    order_keys = jax.random.split(key_order, NSEQ * N_SEQ)
    orders = jax.vmap(lambda single: jax.random.permutation(single, TOK_DEV))(order_keys)
    orders = orders.reshape(NSEQ, N_SEQ, TOK_DEV)
    chosen = (orders < counts[:, :, None]).astype(jnp.int32)
    return chosen.reshape(NSEQ, LEN)


def draw_hidden(key, part):
    values = jax.random.truncated_normal(jax.random.fold_in(key, 31), -6.0, 6.0, (NSEQ, LEN, MODEL_WIDTH), jnp.float32)
    return values.astype(jnp.bfloat16)


def draw_w_query(key, part):
    weight_params = jax.random.truncated_normal(jax.random.fold_in(key, 41), -6.0, 6.0, (MODEL_WIDTH, QUERY_HEADS * HEAD_SIZE), jnp.float32) * MODEL_WIDTH ** (-0.5)
    return weight_params.astype(jnp.bfloat16)


def draw_w_kv(key, part):
    weight_params = jax.random.truncated_normal(jax.random.fold_in(key, 43), -6.0, 6.0, (MODEL_WIDTH, 2 * KEY_VALUE_HEADS * HEAD_SIZE), jnp.float32) * MODEL_WIDTH ** (-0.5)
    return weight_params.astype(jnp.bfloat16)


def shard_levels(key, dims, cuts, low, top_value):
    def one(position, parts):
        heights = jax.random.uniform(jax.random.fold_in(jax.random.fold_in(key, 6), position), (parts,), jnp.float32, low / len(cuts), top_value / len(cuts))
        return jnp.repeat(jnp.exp(heights), dims[position] // parts).reshape((-1,) + (1,) * (len(dims) - position - 1))

    factor_of = one(*cuts[0])
    for cut in cuts[1:]:
        factor_of = factor_of * one(*cut)
    return factor_of


def gaussian(stream_key, shape, width, bound, pieces=(), held_as=jnp.bfloat16):
    level = shard_levels(stream_key, shape, pieces, -0.22, 0.18) if pieces else 1.0
    array = jax.random.normal(stream_key, shape, jnp.float32) * width * level
    return jnp.minimum(jnp.maximum(array, -bound), bound).astype(held_as)


def setup_inputs(seed: int = 0) -> dict:
    seeds = jax.random.split(jax.random.key(seed), 9)
    return {
        "hidden": draw_hidden(jax.random.fold_in(seeds[8], 71), 0),
        "cotangent": gaussian(seeds[1], (NSEQ, LEN, MODEL_WIDTH), 1.0, 6.0, ((0, 8), (1, 64))),
        "picks": draw_picks(jax.random.fold_in(seeds[8], 71), 0),
        "gain": jnp.clip(1.0 + 0.1 * jax.random.normal(seeds[3], (MODEL_WIDTH,), jnp.float32), 0.5, 1.5),
        "router": gaussian(seeds[4], (MODEL_WIDTH,), MODEL_WIDTH ** -0.5, 0.125, (), jnp.float32),
        "w_query": draw_w_query(jax.random.fold_in(seeds[8], 71), 0),
        "w_kv": draw_w_kv(jax.random.fold_in(seeds[8], 71), 0),
        "w_out": gaussian(seeds[7], (QUERY_HEADS * HEAD_SIZE, MODEL_WIDTH), (QUERY_HEADS * HEAD_SIZE) ** -0.5, 0.1875, ((0, 64),)),
    }


EPSILON = 1e-05

def dot_transposed(left, right):
    return lax.dot_general(left, right, (((1,), (1,)), ((), ())), preferred_element_type=jnp.float32)

def sequence_pass(hidden_seq, cotangent_seq, pick_seq, gain, router, w_query, w_kv, w_out):
    key_value_width = KEY_VALUE_HEADS * HEAD_SIZE
    query_group_size = QUERY_HEADS // KEY_VALUE_HEADS
    head_scale = HEAD_SIZE ** (-0.5)
    picked_token_count = CAP * N_SEQ
    token_rows = hidden_seq.astype(jnp.float32)
    grad_rows = cotangent_seq.astype(jnp.float32)
    picked_index = jnp.nonzero(pick_seq, size=picked_token_count)[0].astype(jnp.int32)
    gate_prob = jax.nn.sigmoid(jnp.dot(token_rows, router, precision=lax.Precision.HIGHEST))
    block_float = hidden_seq[picked_index].astype(jnp.float32)
    inv_norm = lax.rsqrt(lax.optimization_barrier(jnp.mean(block_float * block_float, axis=1, keepdims=True)) + EPSILON)
    normed = (block_float * inv_norm * gain[None, :]).astype(jnp.bfloat16)
    query_head_rows = jnp.dot(normed, w_query, preferred_element_type=jnp.float32).astype(jnp.bfloat16)
    key_value_pair = jnp.dot(normed, w_kv, preferred_element_type=jnp.float32).astype(jnp.bfloat16)
    key_head_rows = key_value_pair[:, :key_value_width].reshape(picked_token_count, KEY_VALUE_HEADS, HEAD_SIZE).astype(jnp.float32)
    value_head_rows = key_value_pair[:, key_value_width:].reshape(picked_token_count, KEY_VALUE_HEADS, HEAD_SIZE).astype(jnp.float32)
    query_split_parts = query_head_rows.reshape(picked_token_count, KEY_VALUE_HEADS, query_group_size, HEAD_SIZE).astype(jnp.float32)
    ranks = jnp.arange(picked_token_count)
    allowed = (ranks[None, :] <= ranks[:, None])[:, None, None, :]
    scores = jnp.einsum('cgrd,ngd->cgrn', query_split_parts, key_head_rows) * head_scale
    scores = jnp.where(allowed, scores, -jnp.inf)
    score_top = lax.optimization_barrier(jnp.max(scores, axis=3, keepdims=True))
    score_exp = jnp.exp(scores - score_top)
    attn_probs = score_exp / lax.optimization_barrier(jnp.sum(score_exp, axis=3, keepdims=True))
    probs_half = attn_probs.astype(jnp.bfloat16)
    mixed_heads = jnp.einsum('cgrn,ngd->cgrd', probs_half.astype(jnp.float32), value_head_rows)
    mixed_heads = mixed_heads.astype(jnp.bfloat16).reshape(picked_token_count, QUERY_HEADS * HEAD_SIZE)
    block_out = jnp.dot(mixed_heads, w_out, preferred_element_type=jnp.float32).astype(jnp.bfloat16)
    out_tokens = jnp.zeros(token_rows.shape, jnp.float32).at[picked_index].set(block_out.astype(jnp.float32))
    mixed = (token_rows + gate_prob[:, None] * out_tokens).astype(jnp.bfloat16)
    scaled_grad = (gate_prob[:, None] * grad_rows).astype(jnp.bfloat16)
    through = lax.optimization_barrier(jnp.sum(grad_rows * out_tokens, axis=1))
    grad_logit = through * gate_prob * (1.0 - gate_prob)
    router_part = jnp.dot(grad_logit, token_rows, precision=lax.Precision.HIGHEST)
    gradient_heads = dot_transposed(scaled_grad[picked_index], w_out).astype(jnp.bfloat16)
    gradient_split = gradient_heads.reshape(picked_token_count, KEY_VALUE_HEADS, query_group_size, HEAD_SIZE).astype(jnp.float32)
    grad_probs = jnp.einsum('cgrd,ngd->cgrn', gradient_split, value_head_rows)
    inner_sum = lax.optimization_barrier(jnp.sum(attn_probs * grad_probs, axis=3, keepdims=True))
    grad_scores = (attn_probs * (grad_probs - inner_sum)).astype(jnp.bfloat16).astype(jnp.float32)
    grad_query = (jnp.einsum('cgrn,ngd->cgrd', grad_scores, key_head_rows) * head_scale).astype(jnp.bfloat16)
    grad_query = grad_query.reshape(picked_token_count, QUERY_HEADS * HEAD_SIZE)
    grad_keys = jnp.einsum('cgrn,cgrd->ngd', grad_scores, query_split_parts) * head_scale
    grad_values = jnp.einsum('cgrn,cgrd->ngd', probs_half.astype(jnp.float32), gradient_split)
    grad_kv = jnp.concatenate([grad_keys.reshape(picked_token_count, key_value_width), grad_values.reshape(picked_token_count, key_value_width)], axis=1).astype(jnp.bfloat16)
    grad_normed = dot_transposed(grad_query, w_query) + dot_transposed(grad_kv, w_kv)
    upstream = grad_normed * gain[None, :]
    grad_block = inv_norm * upstream - block_float * inv_norm ** 3 * lax.optimization_barrier(jnp.mean(upstream * block_float, axis=1, keepdims=True))
    grad_block = grad_block.astype(jnp.bfloat16)
    kv_part = lax.dot_general(normed, grad_kv, (((0,), (0,)), ((), ())), preferred_element_type=jnp.float32)
    grad_tokens = jnp.zeros(token_rows.shape, jnp.float32).at[picked_index].set(grad_block.astype(jnp.float32))
    input_grad = (grad_rows + grad_logit[:, None] * router[None, :] + grad_tokens).astype(jnp.bfloat16)
    return (mixed, input_grad, kv_part, router_part)

def reference(hidden, cotangent, picks, gain, router, w_query, w_kv, w_out):

    def per_sequence(members):
        return sequence_pass(members[0], members[1], members[2], gain, router, w_query, w_kv, w_out)
    mixed, input_grad, kv_parts, router_parts = lax.map(per_sequence, (hidden, cotangent, picks))
    return (mixed, input_grad, lax.optimization_barrier(jnp.sum(kv_parts, axis=0)), lax.optimization_barrier(jnp.sum(router_parts, axis=0)))
```

```python
import functools
import math

import jax
import jax.numpy as jnp
from jax import lax
from jax.experimental import pallas as pl
from jax.experimental.pallas import tpu as pltpu
from jax.sharding import PartitionSpec as P

MESH = pl.DeviceIdType.MESH
EPSILON = 1e-05
SLOTS = 32
HEAD = 64
F32, BF16 = jnp.float32, jnp.bfloat16
KEY_MARK = 2.0**100
KEY_BOUND = 2.0**64
NEGATIVE = -1e30
FAR = 1 << 30
WIRE = BF16


def dot(left, right, left_dim=1, right_dim=0):
    return lax.dot_general(
        left, right, (((left_dim,), (right_dim,)), ((), ())), preferred_element_type=F32
    )


def copy_to(source, target, send_sem, recv_sem, device):
    return pltpu.make_async_remote_copy(
        src_ref=source,
        dst_ref=target,
        send_sem=send_sem,
        recv_sem=recv_sem,
        device_id=device,
        device_id_type=MESH,
    )


def kernel(
    n, n_dp, width, group_heads,
    hid, cot, picks, gain, router, wq, wkv, wo,
    mixed_out, igrad_out, kvgrad_out, rgrad_out,
    wproj, wout, kv, kvt, scores, dprobs, qpad, opad, dkv, got_dkv, part, got_part,
    gkv, normed, normed_t, share, got_share, total, row_a, row_b, row_d,
    block, block_grad, block_out, dqkv, upstream,
    p1_send, p1_recv, ring_send, ring_recv, sib_send, sib_recv,
    a_send, a_recv, b_send, b_recv, d_send, d_recv,
):
    seq, dp = lax.axis_index("seq"), lax.axis_index("dp")
    core = lax.rem(dp, 2)
    y, z = lax.div(seq, n), lax.rem(seq, n)
    a = z + core * (y - z)
    b = y + core * (z - y)
    keys = n * SLOTS
    half_heads = group_heads * HEAD
    lanes = 2 * group_heads * SLOTS
    half_width = width // 2
    chunk = keys

    def seq_of(b_, a_):
        return (1 - core) * (b_ * n + a_) + core * (a_ * n + b_)

    def peer_a(j):
        return (dp, seq_of(b, lax.rem(a + j, n)))

    def peer_b(j):
        return (dp, seq_of(lax.rem(b + j, n), a))

    def peer_d(j):
        return (lax.rem(dp + j, n_dp), seq)

    sibling = (dp + 1 - 2 * core, seq)

    def each(count, body):
        def step(j, carry):
            body(j)
            return carry

        lax.fori_loop(0, count, step, 0)

    def others(count, body):
        def step(j, carry):
            body(j)
            return carry

        lax.fori_loop(1, count, step, 0)

    barrier = pltpu.get_barrier_semaphore()

    def greet(device):
        pl.semaphore_signal(barrier, inc=1, device_id=device, device_id_type=MESH)

    others(n, lambda j: greet(peer_a(j)))
    others(n, lambda j: greet(peer_b(j)))
    others(n_dp, lambda j: greet(peer_d(j)))

    for side in (0, 1):

        @pl.when(core == side)
        def _():
            cols = slice(side * half_heads, (side + 1) * half_heads)
            wproj[side, y, z, :, :half_heads] = wq[:, cols]
            wproj[side, y, z, :, half_heads:] = wkv[:, side * 128 : (side + 1) * 128]
            wout[side, y, z] = wo[:, side * half_width : (side + 1) * half_width]

    pl.semaphore_wait(barrier, 2 * (n - 1) + n_dp - 1)

    def first(which, ref):
        def make(j):
            own = ref.at[core, y, z]
            return copy_to(own, own, p1_send.at[which, j], p1_recv.at[which, j], peer_a(j))

        return make

    def along_a(which, source, target):
        def make(j):
            return copy_to(source(j), target, a_send.at[which, j], a_recv.at[which, j], peer_a(j))

        return make

    def along_b(which, source, target):
        def make(j):
            return copy_to(source(j), target, b_send.at[which, j], b_recv.at[which, j], peer_b(j))

        return make

    def along_d(which, ref):
        def make(j):
            return copy_to(
                ref.at[dp], ref.at[dp], d_send.at[which, j], d_recv.at[which, j], peer_d(j)
            )

        return make

    def start(make, count=n):
        others(count, lambda j: make(j).start())

    def arrived(make, count=n):
        others(count, lambda j: make(j).wait_recv())

    def sent(make, count=n):
        others(count, lambda j: make(j).wait_send())

    last = n // 2 - 1

    def slab(ref, side, k, part_of=None):
        rows = slice(None) if part_of is None else pl.ds(part_of * (n // 2), n // 2)
        return ref.at[0, k, rows] if side == 0 else ref.at[1, rows, k]

    def ring_start(which, ref, step):
        for side in (0, 1):

            @pl.when(core == side)
            def _():
                for way, block_id, device in (
                    (0, lax.rem(b + n - step, n), peer_b(1)),
                    (1, lax.rem(b + step, n), peer_b(n - 1)),
                ):
                    piece = slab(ref, side, block_id, way if step == last else None)
                    copy_to(
                        piece,
                        piece,
                        ring_send.at[which, step, way],
                        ring_recv.at[which, step, way],
                        device,
                    ).start()

    def ring_copy(which, ref, step, way):
        piece = slab(ref, 0, 0, way if step == last else None)
        return copy_to(
            piece,
            piece,
            ring_send.at[which, step, way],
            ring_recv.at[which, step, way],
            peer_b(1),
        )

    def ring_arrived(which, ref, step):
        for way in (0, 1):
            ring_copy(which, ref, step, way).wait_recv()

    def sib_start(which, ref, slot, block_id):
        for side in (0, 1):

            @pl.when(core == side)
            def _():
                piece = slab(ref, side, block_id)
                copy_to(
                    piece, piece, sib_send.at[which, slot], sib_recv.at[which, slot], sibling
                ).start()

    def sib_copy(which, ref, slot):
        piece = slab(ref, 0, 0)
        return copy_to(piece, piece, sib_send.at[which, slot], sib_recv.at[which, slot], sibling)

    def pass_on(which, ref, step):
        ring_arrived(which, ref, step)
        if step < last:
            ring_start(which, ref, step + 1)
        sib_start(which, ref, 1 + 2 * step, lax.rem(b + n - 1 - step, n))
        if step < last:
            sib_start(which, ref, 2 + 2 * step, lax.rem(b + 1 + step, n))

    start(first(0, wproj))
    start(first(1, wout))

    tokens = hid.shape[1]
    row_id = lax.broadcasted_iota(jnp.int32, (tokens, tokens), 0)
    col_id = lax.broadcasted_iota(jnp.int32, (tokens, tokens), 1)
    pick_row = picks[...].astype(F32)
    pick_wide = jnp.broadcast_to(pick_row, (tokens, tokens))
    pick_col = jnp.sum(jnp.where(row_id == col_id, pick_wide, 0.0), axis=1, keepdims=True)
    rank_col = jnp.sum(jnp.where(col_id < row_id, pick_wide, 0.0), axis=1, keepdims=True)
    pick_tall = jnp.broadcast_to(pick_col, (tokens, tokens))
    rank_row = jnp.sum(jnp.where(row_id < col_id, pick_tall, 0.0), axis=0, keepdims=True)
    slot_row = lax.broadcasted_iota(jnp.int32, (SLOTS, tokens), 0).astype(F32)
    slot_col = lax.broadcasted_iota(jnp.int32, (tokens, SLOTS), 1).astype(F32)
    pack = jnp.where((slot_row == rank_row) & (pick_row > 0.5), 1.0, 0.0)
    spread = jnp.where((slot_col == rank_col) & (pick_col > 0.5), 1.0, 0.0).astype(BF16)
    used = jnp.sum(pack, axis=1, keepdims=True)
    pack = pack.astype(BF16)

    n_chunks = width // chunk

    def at(i):
        return pl.ds(pl.multiple_of(i * chunk, chunk), chunk)

    def gate_step(i, acc):
        return acc + hid[0, :, at(i)].astype(F32) * router[:, at(i)]

    logit = lax.fori_loop(0, n_chunks, gate_step, jnp.zeros((tokens, chunk), F32))
    gate = jax.nn.sigmoid(jnp.sum(logit, axis=1, keepdims=True))

    def pack_step(i, acc):
        rows = dot(pack, hid[0, :, at(i)])
        block[:, at(i)] = rows
        scaled = (gate * cot[0, :, at(i)].astype(F32)).astype(BF16)
        block_grad[:, at(i)] = dot(pack, scaled).astype(BF16)
        return acc + rows * rows

    squares = lax.fori_loop(0, n_chunks, pack_step, jnp.zeros((SLOTS, chunk), F32))
    inv_norm = lax.rsqrt(jnp.sum(squares, axis=1, keepdims=True) * (1.0 / width) + EPSILON)

    def norm_step(i):
        normed[a, :, at(i)] = (block[:, at(i)] * inv_norm * gain[:, at(i)]).astype(BF16)

    each(n_chunks, norm_step)

    arrived(first(0, wproj))
    ring_start(0, wproj, 0)
    sib_start(0, wproj, 0, b)
    for step in range(last + 1):
        pass_on(0, wproj, step)
    arrived(first(1, wout))
    ring_start(1, wout, 0)
    sib_start(1, wout, 0, b)
    for slot in range(n):
        sib_copy(0, wproj, slot).wait_recv()

    def project(side):
        def step(i, acc):
            return acc + dot(normed[a, :, at(i)], wproj[side, i].reshape(chunk, -1))

        zero = jnp.zeros((SLOTS, half_heads + 128), F32)
        return lax.fori_loop(0, n_chunks, step, zero).astype(BF16)

    low_lane = lax.broadcasted_iota(jnp.int32, (SLOTS, 128), 1) < HEAD

    def pad_heads(ref, rows, group):
        for i in range(group_heads // 2):
            pair = rows[:, i * 128 : (i + 1) * 128]
            for parity in (0, 1):
                moved = pair if parity == group else pltpu.roll(pair, HEAD, 1)
                kept = jnp.where(low_lane, moved, 0.0) if group == 0 else jnp.where(low_lane, 0.0, moved)
                at_row = (group * group_heads + 2 * i + parity) * SLOTS
                ref[at_row : at_row + SLOTS, :] = kept.astype(BF16)

    def join_heads(both):
        tall = jnp.transpose(both)
        groups = []
        for group in (0, 1):
            pairs = []
            for i in range(group_heads // 2):
                at_row = (group * group_heads + 2 * i) * SLOTS
                even = tall[at_row : at_row + SLOTS, :]
                odd = tall[at_row + SLOTS : at_row + 2 * SLOTS, :]
                if group == 0:
                    pairs.append(jnp.where(low_lane, even, pltpu.roll(odd, HEAD, 1)))
                else:
                    pairs.append(jnp.where(low_lane, pltpu.roll(even, HEAD, 1), odd))
            groups.append(jnp.concatenate(pairs, axis=1))
        return groups

    low = project(0).astype(F32)
    high = project(1).astype(F32)
    lane_id = lax.broadcasted_iota(jnp.int32, (SLOTS, 128), 1)
    own_keys = jnp.where((lane_id == 0) & (used < 0.5), KEY_MARK, low[:, half_heads:])
    kv[b, a, :, :128] = own_keys.astype(BF16)
    kv[b, a, :, 128:] = high[:, half_heads:].astype(BF16)
    kv_first = along_a(0, lambda j: kv.at[b, a], kv.at[b, a])
    kv_second = along_b(0, lambda j: kv.at[b], kv.at[b])
    start(kv_first)
    pad_heads(qpad, low[:, :half_heads], 0)
    pad_heads(qpad, high[:, :half_heads], 1)
    pass_on(1, wout, 0)
    arrived(kv_first)
    start(kv_second)
    for step in range(1, last):
        pass_on(1, wout, step)
    arrived(kv_second)

    key_row = lax.broadcasted_iota(jnp.int32, (keys, 1), 0)
    query_at = seq * SLOTS + (lax.broadcasted_iota(jnp.int32, (1, lanes), 1) & (SLOTS - 1))
    scale = HEAD**-0.5

    def score_step(i, top):
        rows = kv[i].reshape(keys, 256).astype(F32)
        kvt[i] = jnp.transpose(rows).astype(BF16)
        key_at = seq_of(i, key_row >> 5) * SLOTS + (key_row & (SLOTS - 1))
        key_at = jnp.where(rows[:, 0:1] < KEY_BOUND, key_at, FAR)
        s = dot(rows[:, :128].astype(BF16), qpad[...], 1, 1) * scale
        s = jnp.where(key_at <= query_at, s, NEGATIVE)
        scores[i] = s
        return jnp.maximum(top, jnp.max(s, axis=0, keepdims=True))

    top = lax.fori_loop(0, n, score_step, jnp.full((1, lanes), NEGATIVE, F32))

    def exp_step(i, acc):
        e = jnp.exp(scores[i] - top)
        scores[i] = e
        return acc + jnp.sum(e, axis=0, keepdims=True)

    inv_sum = 1.0 / lax.fori_loop(0, n, exp_step, jnp.zeros((1, lanes), F32))

    if last > 0:
        pass_on(1, wout, last)
    normed_gather = along_a(1, lambda j: normed.at[a], normed.at[a])
    start(normed_gather)
    for slot in range(n):
        sib_copy(1, wout, slot).wait_recv()

    out_rows = n * wout.shape[3]

    def out_at(i):
        return pl.ds(pl.multiple_of(i * out_rows, out_rows), out_rows)

    def head_grad_step(i):
        acc = jnp.zeros((SLOTS, out_rows), F32)
        for side in (0, 1):
            part_grad = block_grad[:, side * half_width : (side + 1) * half_width]
            acc += dot(part_grad, wout[side, i].reshape(out_rows, half_width), 1, 1)
        upstream[:, out_at(i)] = acc

    each(n, head_grad_step)
    for group in (0, 1):
        rows = upstream[:, group * half_heads : (group + 1) * half_heads]
        pad_heads(opad, rows, group)

    def prob_step(i, carry):
        inner, mixed_t = carry
        p = scores[i] * inv_sum
        scores[i] = p
        dp_ = dot(kv[i].reshape(keys, 256)[:, 128:], opad[...], 1, 1)
        dprobs[i] = dp_
        mixed_t += dot(kvt[i, 128:, :], p.astype(BF16))
        return inner + jnp.sum(p * dp_, axis=0, keepdims=True), mixed_t

    inner, mixed_t = lax.fori_loop(
        0, n, prob_step, (jnp.zeros((1, lanes), F32), jnp.zeros((128, lanes), F32))
    )

    send_dkv = along_b(1, lambda j: dkv.at[lax.rem(b + j, n)], got_dkv.at[b])

    def grad_step(j, query_t):
        i = lax.rem(b + j, n)
        p = scores[i]
        ds = (p * (dprobs[i] - inner)).astype(BF16)
        dkv[i, :, :128] = (dot(ds, qpad[...]) * scale).astype(WIRE)
        dkv[i, :, 128:] = dot(p.astype(BF16), opad[...]).astype(WIRE)

        @pl.when(j < n)
        def _():
            send_dkv(lax.rem(j, n)).start()

        return query_t + dot(kvt[i, :128, :], ds)

    query_t = lax.fori_loop(1, n + 1, grad_step, jnp.zeros((128, lanes), F32))

    heads = jnp.concatenate(join_heads(mixed_t), axis=1).astype(BF16)
    for side in (0, 1):
        rows = wout[side].reshape(n * out_rows, half_width)
        block_out[:, side * half_width : (side + 1) * half_width] = dot(heads, rows).astype(BF16)

    def mix_step(i, acc):
        out_tokens = dot(spread, block_out[:, at(i)])
        mixed_out[0, :, at(i)] = (hid[0, :, at(i)].astype(F32) + gate * out_tokens).astype(BF16)
        return acc + cot[0, :, at(i)].astype(F32) * out_tokens

    through = lax.fori_loop(0, n_chunks, mix_step, jnp.zeros((tokens, chunk), F32))
    through = jnp.sum(through, axis=1, keepdims=True)
    grad_logit = through * gate * (1.0 - gate)

    def router_step(i):
        term = hid[0, :, at(i)].astype(F32) * grad_logit
        row_a[a, :, at(i)] = jnp.sum(term, axis=0, keepdims=True)

    each(n_chunks, router_step)
    router_first = along_a(2, lambda j: row_a.at[a], row_a.at[a])
    router_second = along_b(2, lambda j: row_b.at[b], row_b.at[b])
    router_third = along_d(0, row_d)
    start(router_first)

    for group, rows in enumerate(join_heads(query_t * scale)):
        dqkv[group, :, :half_heads] = rows.astype(BF16)
    arrived(normed_gather)

    def turn_step(i):
        rows = normed[:, :, at(i)].reshape(keys, chunk).astype(F32)
        normed_t[i] = jnp.transpose(rows).astype(BF16).reshape(n, SLOTS, keys)

    each(n_chunks, turn_step)

    arrived(send_dkv)
    mine = dkv[b].astype(F32)
    mine = lax.fori_loop(
        1, n, lambda j, acc: acc + got_dkv[lax.rem(b + j, n)].astype(F32), mine
    )
    part[...] = mine.reshape(n, SLOTS, 256)
    send_part = along_a(3, lambda j: part.at[lax.rem(a + j, n)], got_part.at[a])
    start(send_part)
    arrived(router_first)
    row_b[b] = jnp.sum(row_a[...], axis=0)
    start(router_second)
    arrived(send_part)
    own = part[a]
    own = lax.fori_loop(1, n, lambda j, acc: acc + got_part[lax.rem(a + j, n)], own)
    grad_kv = own.astype(BF16)
    gkv[a] = grad_kv
    gkv_gather = along_a(4, lambda j: gkv.at[a], gkv.at[a])
    start(gkv_gather)
    dqkv[0, :, half_heads:] = grad_kv[:, :128]
    dqkv[1, :, half_heads:] = grad_kv[:, 128:]

    def back_step(i, acc):
        grads = dot(dqkv[0], wproj[0, i].reshape(chunk, -1), 1, 1)
        grads += dot(dqkv[1], wproj[1, i].reshape(chunk, -1), 1, 1)
        u = grads * gain[:, at(i)]
        upstream[:, at(i)] = u
        return acc + u * block[:, at(i)]

    along = lax.fori_loop(0, n_chunks, back_step, jnp.zeros((SLOTS, chunk), F32))
    along = jnp.sum(along, axis=1, keepdims=True) * (1.0 / width)

    arrived(gkv_gather)
    every = gkv[...].reshape(keys, 256)

    def share_step(i):
        place = (1 - core) * (i * n + a) + core * (a * n + i)
        share[i] = dot(normed_t[lax.div(place, n), lax.rem(place, n)], every)

    each(n, share_step)
    send_share = along_b(3, lambda j: share.at[lax.rem(b + j, n)], got_share.at[b])
    start(send_share)

    arrived(router_second)
    row_d[dp] = jnp.sum(row_b[...], axis=0)
    start(router_third, n_dp)

    cubed = inv_norm * inv_norm * inv_norm * along

    def input_step(i):
        rows = inv_norm * upstream[:, at(i)] - block[:, at(i)] * cubed
        tokens_grad = dot(spread, rows.astype(BF16))
        grads = cot[0, :, at(i)].astype(F32) + grad_logit * router[:, at(i)] + tokens_grad
        igrad_out[0, :, at(i)] = grads.astype(BF16)

    each(n_chunks, input_step)

    arrived(send_share)
    own = share[b]
    own = lax.fori_loop(1, n, lambda j, acc: acc + got_share[lax.rem(b + j, n)], own)
    total[dp] = own
    send_total = along_d(1, total)
    start(send_total, n_dp)
    arrived(router_third, n_dp)
    row = jnp.sum(row_d[...], axis=0)
    per_tile = 128 // SLOTS
    tile = jnp.zeros((1, SLOTS), F32)
    for i in range(width // SLOTS):
        tile = jnp.where(seq == i, row[:, i * SLOTS : (i + 1) * SLOTS], tile)
    rgrad_out[...] = tile
    arrived(send_total, n_dp)
    kvgrad_out[...] = jnp.sum(total[...], axis=0)

    sent(first(0, wproj))
    sent(first(1, wout))
    for which, ref in ((0, wproj), (1, wout)):
        for step in range(last + 1):
            for way in (0, 1):
                ring_copy(which, ref, step, way).wait_send()
        for slot in range(n):
            sib_copy(which, ref, slot).wait_send()
    for make in (kv_first, kv_second, normed_gather, send_dkv, router_first, router_second):
        sent(make)
    for make in (send_part, gkv_gather, send_share):
        sent(make)
    sent(router_third, n_dp)
    sent(send_total, n_dp)


def local(hidden, cotangent, picks, gain, router, w_query, w_kv, w_out):
    n_dp, n_seq = lax.axis_size("dp"), lax.axis_size("seq")
    n = math.isqrt(n_seq)
    tokens, width = hidden.shape[1:]
    half_heads = w_query.shape[1] // 2
    group_heads = half_heads // HEAD
    out_slab = w_out.shape[0]
    keys = n * SLOTS
    lanes = 2 * group_heads * SLOTS
    vmem = pl.BlockSpec(memory_space=pltpu.VMEM)
    dma = pltpu.SemaphoreType.DMA
    outs = pl.pallas_call(
        functools.partial(kernel, n, n_dp, width, group_heads),
        out_shape=(
            jax.ShapeDtypeStruct(hidden.shape, BF16),
            jax.ShapeDtypeStruct(hidden.shape, BF16),
            jax.ShapeDtypeStruct((SLOTS, 256), F32),
            jax.ShapeDtypeStruct((1, SLOTS), F32),
        ),
        in_specs=[vmem] * 8,
        out_specs=(vmem,) * 4,
        scratch_shapes=[
            pltpu.VMEM((2, n, n, SLOTS, half_heads + 128), BF16),
            pltpu.VMEM((2, n, n, out_slab, width // 2), BF16),
            pltpu.VMEM((n, n, SLOTS, 256), BF16),
            pltpu.VMEM((n, 256, keys), BF16),
            pltpu.VMEM((n, keys, lanes), F32),
            pltpu.VMEM((n, keys, lanes), F32),
            pltpu.VMEM((lanes, 128), BF16),
            pltpu.VMEM((lanes, 128), BF16),
            pltpu.VMEM((n, keys, 256), WIRE),
            pltpu.VMEM((n, keys, 256), WIRE),
            pltpu.VMEM((n, SLOTS, 256), F32),
            pltpu.VMEM((n, SLOTS, 256), F32),
            pltpu.VMEM((n, SLOTS, 256), BF16),
            pltpu.VMEM((n, SLOTS, width), BF16),
            pltpu.VMEM((n, n, SLOTS, keys), BF16),
            pltpu.VMEM((n, SLOTS, 256), F32),
            pltpu.VMEM((n, SLOTS, 256), F32),
            pltpu.VMEM((n_dp, SLOTS, 256), F32),
            pltpu.VMEM((n, 1, width), F32),
            pltpu.VMEM((n, 1, width), F32),
            pltpu.VMEM((n_dp, 1, width), F32),
            pltpu.VMEM((SLOTS, width), F32),
            pltpu.VMEM((SLOTS, width), BF16),
            pltpu.VMEM((SLOTS, width), BF16),
            pltpu.VMEM((2, SLOTS, half_heads + 128), BF16),
            pltpu.VMEM((SLOTS, width), F32),
            dma((2, n)),
            dma((2, n)),
            dma((2, n // 2, 2)),
            dma((2, n // 2, 2)),
            dma((2, n)),
            dma((2, n)),
            dma((5, n)),
            dma((5, n)),
            dma((4, n)),
            dma((4, n)),
            dma((2, n_dp)),
            dma((2, n_dp)),
        ],
        compiler_params=pltpu.CompilerParams(
            collective_id=0, has_side_effects=True, vmem_limit_bytes=58 * 1024 * 1024
        ),
    )(
        hidden, cotangent, picks, gain.reshape(1, -1), router.reshape(1, -1), w_query, w_kv, w_out
    )
    mixed, input_grad, kv_grad, router_grad = outs
    return mixed, input_grad, kv_grad, router_grad.reshape(-1)


def solution(mesh):
    rows = P("dp", "seq", None)
    weight = P("seq", None)
    return jax.shard_map(
        local,
        mesh=mesh,
        in_specs=(rows, rows, P("dp", "seq"), P(), P(), weight, weight, weight),
        out_specs=(rows, rows, weight, P("seq")),
        check_vma=False,
    )
```

```python
import functools
import math

import jax
import jax.numpy as jnp
from jax import lax
from jax.experimental import pallas as pl
from jax.experimental.pallas import tpu as pltpu
from jax.sharding import PartitionSpec as P

MESH = pl.DeviceIdType.MESH
EPSILON = 1e-05
SLOTS = 32
HEAD = 64
F32, BF16 = jnp.float32, jnp.bfloat16
KEY_MARK = 2.0**100
KEY_BOUND = 2.0**64
NEGATIVE = -1e30
FAR = 1 << 30
PIECES = (4, 2)


def dot(left, right, left_dim=1, right_dim=0):
    return lax.dot_general(
        left, right, (((left_dim,), (right_dim,)), ((), ())), preferred_element_type=F32
    )


def copy_to(source, target, send_sem, recv_sem, device):
    return pltpu.make_async_remote_copy(
        src_ref=source,
        dst_ref=target,
        send_sem=send_sem,
        recv_sem=recv_sem,
        device_id=device,
        device_id_type=MESH,
    )


def kernel(
    n, n_dp, width, group_heads,
    hid, cot, picks, gain, router, wq, wkv, wo,
    mixed_out, igrad_out, kvgrad_out, rgrad_out,
    wproj, wout, kv, kvt, scores, dprobs, qpad, opad, dkv, got_dkv, part, got_part,
    gkv, normed, slices, normed_t, share, got_share, total, row_a, row_b, row_d,
    block, block_grad, block_out, dqkv, upstream,
    p1_send, p1_recv, ring_send, ring_recv, sib_send, sib_recv,
    x_send, x_recv, rs_send, rs_recv, d_send, d_recv,
):
    seq, dp = lax.axis_index("seq"), lax.axis_index("dp")
    core = lax.rem(dp, 2)
    y, z = lax.div(seq, n), lax.rem(seq, n)
    a = z + core * (y - z)
    b = y + core * (z - y)
    keys = n * SLOTS
    half_heads = group_heads * HEAD
    lanes = 2 * group_heads * SLOTS
    half_width = width // 2
    chunk = keys

    def seq_of(b_, a_):
        return (1 - core) * (b_ * n + a_) + core * (a_ * n + b_)

    def peer_a(j):
        return (dp, seq_of(b, lax.rem(a + j, n)))

    def peer_b(j):
        return (dp, seq_of(lax.rem(b + j, n), a))

    def peer_y(j):
        return (dp, lax.rem(y + j, n) * n + z)

    def peer_z(j):
        return (dp, y * n + lax.rem(z + j, n))

    def peer_d(j):
        return (lax.rem(dp + j, n_dp), seq)

    sibling = (dp + 1 - 2 * core, seq)

    def each(count, body):
        def step(j, carry):
            body(j)
            return carry

        lax.fori_loop(0, count, step, 0)

    def others(count, body):
        def step(j, carry):
            body(j)
            return carry

        lax.fori_loop(1, count, step, 0)

    barrier = pltpu.get_barrier_semaphore()

    def greet(device):
        pl.semaphore_signal(barrier, inc=1, device_id=device, device_id_type=MESH)

    others(n, lambda j: greet(peer_a(j)))
    others(n, lambda j: greet(peer_b(j)))
    others(n_dp, lambda j: greet(peer_d(j)))

    for side in (0, 1):

        @pl.when(core == side)
        def _():
            cols = slice(side * half_heads, (side + 1) * half_heads)
            wproj[side, y, z, :, :half_heads] = wq[:, cols]
            wproj[side, y, z, :, half_heads:] = wkv[:, side * 128 : (side + 1) * 128]
            wout[side, y, z] = wo[:, side * half_width : (side + 1) * half_width]

    tokens = hid.shape[1]
    row_id = lax.broadcasted_iota(jnp.int32, (tokens, tokens), 0)
    col_id = lax.broadcasted_iota(jnp.int32, (tokens, tokens), 1)
    pick_row = picks[...].astype(F32)
    pick_wide = jnp.broadcast_to(pick_row, (tokens, tokens))
    pick_col = jnp.sum(jnp.where(row_id == col_id, pick_wide, 0.0), axis=1, keepdims=True)
    rank_col = jnp.sum(jnp.where(col_id < row_id, pick_wide, 0.0), axis=1, keepdims=True)
    pick_tall = jnp.broadcast_to(pick_col, (tokens, tokens))
    rank_row = jnp.sum(jnp.where(row_id < col_id, pick_tall, 0.0), axis=0, keepdims=True)
    slot_row = lax.broadcasted_iota(jnp.int32, (SLOTS, tokens), 0).astype(F32)
    slot_col = lax.broadcasted_iota(jnp.int32, (tokens, SLOTS), 1).astype(F32)
    pack = jnp.where((slot_row == rank_row) & (pick_row > 0.5), 1.0, 0.0)
    spread = jnp.where((slot_col == rank_col) & (pick_col > 0.5), 1.0, 0.0).astype(BF16)
    used = jnp.sum(pack, axis=1, keepdims=True)
    pack = pack.astype(BF16)

    n_chunks = width // chunk

    def at(i):
        return pl.ds(pl.multiple_of(i * chunk, chunk), chunk)

    def gate_step(i, acc):
        return acc + hid[0, :, at(i)].astype(F32) * router[:, at(i)]

    logit = lax.fori_loop(0, n_chunks, gate_step, jnp.zeros((tokens, chunk), F32))
    gate = jax.nn.sigmoid(jnp.sum(logit, axis=1, keepdims=True))

    pl.semaphore_wait(barrier, 2 * (n - 1) + n_dp - 1)

    outgoing = []

    def first(which, ref):
        def make(j):
            own = ref.at[core, y, z]
            return copy_to(own, own, p1_send.at[which, j], p1_recv.at[which, j], peer_a(j))

        return make

    def along(peer, which, source, target):
        def make(j):
            return copy_to(source(j), target, x_send.at[which, j], x_recv.at[which, j], peer(j))

        return make

    def along_d(which, ref):
        def make(j):
            return copy_to(
                ref.at[dp], ref.at[dp], d_send.at[which, j], d_recv.at[which, j], peer_d(j)
            )

        return make

    def start(make, count=n):
        others(count, lambda j: make(j).start())
        outgoing.append(lambda: sent(make, count))

    def arrived(make, count=n):
        others(count, lambda j: make(j).wait_recv())

    def sent(make, count=n):
        others(count, lambda j: make(j).wait_send())

    last = n // 2 - 1

    def slab(ref, side, k, which=0, piece=None):
        size = n // PIECES[which]
        rows = slice(None) if piece is None else pl.ds(piece * size, size)
        return ref.at[0, k, rows] if side == 0 else ref.at[1, rows, k]

    def goes(which, step, way, piece):
        return step < last or (piece < PIECES[which] // 2) == (way == 0)

    def ring_start(which, ref, step, piece):
        for side in (0, 1):

            @pl.when(core == side)
            def _():
                for way, block_id, device in (
                    (0, lax.rem(b + n - step, n), peer_b(1)),
                    (1, lax.rem(b + step, n), peer_b(n - 1)),
                ):
                    if goes(which, step, way, piece):
                        rows = slab(ref, side, block_id, which, piece)
                        copy_to(
                            rows,
                            rows,
                            ring_send.at[which, step, way, piece],
                            ring_recv.at[which, step, way, piece],
                            device,
                        ).start()

        for way in (0, 1):
            if goes(which, step, way, piece):
                outgoing.append(
                    lambda way=way: ring_copy(which, ref, step, way, piece).wait_send()
                )

    def ring_copy(which, ref, step, way, piece):
        rows = slab(ref, 0, 0, which, piece)
        return copy_to(
            rows,
            rows,
            ring_send.at[which, step, way, piece],
            ring_recv.at[which, step, way, piece],
            peer_b(1),
        )

    def sib_start(which, ref, slot, block_id):
        for side in (0, 1):

            @pl.when(core == side)
            def _():
                rows = slab(ref, side, block_id)
                copy_to(
                    rows, rows, sib_send.at[which, slot], sib_recv.at[which, slot], sibling
                ).start()

        outgoing.append(lambda: sib_copy(which, ref, slot).wait_send())

    def sib_copy(which, ref, slot):
        rows = slab(ref, 0, 0)
        return copy_to(rows, rows, sib_send.at[which, slot], sib_recv.at[which, slot], sibling)

    def pass_first(which, ref):
        for piece in range(PIECES[which]):
            ring_start(which, ref, 0, piece)
        sib_start(which, ref, 0, b)

    def pass_on(which, ref, step):
        for piece in range(PIECES[which]):
            for way in (0, 1):
                if goes(which, step, way, piece):
                    ring_copy(which, ref, step, way, piece).wait_recv()
            if step < last:
                ring_start(which, ref, step + 1, piece)
        sib_start(which, ref, 1 + 2 * step, lax.rem(b + n - 1 - step, n))
        if step < last:
            sib_start(which, ref, 2 + 2 * step, lax.rem(b + 1 + step, n))

    start(first(0, wproj))

    def pack_step(i, acc):
        rows = dot(pack, hid[0, :, at(i)])
        block[:, at(i)] = rows
        scaled = (gate * cot[0, :, at(i)].astype(F32)).astype(BF16)
        block_grad[:, at(i)] = dot(pack, scaled).astype(BF16)
        return acc + rows * rows

    squares = lax.fori_loop(0, n_chunks, pack_step, jnp.zeros((SLOTS, chunk), F32))
    inv_norm = lax.rsqrt(jnp.sum(squares, axis=1, keepdims=True) * (1.0 / width) + EPSILON)

    def norm_step(i):
        normed[:, at(i)] = (block[:, at(i)] * inv_norm * gain[:, at(i)]).astype(BF16)

    each(n_chunks, norm_step)

    slices[y] = normed[:, at(y)]
    send_slices = along(peer_y, 5, lambda j: normed.at[:, at(lax.rem(y + j, n))], slices.at[y])

    arrived(first(0, wproj))
    pass_first(0, wproj)
    start(first(1, wout))
    start(send_slices)
    for step in range(last + 1):
        pass_on(0, wproj, step)
    arrived(first(1, wout))
    pass_first(1, wout)
    for slot in range(n):
        sib_copy(0, wproj, slot).wait_recv()

    def project(side):
        def step(i, acc):
            return acc + dot(normed[:, at(i)], wproj[side, i].reshape(chunk, -1))

        zero = jnp.zeros((SLOTS, half_heads + 128), F32)
        return lax.fori_loop(0, n_chunks, step, zero).astype(BF16)

    low_lane = lax.broadcasted_iota(jnp.int32, (SLOTS, 128), 1) < HEAD

    def pad_heads(ref, rows, group):
        for i in range(group_heads // 2):
            pair = rows[:, i * 128 : (i + 1) * 128]
            for parity in (0, 1):
                moved = pair if parity == group else pltpu.roll(pair, HEAD, 1)
                kept = jnp.where(low_lane, moved, 0.0) if group == 0 else jnp.where(low_lane, 0.0, moved)
                at_row = (group * group_heads + 2 * i + parity) * SLOTS
                ref[at_row : at_row + SLOTS, :] = kept.astype(BF16)

    def join_heads(both):
        tall = jnp.transpose(both)
        groups = []
        for group in (0, 1):
            pairs = []
            for i in range(group_heads // 2):
                at_row = (group * group_heads + 2 * i) * SLOTS
                even = tall[at_row : at_row + SLOTS, :]
                odd = tall[at_row + SLOTS : at_row + 2 * SLOTS, :]
                if group == 0:
                    pairs.append(jnp.where(low_lane, even, pltpu.roll(odd, HEAD, 1)))
                else:
                    pairs.append(jnp.where(low_lane, pltpu.roll(even, HEAD, 1), odd))
            groups.append(jnp.concatenate(pairs, axis=1))
        return groups

    low = project(0).astype(F32)
    high = project(1).astype(F32)
    lane_id = lax.broadcasted_iota(jnp.int32, (SLOTS, 128), 1)
    own_keys = jnp.where((lane_id == 0) & (used < 0.5), KEY_MARK, low[:, half_heads:])
    kv[b, a, :, :128] = own_keys.astype(BF16)
    kv[b, a, :, 128:] = high[:, half_heads:].astype(BF16)
    kv_first = along(peer_a, 0, lambda j: kv.at[b, a], kv.at[b, a])
    kv_second = along(peer_b, 1, lambda j: kv.at[b], kv.at[b])
    start(kv_first)
    pad_heads(qpad, low[:, :half_heads], 0)
    pad_heads(qpad, high[:, :half_heads], 1)
    pass_on(1, wout, 0)
    arrived(kv_first)
    start(kv_second)
    if last > 1:
        pass_on(1, wout, 1)

    key_row = lax.broadcasted_iota(jnp.int32, (keys, 1), 0)
    query_at = seq * SLOTS + (lax.broadcasted_iota(jnp.int32, (1, lanes), 1) & (SLOTS - 1))
    scale = HEAD**-0.5

    def score_step(i, top):
        rows = kv[i].reshape(keys, 256).astype(F32)
        kvt[i] = jnp.transpose(rows).astype(BF16)
        key_at = seq_of(i, key_row >> 5) * SLOTS + (key_row & (SLOTS - 1))
        key_at = jnp.where(rows[:, 0:1] < KEY_BOUND, key_at, FAR)
        s = dot(rows[:, :128].astype(BF16), qpad[...], 1, 1) * scale
        s = jnp.where(key_at <= query_at, s, NEGATIVE)
        scores[i] = s
        return jnp.maximum(top, jnp.max(s, axis=0, keepdims=True))

    top = score_step(b, jnp.full((1, lanes), NEGATIVE, F32))
    for step in range(2, last):
        pass_on(1, wout, step)

    def next_score_step(t, top):
        after, odd = lax.div(t, 2), lax.rem(t, 2)
        j = (1 - odd) * (1 + after) + odd * (n - 1 - after)
        kv_second(j).wait_recv()
        return score_step(lax.rem(b + n - j, n), top)

    top = lax.fori_loop(0, n - 1, next_score_step, top)

    if last > 0:
        pass_on(1, wout, last)
    for slot in range(n):
        sib_copy(1, wout, slot).wait_recv()

    out_rows = n * wout.shape[3]

    def out_at(i):
        return pl.ds(pl.multiple_of(i * out_rows, out_rows), out_rows)

    def head_grad_step(i):
        acc = jnp.zeros((SLOTS, out_rows), F32)
        for side in (0, 1):
            part_grad = block_grad[:, side * half_width : (side + 1) * half_width]
            acc += dot(part_grad, wout[side, i].reshape(out_rows, half_width), 1, 1)
        upstream[:, out_at(i)] = acc

    each(n, head_grad_step)
    for group in (0, 1):
        rows = upstream[:, group * half_heads : (group + 1) * half_heads]
        pad_heads(opad, rows, group)

    def exp_step(i, carry):
        total_exp, inner = carry
        e = jnp.exp(scores[i] - top)
        scores[i] = e
        grads = dot(kv[i].reshape(keys, 256)[:, 128:], opad[...], 1, 1)
        dprobs[i] = grads
        total_exp += jnp.sum(e, axis=0, keepdims=True)
        return total_exp, inner + jnp.sum(e * grads, axis=0, keepdims=True)

    zero = jnp.zeros((1, lanes), F32)
    total_exp, inner = lax.fori_loop(0, n, exp_step, (zero, zero))
    inv_sum = 1.0 / total_exp
    inner = inner * inv_sum

    def rs_slab(step, way):
        return lax.rem(b + n + (1 - 2 * way) * (n // 2 - step), n)

    def rs_copy(step, way, kind):
        return copy_to(
            dkv.at[kind, rs_slab(step, way)],
            got_dkv.at[way, kind, step],
            rs_send.at[way, kind, step],
            rs_recv.at[way, kind, step],
            peer_b(1 + way * (n - 2)),
        )

    def rs_start(step, way, kind):
        rs_copy(step, way, kind).start()
        outgoing.append(lambda: rs_copy(step, way, kind).wait_send())

    def grad_step(t, carry):
        mixed_t, query_t = carry
        i = rs_slab(lax.div(t + 1, 2), 1 - lax.rem(t, 2))
        p = scores[i] * inv_sum
        half = p.astype(BF16)
        ds = (p * (dprobs[i] - inner)).astype(BF16)
        dkv[0, i] = dot(ds, qpad[...]) * scale
        dkv[1, i] = dot(half, opad[...])

        @pl.when(t == 0)
        def _():
            rs_copy(0, 0, 0).start()
            rs_copy(0, 1, 1).start()

        return mixed_t + dot(kvt[i, 128:, :], half), query_t + dot(kvt[i, :128, :], ds)

    zero = jnp.zeros((128, lanes), F32)
    mixed_t, query_t = lax.fori_loop(0, n, grad_step, (zero, zero))
    outgoing.append(lambda: rs_copy(0, 0, 0).wait_send())
    outgoing.append(lambda: rs_copy(0, 1, 1).wait_send())

    def rs_step(step):
        for way in (0, 1):
            for kind in (0, 1):
                if step > 1 or kind == way:
                    rs_copy(step - 1, way, kind).wait_recv()
                    dkv[kind, rs_slab(step, way)] += got_dkv[way, kind, step - 1]
                rs_start(step, way, kind)

    rs_step(1)

    heads = jnp.concatenate(join_heads(mixed_t), axis=1).astype(BF16)
    for side in (0, 1):
        rows = wout[side].reshape(n * out_rows, half_width)
        block_out[:, side * half_width : (side + 1) * half_width] = dot(heads, rows).astype(BF16)

    if last > 1:
        rs_step(2)

    def mix_step(i, acc):
        out_tokens = dot(spread, block_out[:, at(i)])
        mixed_out[0, :, at(i)] = (hid[0, :, at(i)].astype(F32) + gate * out_tokens).astype(BF16)
        return acc + cot[0, :, at(i)].astype(F32) * out_tokens

    through = lax.fori_loop(0, n_chunks, mix_step, jnp.zeros((tokens, chunk), F32))
    through = jnp.sum(through, axis=1, keepdims=True)
    grad_logit = through * gate * (1.0 - gate)

    def router_step(i):
        term = hid[0, :, at(i)].astype(F32) * grad_logit
        row_a[a, :, at(i)] = jnp.sum(term, axis=0, keepdims=True)

    each(n_chunks, router_step)
    router_first = along(peer_a, 2, lambda j: row_a.at[a], row_a.at[a])
    router_second = along(peer_b, 3, lambda j: row_b.at[b], row_b.at[b])
    router_third = along_d(0, row_d)
    start(router_first)

    for group, rows in enumerate(join_heads(query_t * scale)):
        dqkv[group, :, :half_heads] = rows.astype(BF16)
    for step in range(3, last + 1):
        rs_step(step)
    arrived(send_slices)
    normed_t[...] = jnp.transpose(slices[...].reshape(keys, chunk).astype(F32)).astype(BF16)

    for kind in (0, 1):
        mine = dkv[kind, b]
        for way in (0, 1):
            rs_copy(last, way, kind).wait_recv()
            mine += got_dkv[way, kind, last]
        part[:, :, kind * 128 : (kind + 1) * 128] = mine.reshape(n, SLOTS, 128)
    send_part = along(peer_a, 4, lambda j: part.at[lax.rem(a + j, n)], got_part.at[a])
    start(send_part)
    arrived(router_first)
    row_b[b] = jnp.sum(row_a[...], axis=0)
    start(router_second)
    arrived(send_part)
    own = part[a]
    own = lax.fori_loop(1, n, lambda j, acc: acc + got_part[lax.rem(a + j, n)], own)
    grad_kv = own.astype(BF16)
    gkv[y] = grad_kv
    gkv_gather = along(peer_y, 6, lambda j: gkv.at[y], gkv.at[y])
    start(gkv_gather)
    dqkv[0, :, half_heads:] = grad_kv[:, :128]
    dqkv[1, :, half_heads:] = grad_kv[:, 128:]

    def back_step(i, acc):
        grads = dot(dqkv[0], wproj[0, i].reshape(chunk, -1), 1, 1)
        grads += dot(dqkv[1], wproj[1, i].reshape(chunk, -1), 1, 1)
        u = grads * gain[:, at(i)]
        upstream[:, at(i)] = u
        return acc + u * block[:, at(i)]

    overlap = lax.fori_loop(0, n_chunks, back_step, jnp.zeros((SLOTS, chunk), F32))
    overlap = jnp.sum(overlap, axis=1, keepdims=True) * (1.0 / width)

    arrived(gkv_gather)
    share[...] = dot(normed_t[...], gkv[...].reshape(keys, 256)).reshape(n, SLOTS, 256)
    send_share = along(peer_z, 7, lambda j: share.at[lax.rem(z + j, n)], got_share.at[z])
    start(send_share)

    arrived(router_second)
    row_d[dp] = jnp.sum(row_b[...], axis=0)
    start(router_third, n_dp)

    cubed = inv_norm * inv_norm * inv_norm * overlap

    def input_step(i):
        rows = inv_norm * upstream[:, at(i)] - block[:, at(i)] * cubed
        tokens_grad = dot(spread, rows.astype(BF16))
        grads = cot[0, :, at(i)].astype(F32) + grad_logit * router[:, at(i)] + tokens_grad
        igrad_out[0, :, at(i)] = grads.astype(BF16)

    each(n_chunks, input_step)

    arrived(send_share)
    own = share[z]
    own = lax.fori_loop(1, n, lambda j, acc: acc + got_share[lax.rem(z + j, n)], own)
    total[dp] = own
    send_total = along_d(1, total)
    start(send_total, n_dp)
    arrived(router_third, n_dp)
    row = jnp.sum(row_d[...], axis=0)
    per_tile = 128 // SLOTS
    tile = jnp.zeros((1, SLOTS), F32)
    for i in range(width // SLOTS):
        tile = jnp.where(seq == i, row[:, i * SLOTS : (i + 1) * SLOTS], tile)
    rgrad_out[...] = tile
    arrived(send_total, n_dp)
    kvgrad_out[...] = jnp.sum(total[...], axis=0)

    for wait in outgoing:
        wait()


def local(hidden, cotangent, picks, gain, router, w_query, w_kv, w_out):
    n_dp, n_seq = lax.axis_size("dp"), lax.axis_size("seq")
    n = math.isqrt(n_seq)
    tokens, width = hidden.shape[1:]
    half_heads = w_query.shape[1] // 2
    group_heads = half_heads // HEAD
    out_slab = w_out.shape[0]
    keys = n * SLOTS
    lanes = 2 * group_heads * SLOTS
    vmem = pl.BlockSpec(memory_space=pltpu.VMEM)
    dma = pltpu.SemaphoreType.DMA
    outs = pl.pallas_call(
        functools.partial(kernel, n, n_dp, width, group_heads),
        out_shape=(
            jax.ShapeDtypeStruct(hidden.shape, BF16),
            jax.ShapeDtypeStruct(hidden.shape, BF16),
            jax.ShapeDtypeStruct((SLOTS, 256), F32),
            jax.ShapeDtypeStruct((1, SLOTS), F32),
        ),
        in_specs=[vmem] * 8,
        out_specs=(vmem,) * 4,
        scratch_shapes=[
            pltpu.VMEM((2, n, n, SLOTS, half_heads + 128), BF16),
            pltpu.VMEM((2, n, n, out_slab, width // 2), BF16),
            pltpu.VMEM((n, n, SLOTS, 256), BF16),
            pltpu.VMEM((n, 256, keys), BF16),
            pltpu.VMEM((n, keys, lanes), F32),
            pltpu.VMEM((n, keys, lanes), F32),
            pltpu.VMEM((lanes, 128), BF16),
            pltpu.VMEM((lanes, 128), BF16),
            pltpu.VMEM((2, n, keys, 128), F32),
            pltpu.VMEM((2, 2, n // 2, keys, 128), F32),
            pltpu.VMEM((n, SLOTS, 256), F32),
            pltpu.VMEM((n, SLOTS, 256), F32),
            pltpu.VMEM((n, SLOTS, 256), BF16),
            pltpu.VMEM((SLOTS, width), BF16),
            pltpu.VMEM((n, SLOTS, keys), BF16),
            pltpu.VMEM((keys, keys), BF16),
            pltpu.VMEM((n, SLOTS, 256), F32),
            pltpu.VMEM((n, SLOTS, 256), F32),
            pltpu.VMEM((n_dp, SLOTS, 256), F32),
            pltpu.VMEM((n, 1, width), F32),
            pltpu.VMEM((n, 1, width), F32),
            pltpu.VMEM((n_dp, 1, width), F32),
            pltpu.VMEM((SLOTS, width), F32),
            pltpu.VMEM((SLOTS, width), BF16),
            pltpu.VMEM((SLOTS, width), BF16),
            pltpu.VMEM((2, SLOTS, half_heads + 128), BF16),
            pltpu.VMEM((SLOTS, width), F32),
            dma((2, n)),
            dma((2, n)),
            dma((2, n // 2, 2, max(PIECES))),
            dma((2, n // 2, 2, max(PIECES))),
            dma((2, n)),
            dma((2, n)),
            dma((8, n)),
            dma((8, n)),
            dma((2, 2, n // 2)),
            dma((2, 2, n // 2)),
            dma((2, n_dp)),
            dma((2, n_dp)),
        ],
        compiler_params=pltpu.CompilerParams(
            collective_id=0, has_side_effects=True, vmem_limit_bytes=58 * 1024 * 1024
        ),
    )(
        hidden, cotangent, picks, gain.reshape(1, -1), router.reshape(1, -1), w_query, w_kv, w_out
    )
    mixed, input_grad, kv_grad, router_grad = outs
    return mixed, input_grad, kv_grad, router_grad.reshape(-1)


def solution(mesh):
    rows = P("dp", "seq", None)
    weight = P("seq", None)
    return jax.shard_map(
        local,
        mesh=mesh,
        in_specs=(rows, rows, P("dp", "seq"), P(), P(), weight, weight, weight),
        out_specs=(rows, rows, weight, P("seq")),
        check_vma=False,
    )
```

```python
import functools
import math

import jax
import jax.numpy as jnp
from jax import lax
from jax.experimental import pallas as pl
from jax.experimental.pallas import tpu as pltpu
from jax.sharding import PartitionSpec as P

MESH = pl.DeviceIdType.MESH
EPSILON = 1e-05
SLOTS = 32
HEAD = 64
F32, BF16 = jnp.float32, jnp.bfloat16
KEY_MARK = 2.0**100
KEY_BOUND = 2.0**64
NEGATIVE = -1e30
FAR = 1 << 30
PIECES = (2, 2)


def dot(left, right, left_dim=1, right_dim=0):
    return lax.dot_general(
        left, right, (((left_dim,), (right_dim,)), ((), ())), preferred_element_type=F32
    )


def copy_to(source, target, send_sem, recv_sem, device):
    return pltpu.make_async_remote_copy(
        src_ref=source,
        dst_ref=target,
        send_sem=send_sem,
        recv_sem=recv_sem,
        device_id=device,
        device_id_type=MESH,
    )


def kernel(
    n, n_dp, width, group_heads,
    hid, cot, picks, gain, router, wq, wkv, wo,
    mixed_out, igrad_out, kvgrad_out, rgrad_out,
    wquery, wout, wkeys, kv, kvt, scores, dprobs, qpad, opad, dkv, got_dkv, part, got_part,
    gkv, normed, slices, normed_t, share, got_share, total, row_a, row_b, row_d,
    block, block_grad, block_out, dqkv, upstream,
    p1_send, p1_recv, ring_send, ring_recv, sib_send, sib_recv,
    x_send, x_recv, rs_send, rs_recv, d_send, d_recv,
):
    seq, dp = lax.axis_index("seq"), lax.axis_index("dp")
    core = lax.rem(dp, 2)
    y, z = lax.div(seq, n), lax.rem(seq, n)
    a = z + core * (y - z)
    b = y + core * (z - y)
    keys = n * SLOTS
    half_heads = group_heads * HEAD
    lanes = 2 * group_heads * SLOTS
    half_width = width // 2
    chunk = keys

    def seq_of(b_, a_):
        return (1 - core) * (b_ * n + a_) + core * (a_ * n + b_)

    def peer_a(j):
        return (dp, seq_of(b, lax.rem(a + j, n)))

    def peer_b(j):
        return (dp, seq_of(lax.rem(b + j, n), a))

    def peer_y(j):
        return (dp, lax.rem(y + j, n) * n + z)

    def peer_z(j):
        return (dp, y * n + lax.rem(z + j, n))

    def peer_d(j):
        return (lax.rem(dp + j, n_dp), seq)

    sibling = (dp + 1 - 2 * core, seq)

    def each(count, body):
        def step(j, carry):
            body(j)
            return carry

        lax.fori_loop(0, count, step, 0)

    def others(count, body):
        def step(j, carry):
            body(j)
            return carry

        lax.fori_loop(1, count, step, 0)

    barrier = pltpu.get_barrier_semaphore()

    def greet(device):
        pl.semaphore_signal(barrier, inc=1, device_id=device, device_id_type=MESH)

    others(n, lambda j: greet(peer_a(j)))
    others(n, lambda j: greet(peer_b(j)))
    others(n_dp, lambda j: greet(peer_d(j)))

    for side in (0, 1):

        @pl.when(core == side)
        def _():
            cols = slice(side * half_heads, (side + 1) * half_heads)
            wquery[side, y, z] = wq[:, cols]
            wkeys[side, y, z] = wkv[:, side * 128 : (side + 1) * 128]
            wout[side, y, z] = wo[:, side * half_width : (side + 1) * half_width]

    tokens = hid.shape[1]
    row_id = lax.broadcasted_iota(jnp.int32, (tokens, tokens), 0)
    col_id = lax.broadcasted_iota(jnp.int32, (tokens, tokens), 1)
    pick_row = picks[...].astype(F32)
    pick_wide = jnp.broadcast_to(pick_row, (tokens, tokens))
    pick_col = jnp.sum(jnp.where(row_id == col_id, pick_wide, 0.0), axis=1, keepdims=True)
    rank_col = jnp.sum(jnp.where(col_id < row_id, pick_wide, 0.0), axis=1, keepdims=True)
    pick_tall = jnp.broadcast_to(pick_col, (tokens, tokens))
    rank_row = jnp.sum(jnp.where(row_id < col_id, pick_tall, 0.0), axis=0, keepdims=True)
    slot_row = lax.broadcasted_iota(jnp.int32, (SLOTS, tokens), 0).astype(F32)
    slot_col = lax.broadcasted_iota(jnp.int32, (tokens, SLOTS), 1).astype(F32)
    pack = jnp.where((slot_row == rank_row) & (pick_row > 0.5), 1.0, 0.0)
    spread = jnp.where((slot_col == rank_col) & (pick_col > 0.5), 1.0, 0.0).astype(BF16)
    used = jnp.sum(pack, axis=1, keepdims=True)
    pack = pack.astype(BF16)

    n_chunks = width // chunk

    def at(i):
        return pl.ds(pl.multiple_of(i * chunk, chunk), chunk)

    def gate_step(i, acc):
        return acc + hid[0, :, at(i)].astype(F32) * router[:, at(i)]

    logit = lax.fori_loop(0, n_chunks, gate_step, jnp.zeros((tokens, chunk), F32))
    gate = jax.nn.sigmoid(jnp.sum(logit, axis=1, keepdims=True))

    pl.semaphore_wait(barrier, 2 * (n - 1) + n_dp - 1)

    outgoing = []

    def first(which, ref):
        def make(j):
            own = ref.at[core, y, z]
            return copy_to(own, own, p1_send.at[which, j], p1_recv.at[which, j], peer_a(j))

        return make

    def along(peer, which, source, target):
        def make(j):
            return copy_to(source(j), target, x_send.at[which, j], x_recv.at[which, j], peer(j))

        return make

    def along_d(which, ref):
        def make(j):
            return copy_to(
                ref.at[dp], ref.at[dp], d_send.at[which, j], d_recv.at[which, j], peer_d(j)
            )

        return make

    def start(make, count=n):
        others(count, lambda j: make(j).start())
        outgoing.append(lambda: sent(make, count))

    def arrived(make, count=n):
        others(count, lambda j: make(j).wait_recv())

    def sent(make, count=n):
        others(count, lambda j: make(j).wait_send())

    last = n // 2 - 1

    def slab(ref, side, k, which=0, piece=None):
        size = n // PIECES[which]
        rows = slice(None) if piece is None else pl.ds(piece * size, size)
        return ref.at[0, k, rows] if side == 0 else ref.at[1, rows, k]

    def goes(which, step, way, piece):
        return step < last or (piece < PIECES[which] // 2) == (way == 0)

    def ring_start(which, ref, step, piece):
        for side in (0, 1):

            @pl.when(core == side)
            def _():
                for way, block_id, device in (
                    (0, lax.rem(b + n - step, n), peer_b(1)),
                    (1, lax.rem(b + step, n), peer_b(n - 1)),
                ):
                    if goes(which, step, way, piece):
                        rows = slab(ref, side, block_id, which, piece)
                        copy_to(
                            rows,
                            rows,
                            ring_send.at[which, step, way, piece],
                            ring_recv.at[which, step, way, piece],
                            device,
                        ).start()

        for way in (0, 1):
            if goes(which, step, way, piece):
                outgoing.append(
                    lambda way=way: ring_copy(which, ref, step, way, piece).wait_send()
                )

    def ring_copy(which, ref, step, way, piece):
        rows = slab(ref, 0, 0, which, piece)
        return copy_to(
            rows,
            rows,
            ring_send.at[which, step, way, piece],
            ring_recv.at[which, step, way, piece],
            peer_b(1),
        )

    def sib_start(which, ref, slot, block_id):
        for side in (0, 1):

            @pl.when(core == side)
            def _():
                rows = slab(ref, side, block_id)
                copy_to(
                    rows, rows, sib_send.at[which, slot], sib_recv.at[which, slot], sibling
                ).start()

        outgoing.append(lambda: sib_copy(which, ref, slot).wait_send())

    def sib_copy(which, ref, slot):
        rows = slab(ref, 0, 0)
        return copy_to(rows, rows, sib_send.at[which, slot], sib_recv.at[which, slot], sibling)

    def pass_first(which, ref):
        for piece in range(PIECES[which]):
            ring_start(which, ref, 0, piece)
        sib_start(which, ref, 0, b)

    def pass_on(which, ref, step):
        for piece in range(PIECES[which]):
            for way in (0, 1):
                if goes(which, step, way, piece):
                    ring_copy(which, ref, step, way, piece).wait_recv()
            if step < last:
                ring_start(which, ref, step + 1, piece)
        sib_start(which, ref, 1 + 2 * step, lax.rem(b + n - 1 - step, n))
        if step < last:
            sib_start(which, ref, 2 + 2 * step, lax.rem(b + 1 + step, n))

    start(first(2, wkeys))
    start(first(0, wquery))

    def pack_step(i, acc):
        rows = dot(pack, hid[0, :, at(i)])
        block[:, at(i)] = rows
        scaled = (gate * cot[0, :, at(i)].astype(F32)).astype(BF16)
        block_grad[:, at(i)] = dot(pack, scaled).astype(BF16)
        return acc + rows * rows

    squares = lax.fori_loop(0, n_chunks, pack_step, jnp.zeros((SLOTS, chunk), F32))
    inv_norm = lax.rsqrt(jnp.sum(squares, axis=1, keepdims=True) * (1.0 / width) + EPSILON)

    def norm_step(i):
        normed[:, at(i)] = (block[:, at(i)] * inv_norm * gain[:, at(i)]).astype(BF16)

    each(n_chunks, norm_step)

    slices[y] = normed[:, at(y)]
    send_slices = along(peer_y, 5, lambda j: normed.at[:, at(lax.rem(y + j, n))], slices.at[y])

    def keys_copy(side, block_id, j):
        rows = slab(wkeys, side, block_id)
        return copy_to(rows, rows, x_send.at[8, j], x_recv.at[8, j], peer_b(j))

    def keys_start():
        for side in (0, 1):

            @pl.when(core == side)
            def _():
                others(n, lambda j: keys_copy(side, b, j).start())

        outgoing.append(lambda: others(n, lambda j: keys_copy(0, 0, j).wait_send()))

    def keys_arrived(t):
        after, odd = lax.div(t, 2), lax.rem(t, 2)
        j = (1 - odd) * (1 + after) + odd * (n - 1 - after)
        keys_copy(0, 0, j).wait_recv()
        for side in (0, 1):

            @pl.when(core == side)
            def _():
                rows = slab(wkeys, side, lax.rem(b + n - j, n))
                copy_to(
                    rows, rows, sib_send.at[2, t + 1], sib_recv.at[2, t + 1], sibling
                ).start()

    arrived(first(2, wkeys))
    keys_start()
    sib_start(2, wkeys, 0, b)
    arrived(first(0, wquery))
    pass_first(0, wquery)
    start(first(1, wout))
    each(n - 1, keys_arrived)
    outgoing.append(
        lambda: others(n, lambda slot: sib_copy(2, wkeys, slot).wait_send())
    )
    each(n, lambda slot: sib_copy(2, wkeys, slot).wait_recv())

    def project(ref, side):
        def step(i, acc):
            return acc + dot(normed[:, at(i)], ref[side, i].reshape(chunk, -1))

        zero = jnp.zeros((SLOTS, ref.shape[-1]), F32)
        return lax.fori_loop(0, n_chunks, step, zero).astype(BF16)

    lane_id = lax.broadcasted_iota(jnp.int32, (SLOTS, 128), 1)
    own_keys = project(wkeys, 0).astype(F32)
    own_keys = jnp.where((lane_id == 0) & (used < 0.5), KEY_MARK, own_keys)
    kv[b, a, :, :128] = own_keys.astype(BF16)
    kv[b, a, :, 128:] = project(wkeys, 1)
    kv_first = along(peer_a, 0, lambda j: kv.at[b, a], kv.at[b, a])
    kv_second = along(peer_b, 1, lambda j: kv.at[b], kv.at[b])
    start(kv_first)
    pass_on(0, wquery, 0)
    arrived(first(1, wout))
    pass_first(1, wout)
    arrived(kv_first)
    start(kv_second)
    start(send_slices)
    for which, ref, step in (
        (0, wquery, 1),
        (1, wout, 0),
        (0, wquery, 2),
        (1, wout, 1),
        (0, wquery, 3),
    ):
        if step <= last:
            pass_on(which, ref, step)
    for slot in range(n):
        sib_copy(0, wquery, slot).wait_recv()

    low_lane = lax.broadcasted_iota(jnp.int32, (SLOTS, 128), 1) < HEAD

    def pad_heads(ref, rows, group):
        for i in range(group_heads // 2):
            pair = rows[:, i * 128 : (i + 1) * 128]
            for parity in (0, 1):
                moved = pair if parity == group else pltpu.roll(pair, HEAD, 1)
                kept = jnp.where(low_lane, moved, 0.0) if group == 0 else jnp.where(low_lane, 0.0, moved)
                at_row = (group * group_heads + 2 * i + parity) * SLOTS
                ref[at_row : at_row + SLOTS, :] = kept.astype(BF16)

    def join_heads(both):
        tall = jnp.transpose(both)
        groups = []
        for group in (0, 1):
            pairs = []
            for i in range(group_heads // 2):
                at_row = (group * group_heads + 2 * i) * SLOTS
                even = tall[at_row : at_row + SLOTS, :]
                odd = tall[at_row + SLOTS : at_row + 2 * SLOTS, :]
                if group == 0:
                    pairs.append(jnp.where(low_lane, even, pltpu.roll(odd, HEAD, 1)))
                else:
                    pairs.append(jnp.where(low_lane, pltpu.roll(even, HEAD, 1), odd))
            groups.append(jnp.concatenate(pairs, axis=1))
        return groups

    for group in (0, 1):
        pad_heads(qpad, project(wquery, group).astype(F32), group)

    key_row = lax.broadcasted_iota(jnp.int32, (keys, 1), 0)
    query_at = seq * SLOTS + (lax.broadcasted_iota(jnp.int32, (1, lanes), 1) & (SLOTS - 1))
    scale = HEAD**-0.5

    def score_step(i, top):
        rows = kv[i].reshape(keys, 256).astype(F32)
        kvt[i] = jnp.transpose(rows).astype(BF16)
        key_at = seq_of(i, key_row >> 5) * SLOTS + (key_row & (SLOTS - 1))
        key_at = jnp.where(rows[:, 0:1] < KEY_BOUND, key_at, FAR)
        s = dot(rows[:, :128].astype(BF16), qpad[...], 1, 1) * scale
        s = jnp.where(key_at <= query_at, s, NEGATIVE)
        scores[i] = s
        return jnp.maximum(top, jnp.max(s, axis=0, keepdims=True))

    top = score_step(b, jnp.full((1, lanes), NEGATIVE, F32))

    def next_score_step(t, top):
        after, odd = lax.div(t, 2), lax.rem(t, 2)
        j = (1 - odd) * (1 + after) + odd * (n - 1 - after)
        kv_second(j).wait_recv()
        return score_step(lax.rem(b + n - j, n), top)

    top = lax.fori_loop(0, n - 1, next_score_step, top)

    for step in range(2, last + 1):
        pass_on(1, wout, step)
    for slot in range(n):
        sib_copy(1, wout, slot).wait_recv()

    out_rows = n * wout.shape[3]

    def out_at(i):
        return pl.ds(pl.multiple_of(i * out_rows, out_rows), out_rows)

    def head_grad_step(i):
        acc = jnp.zeros((SLOTS, out_rows), F32)
        for side in (0, 1):
            part_grad = block_grad[:, side * half_width : (side + 1) * half_width]
            acc += dot(part_grad, wout[side, i].reshape(out_rows, half_width), 1, 1)
        upstream[:, out_at(i)] = acc

    each(n, head_grad_step)
    for group in (0, 1):
        rows = upstream[:, group * half_heads : (group + 1) * half_heads]
        pad_heads(opad, rows, group)

    def exp_step(i, carry):
        total_exp, inner = carry
        e = jnp.exp(scores[i] - top)
        scores[i] = e
        grads = dot(kv[i].reshape(keys, 256)[:, 128:], opad[...], 1, 1)
        dprobs[i] = grads
        total_exp += jnp.sum(e, axis=0, keepdims=True)
        return total_exp, inner + jnp.sum(e * grads, axis=0, keepdims=True)

    zero = jnp.zeros((1, lanes), F32)
    total_exp, inner = lax.fori_loop(0, n, exp_step, (zero, zero))
    inv_sum = 1.0 / total_exp
    inner = inner * inv_sum

    def rs_slab(step, way):
        return lax.rem(b + n + (1 - 2 * way) * (n // 2 - step), n)

    def rs_copy(step, way, kind):
        return copy_to(
            dkv.at[kind, rs_slab(step, way)],
            got_dkv.at[way, kind, step],
            rs_send.at[way, kind, step],
            rs_recv.at[way, kind, step],
            peer_b(1 + way * (n - 2)),
        )

    def rs_start(step, way, kind):
        rs_copy(step, way, kind).start()
        outgoing.append(lambda: rs_copy(step, way, kind).wait_send())

    def grad_step(t, carry):
        mixed_t, query_t = carry
        i = rs_slab(lax.div(t + 1, 2), 1 - lax.rem(t, 2))
        p = scores[i] * inv_sum
        half = p.astype(BF16)
        ds = (p * (dprobs[i] - inner)).astype(BF16)
        dkv[0, i] = dot(ds, qpad[...]) * scale
        dkv[1, i] = dot(half, opad[...])

        @pl.when(t == 0)
        def _():
            rs_copy(0, 0, 0).start()
            rs_copy(0, 1, 1).start()

        return mixed_t + dot(kvt[i, 128:, :], half), query_t + dot(kvt[i, :128, :], ds)

    zero = jnp.zeros((128, lanes), F32)
    mixed_t, query_t = lax.fori_loop(0, n, grad_step, (zero, zero))
    outgoing.append(lambda: rs_copy(0, 0, 0).wait_send())
    outgoing.append(lambda: rs_copy(0, 1, 1).wait_send())

    def rs_step(step):
        for way in (0, 1):
            for kind in (0, 1):
                if step > 1 or kind == way:
                    rs_copy(step - 1, way, kind).wait_recv()
                    dkv[kind, rs_slab(step, way)] += got_dkv[way, kind, step - 1]
                rs_start(step, way, kind)

    rs_step(1)

    heads = jnp.concatenate(join_heads(mixed_t), axis=1).astype(BF16)
    for side in (0, 1):
        rows = wout[side].reshape(n * out_rows, half_width)
        block_out[:, side * half_width : (side + 1) * half_width] = dot(heads, rows).astype(BF16)

    if last > 1:
        rs_step(2)

    def mix_step(i, acc):
        out_tokens = dot(spread, block_out[:, at(i)])
        mixed_out[0, :, at(i)] = (hid[0, :, at(i)].astype(F32) + gate * out_tokens).astype(BF16)
        return acc + cot[0, :, at(i)].astype(F32) * out_tokens

    through = lax.fori_loop(0, n_chunks, mix_step, jnp.zeros((tokens, chunk), F32))
    through = jnp.sum(through, axis=1, keepdims=True)
    grad_logit = through * gate * (1.0 - gate)

    def router_step(i):
        term = hid[0, :, at(i)].astype(F32) * grad_logit
        row_a[a, :, at(i)] = jnp.sum(term, axis=0, keepdims=True)

    each(n_chunks, router_step)
    router_first = along(peer_a, 2, lambda j: row_a.at[a], row_a.at[a])
    router_second = along(peer_b, 3, lambda j: row_b.at[b], row_b.at[b])
    router_third = along_d(0, row_d)
    start(router_first)

    for group, rows in enumerate(join_heads(query_t * scale)):
        dqkv[group, :, :half_heads] = rows.astype(BF16)
    for step in range(3, last + 1):
        rs_step(step)
    arrived(send_slices)
    normed_t[...] = jnp.transpose(slices[...].reshape(keys, chunk).astype(F32)).astype(BF16)

    for kind in (0, 1):
        mine = dkv[kind, b]
        for way in (0, 1):
            rs_copy(last, way, kind).wait_recv()
            mine += got_dkv[way, kind, last]
        part[:, :, kind * 128 : (kind + 1) * 128] = mine.reshape(n, SLOTS, 128)
    send_part = along(peer_a, 4, lambda j: part.at[lax.rem(a + j, n)], got_part.at[a])
    start(send_part)
    arrived(router_first)
    row_b[b] = jnp.sum(row_a[...], axis=0)
    start(router_second)
    arrived(send_part)
    own = part[a]
    own = lax.fori_loop(1, n, lambda j, acc: acc + got_part[lax.rem(a + j, n)], own)
    grad_kv = own.astype(BF16)
    gkv[y] = grad_kv
    gkv_gather = along(peer_y, 6, lambda j: gkv.at[y], gkv.at[y])
    start(gkv_gather)
    dqkv[0, :, half_heads:] = grad_kv[:, :128]
    dqkv[1, :, half_heads:] = grad_kv[:, 128:]

    def back_step(i, acc):
        grads = jnp.zeros((SLOTS, chunk), F32)
        for side in (0, 1):
            grads += dot(dqkv[side, :, :half_heads], wquery[side, i].reshape(chunk, -1), 1, 1)
            grads += dot(dqkv[side, :, half_heads:], wkeys[side, i].reshape(chunk, -1), 1, 1)
        u = grads * gain[:, at(i)]
        upstream[:, at(i)] = u
        return acc + u * block[:, at(i)]

    overlap = lax.fori_loop(0, n_chunks, back_step, jnp.zeros((SLOTS, chunk), F32))
    overlap = jnp.sum(overlap, axis=1, keepdims=True) * (1.0 / width)

    arrived(gkv_gather)
    share[...] = dot(normed_t[...], gkv[...].reshape(keys, 256)).reshape(n, SLOTS, 256)
    send_share = along(peer_z, 7, lambda j: share.at[lax.rem(z + j, n)], got_share.at[z])
    start(send_share)

    arrived(router_second)
    row_d[dp] = jnp.sum(row_b[...], axis=0)
    start(router_third, n_dp)

    cubed = inv_norm * inv_norm * inv_norm * overlap

    def input_step(i):
        rows = inv_norm * upstream[:, at(i)] - block[:, at(i)] * cubed
        tokens_grad = dot(spread, rows.astype(BF16))
        grads = cot[0, :, at(i)].astype(F32) + grad_logit * router[:, at(i)] + tokens_grad
        igrad_out[0, :, at(i)] = grads.astype(BF16)

    each(n_chunks, input_step)

    arrived(send_share)
    own = share[z]
    own = lax.fori_loop(1, n, lambda j, acc: acc + got_share[lax.rem(z + j, n)], own)
    total[dp] = own
    send_total = along_d(1, total)
    start(send_total, n_dp)
    arrived(router_third, n_dp)
    row = jnp.sum(row_d[...], axis=0)
    per_tile = 128 // SLOTS
    tile = jnp.zeros((1, SLOTS), F32)
    for i in range(width // SLOTS):
        tile = jnp.where(seq == i, row[:, i * SLOTS : (i + 1) * SLOTS], tile)
    rgrad_out[...] = tile
    arrived(send_total, n_dp)
    kvgrad_out[...] = jnp.sum(total[...], axis=0)

    for wait in outgoing:
        wait()


def local(hidden, cotangent, picks, gain, router, w_query, w_kv, w_out):
    n_dp, n_seq = lax.axis_size("dp"), lax.axis_size("seq")
    n = math.isqrt(n_seq)
    tokens, width = hidden.shape[1:]
    half_heads = w_query.shape[1] // 2
    group_heads = half_heads // HEAD
    out_slab = w_out.shape[0]
    keys = n * SLOTS
    lanes = 2 * group_heads * SLOTS
    vmem = pl.BlockSpec(memory_space=pltpu.VMEM)
    dma = pltpu.SemaphoreType.DMA
    outs = pl.pallas_call(
        functools.partial(kernel, n, n_dp, width, group_heads),
        out_shape=(
            jax.ShapeDtypeStruct(hidden.shape, BF16),
            jax.ShapeDtypeStruct(hidden.shape, BF16),
            jax.ShapeDtypeStruct((SLOTS, 256), F32),
            jax.ShapeDtypeStruct((1, SLOTS), F32),
        ),
        in_specs=[vmem] * 8,
        out_specs=(vmem,) * 4,
        scratch_shapes=[
            pltpu.VMEM((2, n, n, SLOTS, half_heads), BF16),
            pltpu.VMEM((2, n, n, out_slab, width // 2), BF16),
            pltpu.VMEM((2, n, n, SLOTS, 128), BF16),
            pltpu.VMEM((n, n, SLOTS, 256), BF16),
            pltpu.VMEM((n, 256, keys), BF16),
            pltpu.VMEM((n, keys, lanes), F32),
            pltpu.VMEM((n, keys, lanes), F32),
            pltpu.VMEM((lanes, 128), BF16),
            pltpu.VMEM((lanes, 128), BF16),
            pltpu.VMEM((2, n, keys, 128), F32),
            pltpu.VMEM((2, 2, n // 2, keys, 128), F32),
            pltpu.VMEM((n, SLOTS, 256), F32),
            pltpu.VMEM((n, SLOTS, 256), F32),
            pltpu.VMEM((n, SLOTS, 256), BF16),
            pltpu.VMEM((SLOTS, width), BF16),
            pltpu.VMEM((n, SLOTS, keys), BF16),
            pltpu.VMEM((keys, keys), BF16),
            pltpu.VMEM((n, SLOTS, 256), F32),
            pltpu.VMEM((n, SLOTS, 256), F32),
            pltpu.VMEM((n_dp, SLOTS, 256), F32),
            pltpu.VMEM((n, 1, width), F32),
            pltpu.VMEM((n, 1, width), F32),
            pltpu.VMEM((n_dp, 1, width), F32),
            pltpu.VMEM((SLOTS, width), F32),
            pltpu.VMEM((SLOTS, width), BF16),
            pltpu.VMEM((SLOTS, width), BF16),
            pltpu.VMEM((2, SLOTS, half_heads + 128), BF16),
            pltpu.VMEM((SLOTS, width), F32),
            dma((3, n)),
            dma((3, n)),
            dma((2, n // 2, 2, max(PIECES))),
            dma((2, n // 2, 2, max(PIECES))),
            dma((3, n)),
            dma((3, n)),
            dma((9, n)),
            dma((9, n)),
            dma((2, 2, n // 2)),
            dma((2, 2, n // 2)),
            dma((2, n_dp)),
            dma((2, n_dp)),
        ],
        compiler_params=pltpu.CompilerParams(
            collective_id=0, has_side_effects=True, vmem_limit_bytes=58 * 1024 * 1024
        ),
    )(
        hidden, cotangent, picks, gain.reshape(1, -1), router.reshape(1, -1), w_query, w_kv, w_out
    )
    mixed, input_grad, kv_grad, router_grad = outs
    return mixed, input_grad, kv_grad, router_grad.reshape(-1)


def solution(mesh):
    rows = P("dp", "seq", None)
    weight = P("seq", None)
    return jax.shard_map(
        local,
        mesh=mesh,
        in_specs=(rows, rows, P("dp", "seq"), P(), P(), weight, weight, weight),
        out_specs=(rows, rows, weight, P("seq")),
        check_vma=False,
    )
```

```python
import functools
import math

import jax
import jax.numpy as jnp
from jax import lax
from jax.experimental import pallas as pl
from jax.experimental.pallas import tpu as pltpu
from jax.sharding import PartitionSpec as P

MESH = pl.DeviceIdType.MESH
EPSILON = 1e-05
SLOTS = 32
HEAD = 64
F32, BF16 = jnp.float32, jnp.bfloat16
KEY_MARK = 2.0**100
KEY_BOUND = 2.0**64
NEGATIVE = -1e30
FAR = 1 << 30
PIECES = 4


def dot(left, right, left_dim=1, right_dim=0):
    return lax.dot_general(
        left, right, (((left_dim,), (right_dim,)), ((), ())), preferred_element_type=F32
    )


def copy_to(source, target, send_sem, recv_sem, device):
    return pltpu.make_async_remote_copy(
        src_ref=source,
        dst_ref=target,
        send_sem=send_sem,
        recv_sem=recv_sem,
        device_id=device,
        device_id_type=MESH,
    )


def kernel(
    n, n_dp, width, group_heads,
    hid, cot, picks, gain, router, wq, wkv, wo,
    mixed_out, igrad_out, kvgrad_out, rgrad_out,
    wproj, wout, kv, kvt, scores, dprobs, qpad, opad, dkv, got_dkv, part, got_part,
    gkv, normed, slices, normed_t, share, pair, got_share, total, final, row_a, row_b, row_d,
    block, block_grad, block_out, dqkv, upstream,
    p1_send, p1_recv, ring_send, ring_recv, sib_send, sib_recv,
    x_send, x_recv, rs_send, rs_recv, d_send, d_recv, o_send, o_recv, t_send, t_recv,
):
    seq, dp = lax.axis_index("seq"), lax.axis_index("dp")
    core = lax.rem(dp, 2)
    y, z = lax.div(seq, n), lax.rem(seq, n)
    a = z + core * (y - z)
    b = y + core * (z - y)
    keys = n * SLOTS
    half_heads = group_heads * HEAD
    lanes = 2 * group_heads * SLOTS
    chips = n_dp // 2
    out_cols = width // n_dp
    chunk = keys

    def seq_of(b_, a_):
        return (1 - core) * (b_ * n + a_) + core * (a_ * n + b_)

    def peer_a(j):
        return (dp, seq_of(b, lax.rem(a + j, n)))

    def peer_b(j):
        return (dp, seq_of(lax.rem(b + j, n), a))

    def peer_y(j):
        return (dp, lax.rem(y + j, n) * n + z)

    def peer_z(j):
        return (dp, y * n + lax.rem(z + j, n))

    def peer_x(j):
        return (lax.rem(dp + 2 * j, n_dp), seq)

    def peer_d(j):
        return (lax.rem(dp + j, n_dp), seq)

    sibling = (dp + 1 - 2 * core, seq)

    def each(count, body):
        def step(j, carry):
            body(j)
            return carry

        lax.fori_loop(0, count, step, 0)

    def others(count, body):
        def step(j, carry):
            body(j)
            return carry

        lax.fori_loop(1, count, step, 0)

    barrier = pltpu.get_barrier_semaphore()

    def greet(device):
        pl.semaphore_signal(barrier, inc=1, device_id=device, device_id_type=MESH)

    others(n, lambda j: greet(peer_a(j)))
    others(n, lambda j: greet(peer_b(j)))
    others(n_dp, lambda j: greet(peer_d(j)))

    for side in (0, 1):

        @pl.when(core == side)
        def _():
            cols = slice(side * half_heads, (side + 1) * half_heads)
            wproj[side, y, z, :, :half_heads] = wq[:, cols]
            wproj[side, y, z, :, half_heads:] = wkv[:, side * 128 : (side + 1) * 128]

    def cols_of(d):
        return pl.ds(pl.multiple_of(d * out_cols, out_cols), out_cols)

    wout[dp, y, z] = wo[:, cols_of(dp)]

    tokens = hid.shape[1]
    row_id = lax.broadcasted_iota(jnp.int32, (tokens, tokens), 0)
    col_id = lax.broadcasted_iota(jnp.int32, (tokens, tokens), 1)
    pick_row = picks[...].astype(F32)
    pick_wide = jnp.broadcast_to(pick_row, (tokens, tokens))
    pick_col = jnp.sum(jnp.where(row_id == col_id, pick_wide, 0.0), axis=1, keepdims=True)
    rank_col = jnp.sum(jnp.where(col_id < row_id, pick_wide, 0.0), axis=1, keepdims=True)
    pick_tall = jnp.broadcast_to(pick_col, (tokens, tokens))
    rank_row = jnp.sum(jnp.where(row_id < col_id, pick_tall, 0.0), axis=0, keepdims=True)
    slot_row = lax.broadcasted_iota(jnp.int32, (SLOTS, tokens), 0).astype(F32)
    slot_col = lax.broadcasted_iota(jnp.int32, (tokens, SLOTS), 1).astype(F32)
    pack = jnp.where((slot_row == rank_row) & (pick_row > 0.5), 1.0, 0.0)
    spread = jnp.where((slot_col == rank_col) & (pick_col > 0.5), 1.0, 0.0).astype(BF16)
    used = jnp.sum(pack, axis=1, keepdims=True)
    pack = pack.astype(BF16)

    n_chunks = width // chunk

    def at(i):
        return pl.ds(pl.multiple_of(i * chunk, chunk), chunk)

    def gate_step(i, acc):
        return acc + hid[0, :, at(i)].astype(F32) * router[:, at(i)]

    logit = lax.fori_loop(0, n_chunks, gate_step, jnp.zeros((tokens, chunk), F32))
    gate = jax.nn.sigmoid(jnp.sum(logit, axis=1, keepdims=True))

    pl.semaphore_wait(barrier, 2 * (n - 1) + n_dp - 1)

    outgoing = []

    def first(which, own):
        def make(j):
            return copy_to(own, own, p1_send.at[which, j], p1_recv.at[which, j], peer_a(j))

        return make

    def along(peer, which, source, target):
        def make(j):
            return copy_to(source(j), target, x_send.at[which, j], x_recv.at[which, j], peer(j))

        return make

    def along_d(which, ref):
        def make(j):
            return copy_to(
                ref.at[dp], ref.at[dp], d_send.at[which, j], d_recv.at[which, j], peer_d(j)
            )

        return make

    def start(make, count=n):
        others(count, lambda j: make(j).start())
        outgoing.append(lambda: sent(make, count))

    def arrived(make, count=n):
        others(count, lambda j: make(j).wait_recv())

    def sent(make, count=n):
        others(count, lambda j: make(j).wait_send())

    last = n // 2 - 1

    def slab(side, k, piece=None):
        size = n // PIECES
        rows = slice(None) if piece is None else pl.ds(piece * size, size)
        return wproj.at[0, k, rows] if side == 0 else wproj.at[1, rows, k]

    def goes(step, way, piece):
        return step < last or (piece < PIECES // 2) == (way == 0)

    def ring_copy(step, way, piece, rows, device):
        return copy_to(
            rows, rows, ring_send.at[step, way, piece], ring_recv.at[step, way, piece], device
        )

    def any_ring_copy(step, way, piece):
        return ring_copy(step, way, piece, slab(0, 0, piece), peer_b(1))

    def ring_start(step, piece):
        for side in (0, 1):

            @pl.when(core == side)
            def _():
                for way, block_id, device in (
                    (0, lax.rem(b + n - step, n), peer_b(1)),
                    (1, lax.rem(b + step, n), peer_b(n - 1)),
                ):
                    if goes(step, way, piece):
                        ring_copy(step, way, piece, slab(side, block_id, piece), device).start()

        for way in (0, 1):
            if goes(step, way, piece):
                outgoing.append(lambda way=way: any_ring_copy(step, way, piece).wait_send())

    def sib_copy(which, slot, rows):
        return copy_to(rows, rows, sib_send.at[which, slot], sib_recv.at[which, slot], sibling)

    def any_sib_copy(which, slot):
        return sib_copy(which, slot, slab(0, 0) if which == 0 else wout.at[0])

    def sib_start(slot, block_id):
        for side in (0, 1):

            @pl.when(core == side)
            def _():
                sib_copy(0, slot, slab(side, block_id)).start()

        outgoing.append(lambda: any_sib_copy(0, slot).wait_send())

    def pass_on(step):
        for piece in range(PIECES):
            for way in (0, 1):
                if goes(step, way, piece):
                    any_ring_copy(step, way, piece).wait_recv()
            if step < last:
                ring_start(step + 1, piece)
        sib_start(1 + 2 * step, lax.rem(b + n - 1 - step, n))
        if step < last:
            sib_start(2 + 2 * step, lax.rem(b + 1 + step, n))

    out_first = first(1, wout.at[dp, y, z])

    def out_second(side, j):
        rows = wout.at[dp, b] if side == 0 else wout.at[dp, :, b]
        return copy_to(rows, rows, x_send.at[8, j], x_recv.at[8, j], peer_b(j))

    def out_second_start():
        for side in (0, 1):

            @pl.when(core == side)
            def _():
                others(n, lambda j: out_second(side, j).start())

        outgoing.append(lambda: others(n, lambda j: out_second(0, j).wait_send()))

    last_x = chips // 2 - 1

    def out_block(distance):
        return lax.rem(dp + 2 * n_dp + 2 * distance, n_dp)

    def out_copy(step, way):
        rows = wout.at[out_block((2 * way - 1) * step)]
        if step == last_x:
            rows = rows.at[pl.ds(way * (n // 2), n // 2)]
        device = peer_x(1 if way == 0 else chips - 1)
        return copy_to(rows, rows, o_send.at[step, way], o_recv.at[step, way], device)

    def out_start(step):
        for way in (0, 1):
            out_copy(step, way).start()
            outgoing.append(lambda way=way: out_copy(step, way).wait_send())

    def out_sib(slot, distance):
        sib_copy(1, slot, wout.at[out_block(distance)]).start()
        outgoing.append(lambda: any_sib_copy(1, slot).wait_send())

    def out_pass_on(step):
        for way in (0, 1):
            out_copy(step, way).wait_recv()
        if step < last_x:
            out_start(step + 1)
        out_sib(1 + 2 * step, -1 - step)
        if step < last_x:
            out_sib(2 + 2 * step, 1 + step)

    start(first(0, wproj.at[core, y, z]))

    def pack_step(i, acc):
        rows = dot(pack, hid[0, :, at(i)])
        block[:, at(i)] = rows
        scaled = (gate * cot[0, :, at(i)].astype(F32)).astype(BF16)
        block_grad[:, at(i)] = dot(pack, scaled).astype(BF16)
        return acc + rows * rows

    squares = lax.fori_loop(0, n_chunks, pack_step, jnp.zeros((SLOTS, chunk), F32))
    inv_norm = lax.rsqrt(jnp.sum(squares, axis=1, keepdims=True) * (1.0 / width) + EPSILON)

    def norm_step(i):
        normed[:, at(i)] = (block[:, at(i)] * inv_norm * gain[:, at(i)]).astype(BF16)

    each(n_chunks, norm_step)

    slices[y] = normed[:, at(y)]
    send_slices = along(peer_y, 5, lambda j: normed.at[:, at(lax.rem(y + j, n))], slices.at[y])

    arrived(first(0, wproj.at[core, y, z]))
    for piece in range(PIECES):
        ring_start(0, piece)
    sib_start(0, b)
    start(out_first)
    start(send_slices)
    for step in range(last + 1):
        pass_on(step)
        if step == 0:
            arrived(out_first)
            out_second_start()
    for slot in range(n):
        any_sib_copy(0, slot).wait_recv()

    def project(side):
        def step(i, acc):
            return acc + dot(normed[:, at(i)], wproj[side, i].reshape(chunk, -1))

        zero = jnp.zeros((SLOTS, half_heads + 128), F32)
        return lax.fori_loop(0, n_chunks, step, zero).astype(BF16)

    low_lane = lax.broadcasted_iota(jnp.int32, (SLOTS, 128), 1) < HEAD

    def pad_heads(ref, rows, group):
        for i in range(group_heads // 2):
            pair = rows[:, i * 128 : (i + 1) * 128]
            for parity in (0, 1):
                moved = pair if parity == group else pltpu.roll(pair, HEAD, 1)
                kept = jnp.where(low_lane, moved, 0.0) if group == 0 else jnp.where(low_lane, 0.0, moved)
                at_row = (group * group_heads + 2 * i + parity) * SLOTS
                ref[at_row : at_row + SLOTS, :] = kept.astype(BF16)

    def join_heads(both):
        tall = jnp.transpose(both)
        groups = []
        for group in (0, 1):
            pairs = []
            for i in range(group_heads // 2):
                at_row = (group * group_heads + 2 * i) * SLOTS
                even = tall[at_row : at_row + SLOTS, :]
                odd = tall[at_row + SLOTS : at_row + 2 * SLOTS, :]
                if group == 0:
                    pairs.append(jnp.where(low_lane, even, pltpu.roll(odd, HEAD, 1)))
                else:
                    pairs.append(jnp.where(low_lane, pltpu.roll(even, HEAD, 1), odd))
            groups.append(jnp.concatenate(pairs, axis=1))
        return groups

    low = project(0).astype(F32)
    high = project(1).astype(F32)
    lane_id = lax.broadcasted_iota(jnp.int32, (SLOTS, 128), 1)
    own_keys = jnp.where((lane_id == 0) & (used < 0.5), KEY_MARK, low[:, half_heads:])
    kv[b, a, :, :128] = own_keys.astype(BF16)
    kv[b, a, :, 128:] = high[:, half_heads:].astype(BF16)
    kv_first = along(peer_a, 0, lambda j: kv.at[b, a], kv.at[b, a])
    kv_second = along(peer_b, 1, lambda j: kv.at[b], kv.at[b])
    start(kv_first)
    pad_heads(qpad, low[:, :half_heads], 0)
    pad_heads(qpad, high[:, :half_heads], 1)
    others(n, lambda j: out_second(0, j).wait_recv())
    if chips > 1:
        out_start(0)
    out_sib(0, 0)
    arrived(kv_first)
    start(kv_second)

    key_row = lax.broadcasted_iota(jnp.int32, (keys, 1), 0)
    query_at = seq * SLOTS + (lax.broadcasted_iota(jnp.int32, (1, lanes), 1) & (SLOTS - 1))
    scale = HEAD**-0.5

    def score_step(i, top):
        rows = kv[i].reshape(keys, 256).astype(F32)
        kvt[i] = jnp.transpose(rows).astype(BF16)
        key_at = seq_of(i, key_row >> 5) * SLOTS + (key_row & (SLOTS - 1))
        key_at = jnp.where(rows[:, 0:1] < KEY_BOUND, key_at, FAR)
        s = dot(rows[:, :128].astype(BF16), qpad[...], 1, 1) * scale
        s = jnp.where(key_at <= query_at, s, NEGATIVE)
        scores[i] = s
        return jnp.maximum(top, jnp.max(s, axis=0, keepdims=True))

    top = score_step(b, jnp.full((1, lanes), NEGATIVE, F32))
    for step in range(last_x):
        out_pass_on(step)

    def next_score_step(t, top):
        after, odd = lax.div(t, 2), lax.rem(t, 2)
        j = (1 - odd) * (1 + after) + odd * (n - 1 - after)
        kv_second(j).wait_recv()
        return score_step(lax.rem(b + n - j, n), top)

    top = lax.fori_loop(0, n - 1, next_score_step, top)

    if chips > 1:
        out_pass_on(last_x)
    for slot in range(chips):
        any_sib_copy(1, slot).wait_recv()

    out_rows = n * wout.shape[3]

    def out_at(i):
        return pl.ds(pl.multiple_of(i * out_rows, out_rows), out_rows)

    def head_grad_step(i):
        acc = jnp.zeros((SLOTS, out_rows), F32)
        for d in range(n_dp):
            acc += dot(block_grad[:, cols_of(d)], wout[d, i].reshape(out_rows, out_cols), 1, 1)
        upstream[:, out_at(i)] = acc

    each(n, head_grad_step)
    for group in (0, 1):
        rows = upstream[:, group * half_heads : (group + 1) * half_heads]
        pad_heads(opad, rows, group)

    def exp_step(i, carry):
        total_exp, inner = carry
        e = jnp.exp(scores[i] - top)
        scores[i] = e
        grads = dot(kv[i].reshape(keys, 256)[:, 128:], opad[...], 1, 1)
        dprobs[i] = grads
        total_exp += jnp.sum(e, axis=0, keepdims=True)
        return total_exp, inner + jnp.sum(e * grads, axis=0, keepdims=True)

    zero = jnp.zeros((1, lanes), F32)
    total_exp, inner = lax.fori_loop(0, n, exp_step, (zero, zero))
    inv_sum = 1.0 / total_exp
    inner = inner * inv_sum

    def rs_slab(step, way):
        return lax.rem(b + n + (1 - 2 * way) * (n // 2 - step), n)

    def rs_copy(step, way, kind):
        return copy_to(
            dkv.at[kind, rs_slab(step, way)],
            got_dkv.at[way, kind, step],
            rs_send.at[way, kind, step],
            rs_recv.at[way, kind, step],
            peer_b(1 + way * (n - 2)),
        )

    def rs_start(step, way, kind):
        rs_copy(step, way, kind).start()
        outgoing.append(lambda: rs_copy(step, way, kind).wait_send())

    def grad_step(t, carry):
        mixed_t, query_t = carry
        i = rs_slab(lax.div(t + 1, 2), 1 - lax.rem(t, 2))
        p = scores[i] * inv_sum
        half = p.astype(BF16)
        ds = (p * (dprobs[i] - inner)).astype(BF16)
        dkv[0, i] = dot(ds, qpad[...]) * scale
        dkv[1, i] = dot(half, opad[...])

        @pl.when(t == 0)
        def _():
            rs_copy(0, 0, 0).start()
            rs_copy(0, 1, 1).start()

        return mixed_t + dot(kvt[i, 128:, :], half), query_t + dot(kvt[i, :128, :], ds)

    zero = jnp.zeros((128, lanes), F32)
    mixed_t, query_t = lax.fori_loop(0, n, grad_step, (zero, zero))
    outgoing.append(lambda: rs_copy(0, 0, 0).wait_send())
    outgoing.append(lambda: rs_copy(0, 1, 1).wait_send())

    def rs_step(step):
        for way in (0, 1):
            for kind in (0, 1):
                if step > 1 or kind == way:
                    rs_copy(step - 1, way, kind).wait_recv()
                    dkv[kind, rs_slab(step, way)] += got_dkv[way, kind, step - 1]
                rs_start(step, way, kind)

    rs_step(1)

    heads = jnp.concatenate(join_heads(mixed_t), axis=1).astype(BF16)

    def out_step(d):
        rows = wout[d].reshape(n * out_rows, out_cols)
        block_out[:, cols_of(d)] = dot(heads, rows).astype(BF16)

    each(n_dp, out_step)
    if last > 1:
        rs_step(2)

    def mix_step(i, acc):
        out_tokens = dot(spread, block_out[:, at(i)])
        mixed_out[0, :, at(i)] = (hid[0, :, at(i)].astype(F32) + gate * out_tokens).astype(BF16)
        return acc + cot[0, :, at(i)].astype(F32) * out_tokens

    through = lax.fori_loop(0, n_chunks, mix_step, jnp.zeros((tokens, chunk), F32))
    through = jnp.sum(through, axis=1, keepdims=True)
    grad_logit = through * gate * (1.0 - gate)

    def router_step(i):
        term = hid[0, :, at(i)].astype(F32) * grad_logit
        row_a[a, :, at(i)] = jnp.sum(term, axis=0, keepdims=True)

    each(n_chunks, router_step)
    router_first = along(peer_a, 2, lambda j: row_a.at[a], row_a.at[a])
    router_second = along(peer_b, 3, lambda j: row_b.at[b], row_b.at[b])
    router_third = along_d(0, row_d)
    start(router_first)

    for group, rows in enumerate(join_heads(query_t * scale)):
        dqkv[group, :, :half_heads] = rows.astype(BF16)
    for step in range(3, last + 1):
        rs_step(step)
    arrived(send_slices)
    normed_t[...] = jnp.transpose(slices[...].reshape(keys, chunk).astype(F32)).astype(BF16)

    for kind in (0, 1):
        mine = dkv[kind, b]
        for way in (0, 1):
            rs_copy(last, way, kind).wait_recv()
            mine += got_dkv[way, kind, last]
        part[:, :, kind * 128 : (kind + 1) * 128] = mine.reshape(n, SLOTS, 128)
    send_part = along(peer_a, 4, lambda j: part.at[lax.rem(a + j, n)], got_part.at[a])
    start(send_part)
    arrived(router_first)
    row_b[b] = jnp.sum(row_a[...], axis=0)
    start(router_second)
    arrived(send_part)
    own = part[a]
    own = lax.fori_loop(1, n, lambda j, acc: acc + got_part[lax.rem(a + j, n)], own)
    grad_kv = own.astype(BF16)
    gkv[y] = grad_kv
    gkv_gather = along(peer_y, 6, lambda j: gkv.at[y], gkv.at[y])
    start(gkv_gather)
    dqkv[0, :, half_heads:] = grad_kv[:, :128]
    dqkv[1, :, half_heads:] = grad_kv[:, 128:]

    def back_step(i, acc):
        grads = dot(dqkv[0], wproj[0, i].reshape(chunk, -1), 1, 1)
        grads += dot(dqkv[1], wproj[1, i].reshape(chunk, -1), 1, 1)
        u = grads * gain[:, at(i)]
        upstream[:, at(i)] = u
        return acc + u * block[:, at(i)]

    overlap = lax.fori_loop(0, n_chunks, back_step, jnp.zeros((SLOTS, chunk), F32))
    overlap = jnp.sum(overlap, axis=1, keepdims=True) * (1.0 / width)

    arrived(gkv_gather)
    share[...] = dot(normed_t[...], gkv[...].reshape(keys, 256)).reshape(n, SLOTS, 256)
    half = n // 2
    send_pair = copy_to(
        share.at[pl.ds((1 - core) * half, half)], pair, t_send.at[0], t_recv.at[0], sibling
    )
    send_pair.start()
    arrived(router_second)
    row_d[dp] = jnp.sum(row_b[...], axis=0)
    start(router_third, n_dp)

    cubed = inv_norm * inv_norm * inv_norm * overlap

    send_pair.wait()
    for i in range(half):
        share[core * half + i] += pair[i]

    def share_copy(i):
        to = core * half + i
        rows = share.at[to]
        return copy_to(rows, got_share.at[z], x_send.at[7, i], x_recv.at[7, z], (dp, y * n + to))

    def share_start(i):
        @pl.when(core * half + i != z)
        def _():
            share_copy(i).start()

    def share_sent(i):
        @pl.when(core * half + i != z)
        def _():
            share_copy(i).wait_send()

    each(half, share_start)
    outgoing.append(lambda: each(half, share_sent))

    def input_step(i):
        rows = inv_norm * upstream[:, at(i)] - block[:, at(i)] * cubed
        tokens_grad = dot(spread, rows.astype(BF16))
        grads = cot[0, :, at(i)].astype(F32) + grad_logit * router[:, at(i)] + tokens_grad
        igrad_out[0, :, at(i)] = grads.astype(BF16)

    each(n_chunks, input_step)

    def got_share_copy(j):
        source = lax.rem(z + j, n)
        return copy_to(
            share.at[0], got_share.at[source], x_send.at[7, 0], x_recv.at[7, source], sibling
        )

    x = lax.div(dp, 2)

    def total_copy(j):
        return copy_to(total.at[x], total.at[x], d_send.at[1, j], d_recv.at[1, j], peer_x(j))

    send_final = copy_to(final, final, t_send.at[1], t_recv.at[1], sibling)
    here = lax.div(z, half) == core

    @pl.when(here)
    def _():
        others(n, lambda j: got_share_copy(j).wait_recv())
        mine = share[z]
        total[x] = lax.fori_loop(1, n, lambda j, acc: acc + got_share[lax.rem(z + j, n)], mine)
        others(chips, lambda j: total_copy(j).start())

    arrived(router_third, n_dp)
    row = jnp.sum(row_d[...], axis=0)
    per_tile = 128 // SLOTS
    tile = jnp.zeros((1, SLOTS), F32)
    for i in range(width // SLOTS):
        tile = jnp.where(seq == i, row[:, i * SLOTS : (i + 1) * SLOTS], tile)
    rgrad_out[...] = tile

    @pl.when(here)
    def _():
        others(chips, lambda j: total_copy(j).wait_recv())
        final[...] = jnp.sum(total[...], axis=0)
        send_final.start()
        others(chips, lambda j: total_copy(j).wait_send())
        send_final.wait_send()

    @pl.when(jnp.logical_not(here))
    def _():
        send_final.wait_recv()

    kvgrad_out[...] = final[...]

    for wait in outgoing:
        wait()


def local(hidden, cotangent, picks, gain, router, w_query, w_kv, w_out):
    n_dp, n_seq = lax.axis_size("dp"), lax.axis_size("seq")
    n = math.isqrt(n_seq)
    tokens, width = hidden.shape[1:]
    half_heads = w_query.shape[1] // 2
    group_heads = half_heads // HEAD
    out_slab = w_out.shape[0]
    keys = n * SLOTS
    lanes = 2 * group_heads * SLOTS
    vmem = pl.BlockSpec(memory_space=pltpu.VMEM)
    dma = pltpu.SemaphoreType.DMA
    outs = pl.pallas_call(
        functools.partial(kernel, n, n_dp, width, group_heads),
        out_shape=(
            jax.ShapeDtypeStruct(hidden.shape, BF16),
            jax.ShapeDtypeStruct(hidden.shape, BF16),
            jax.ShapeDtypeStruct((SLOTS, 256), F32),
            jax.ShapeDtypeStruct((1, SLOTS), F32),
        ),
        in_specs=[vmem] * 8,
        out_specs=(vmem,) * 4,
        scratch_shapes=[
            pltpu.VMEM((2, n, n, SLOTS, half_heads + 128), BF16),
            pltpu.VMEM((n_dp, n, n, out_slab, width // n_dp), BF16),
            pltpu.VMEM((n, n, SLOTS, 256), BF16),
            pltpu.VMEM((n, 256, keys), BF16),
            pltpu.VMEM((n, keys, lanes), F32),
            pltpu.VMEM((n, keys, lanes), F32),
            pltpu.VMEM((lanes, 128), BF16),
            pltpu.VMEM((lanes, 128), BF16),
            pltpu.VMEM((2, n, keys, 128), F32),
            pltpu.VMEM((2, 2, n // 2, keys, 128), F32),
            pltpu.VMEM((n, SLOTS, 256), F32),
            pltpu.VMEM((n, SLOTS, 256), F32),
            pltpu.VMEM((n, SLOTS, 256), BF16),
            pltpu.VMEM((SLOTS, width), BF16),
            pltpu.VMEM((n, SLOTS, keys), BF16),
            pltpu.VMEM((keys, keys), BF16),
            pltpu.VMEM((n, SLOTS, 256), F32),
            pltpu.VMEM((n // 2, SLOTS, 256), F32),
            pltpu.VMEM((n, SLOTS, 256), F32),
            pltpu.VMEM((n_dp // 2, SLOTS, 256), F32),
            pltpu.VMEM((SLOTS, 256), F32),
            pltpu.VMEM((n, 1, width), F32),
            pltpu.VMEM((n, 1, width), F32),
            pltpu.VMEM((n_dp, 1, width), F32),
            pltpu.VMEM((SLOTS, width), F32),
            pltpu.VMEM((SLOTS, width), BF16),
            pltpu.VMEM((SLOTS, width), BF16),
            pltpu.VMEM((2, SLOTS, half_heads + 128), BF16),
            pltpu.VMEM((SLOTS, width), F32),
            dma((2, n)),
            dma((2, n)),
            dma((n // 2, 2, PIECES)),
            dma((n // 2, 2, PIECES)),
            dma((2, max(n, n_dp // 2))),
            dma((2, max(n, n_dp // 2))),
            dma((9, n)),
            dma((9, n)),
            dma((2, 2, n // 2)),
            dma((2, 2, n // 2)),
            dma((2, n_dp)),
            dma((2, n_dp)),
            dma((2, 2)),
            dma((2, 2)),
            dma((2,)),
            dma((2,)),
        ],
        compiler_params=pltpu.CompilerParams(
            collective_id=0, has_side_effects=True, vmem_limit_bytes=58 * 1024 * 1024
        ),
    )(
        hidden, cotangent, picks, gain.reshape(1, -1), router.reshape(1, -1), w_query, w_kv, w_out
    )
    mixed, input_grad, kv_grad, router_grad = outs
    return mixed, input_grad, kv_grad, router_grad.reshape(-1)


def solution(mesh):
    rows = P("dp", "seq", None)
    weight = P("seq", None)
    return jax.shard_map(
        local,
        mesh=mesh,
        in_specs=(rows, rows, P("dp", "seq"), P(), P(), weight, weight, weight),
        out_specs=(rows, rows, weight, P("seq")),
        check_vma=False,
    )
```

```python
import functools
import math

import jax
import jax.numpy as jnp
from jax import lax
from jax.experimental import pallas as pl
from jax.experimental.pallas import tpu as pltpu
from jax.sharding import PartitionSpec as P

MESH = pl.DeviceIdType.MESH
EPSILON = 1e-05
SLOTS = 32
HEAD = 64
F32, BF16 = jnp.float32, jnp.bfloat16
KEY_MARK = 2.0**100
KEY_BOUND = 2.0**64
NEGATIVE = -1e30
FAR = 1 << 30
PIECES = 4


def dot(left, right, left_dim=1, right_dim=0):
    return lax.dot_general(
        left, right, (((left_dim,), (right_dim,)), ((), ())), preferred_element_type=F32
    )


def copy_to(source, target, send_sem, recv_sem, device):
    return pltpu.make_async_remote_copy(
        src_ref=source,
        dst_ref=target,
        send_sem=send_sem,
        recv_sem=recv_sem,
        device_id=device,
        device_id_type=MESH,
    )


def kernel(
    n, n_dp, width, group_heads,
    hid, cot, picks, gain, router, wq, wkv, wo,
    mixed_out, igrad_out, kvgrad_out, rgrad_out,
    wquery, wout, wkeys, kv, kvt, scores, dprobs, qpad, opad, dkv, got_dkv, part, got_part,
    gkv, normed, slices, normed_t, share, pair, got_share, total, final, row_a, row_b, row_d,
    block, block_grad, block_out, dqkv, upstream,
    p1_send, p1_recv, ring_send, ring_recv, sib_send, sib_recv,
    x_send, x_recv, rs_send, rs_recv, d_send, d_recv, o_send, o_recv, t_send, t_recv,
):
    seq, dp = lax.axis_index("seq"), lax.axis_index("dp")
    core = lax.rem(dp, 2)
    y, z = lax.div(seq, n), lax.rem(seq, n)
    a = z + core * (y - z)
    b = y + core * (z - y)
    keys = n * SLOTS
    half_heads = group_heads * HEAD
    lanes = 2 * group_heads * SLOTS
    chips = n_dp // 2
    out_cols = width // n_dp
    chunk = keys

    def seq_of(b_, a_):
        return (1 - core) * (b_ * n + a_) + core * (a_ * n + b_)

    def peer_a(j):
        return (dp, seq_of(b, lax.rem(a + j, n)))

    def peer_b(j):
        return (dp, seq_of(lax.rem(b + j, n), a))

    def peer_y(j):
        return (dp, lax.rem(y + j, n) * n + z)

    def peer_z(j):
        return (dp, y * n + lax.rem(z + j, n))

    def peer_x(j):
        return (lax.rem(dp + 2 * j, n_dp), seq)

    def peer_d(j):
        return (lax.rem(dp + j, n_dp), seq)

    sibling = (dp + 1 - 2 * core, seq)

    def each(count, body):
        def step(j, carry):
            body(j)
            return carry

        lax.fori_loop(0, count, step, 0)

    def others(count, body):
        def step(j, carry):
            body(j)
            return carry

        lax.fori_loop(1, count, step, 0)

    barrier = pltpu.get_barrier_semaphore()

    def greet(device):
        pl.semaphore_signal(barrier, inc=1, device_id=device, device_id_type=MESH)

    others(n, lambda j: greet(peer_a(j)))
    others(n, lambda j: greet(peer_b(j)))
    others(n_dp, lambda j: greet(peer_d(j)))

    for side in (0, 1):

        @pl.when(core == side)
        def _():
            cols = slice(side * half_heads, (side + 1) * half_heads)
            wquery[side, y, z] = wq[:, cols]
            wkeys[side, y, z] = wkv[:, side * 128 : (side + 1) * 128]

    def cols_of(d):
        return pl.ds(pl.multiple_of(d * out_cols, out_cols), out_cols)

    wout[dp, y, z] = wo[:, cols_of(dp)]

    tokens = hid.shape[1]
    row_id = lax.broadcasted_iota(jnp.int32, (tokens, tokens), 0)
    col_id = lax.broadcasted_iota(jnp.int32, (tokens, tokens), 1)
    pick_row = picks[...].astype(F32)
    pick_wide = jnp.broadcast_to(pick_row, (tokens, tokens))
    pick_col = jnp.sum(jnp.where(row_id == col_id, pick_wide, 0.0), axis=1, keepdims=True)
    rank_col = jnp.sum(jnp.where(col_id < row_id, pick_wide, 0.0), axis=1, keepdims=True)
    pick_tall = jnp.broadcast_to(pick_col, (tokens, tokens))
    rank_row = jnp.sum(jnp.where(row_id < col_id, pick_tall, 0.0), axis=0, keepdims=True)
    slot_row = lax.broadcasted_iota(jnp.int32, (SLOTS, tokens), 0).astype(F32)
    slot_col = lax.broadcasted_iota(jnp.int32, (tokens, SLOTS), 1).astype(F32)
    pack = jnp.where((slot_row == rank_row) & (pick_row > 0.5), 1.0, 0.0)
    spread = jnp.where((slot_col == rank_col) & (pick_col > 0.5), 1.0, 0.0).astype(BF16)
    used = jnp.sum(pack, axis=1, keepdims=True)
    pack = pack.astype(BF16)

    n_chunks = width // chunk

    def at(i):
        return pl.ds(pl.multiple_of(i * chunk, chunk), chunk)

    def gate_step(i, acc):
        return acc + hid[0, :, at(i)].astype(F32) * router[:, at(i)]

    logit = lax.fori_loop(0, n_chunks, gate_step, jnp.zeros((tokens, chunk), F32))
    gate = jax.nn.sigmoid(jnp.sum(logit, axis=1, keepdims=True))

    pl.semaphore_wait(barrier, 2 * (n - 1) + n_dp - 1)

    outgoing = []

    def first(which, own):
        def make(j):
            return copy_to(own, own, p1_send.at[which, j], p1_recv.at[which, j], peer_a(j))

        return make

    def along(peer, which, source, target):
        def make(j):
            return copy_to(source(j), target, x_send.at[which, j], x_recv.at[which, j], peer(j))

        return make

    def along_d(which, ref):
        def make(j):
            return copy_to(
                ref.at[dp], ref.at[dp], d_send.at[which, j], d_recv.at[which, j], peer_d(j)
            )

        return make

    def start(make, count=n):
        others(count, lambda j: make(j).start())
        outgoing.append(lambda: sent(make, count))

    def arrived(make, count=n):
        others(count, lambda j: make(j).wait_recv())

    def sent(make, count=n):
        others(count, lambda j: make(j).wait_send())

    last = n // 2 - 1

    def slab(side, k, piece=None):
        size = n // PIECES
        rows = slice(None) if piece is None else pl.ds(piece * size, size)
        return wquery.at[0, k, rows] if side == 0 else wquery.at[1, rows, k]

    def goes(step, way, piece):
        return step < last or (piece < PIECES // 2) == (way == 0)

    def ring_copy(step, way, piece, rows, device):
        return copy_to(
            rows, rows, ring_send.at[step, way, piece], ring_recv.at[step, way, piece], device
        )

    def any_ring_copy(step, way, piece):
        return ring_copy(step, way, piece, slab(0, 0, piece), peer_b(1))

    def ring_start(step, piece):
        for side in (0, 1):

            @pl.when(core == side)
            def _():
                for way, block_id, device in (
                    (0, lax.rem(b + n - step, n), peer_b(1)),
                    (1, lax.rem(b + step, n), peer_b(n - 1)),
                ):
                    if goes(step, way, piece):
                        ring_copy(step, way, piece, slab(side, block_id, piece), device).start()

        for way in (0, 1):
            if goes(step, way, piece):
                outgoing.append(lambda way=way: any_ring_copy(step, way, piece).wait_send())

    def sib_copy(which, slot, rows):
        return copy_to(rows, rows, sib_send.at[which, slot], sib_recv.at[which, slot], sibling)

    def any_sib_copy(which, slot):
        return sib_copy(which, slot, (slab(0, 0), wout.at[0], wkeys.at[0, 0])[which])

    def sib_start(slot, block_id):
        for side in (0, 1):

            @pl.when(core == side)
            def _():
                sib_copy(0, slot, slab(side, block_id)).start()

        outgoing.append(lambda: any_sib_copy(0, slot).wait_send())

    def pass_on(step):
        for piece in range(PIECES):
            for way in (0, 1):
                if goes(step, way, piece):
                    any_ring_copy(step, way, piece).wait_recv()
            if step < last:
                ring_start(step + 1, piece)
        sib_start(1 + 2 * step, lax.rem(b + n - 1 - step, n))
        if step < last:
            sib_start(2 + 2 * step, lax.rem(b + 1 + step, n))

    out_first = first(1, wout.at[dp, y, z])

    def out_second(side, j):
        rows = wout.at[dp, b] if side == 0 else wout.at[dp, :, b]
        return copy_to(rows, rows, x_send.at[8, j], x_recv.at[8, j], peer_b(j))

    def out_second_start():
        for side in (0, 1):

            @pl.when(core == side)
            def _():
                others(n, lambda j: out_second(side, j).start())

        outgoing.append(lambda: others(n, lambda j: out_second(0, j).wait_send()))

    last_x = chips // 2 - 1

    def out_block(distance):
        return lax.rem(dp + 2 * n_dp + 2 * distance, n_dp)

    def out_copy(step, way):
        rows = wout.at[out_block((2 * way - 1) * step)]
        if step == last_x:
            rows = rows.at[pl.ds(way * (n // 2), n // 2)]
        device = peer_x(1 if way == 0 else chips - 1)
        return copy_to(rows, rows, o_send.at[step, way], o_recv.at[step, way], device)

    def out_start(step):
        for way in (0, 1):
            out_copy(step, way).start()
            outgoing.append(lambda way=way: out_copy(step, way).wait_send())

    def out_sib(slot, distance):
        sib_copy(1, slot, wout.at[out_block(distance)]).start()
        outgoing.append(lambda: any_sib_copy(1, slot).wait_send())

    def out_pass_on(step):
        for way in (0, 1):
            out_copy(step, way).wait_recv()
        if step < last_x:
            out_start(step + 1)
        out_sib(1 + 2 * step, -1 - step)
        if step < last_x:
            out_sib(2 + 2 * step, 1 + step)

    query_first = first(0, wquery.at[core, y, z])
    keys_first = first(2, wkeys.at[core, y, z])
    start(keys_first)
    start(query_first)

    def pack_step(i, acc):
        rows = dot(pack, hid[0, :, at(i)])
        block[:, at(i)] = rows
        scaled = (gate * cot[0, :, at(i)].astype(F32)).astype(BF16)
        block_grad[:, at(i)] = dot(pack, scaled).astype(BF16)
        return acc + rows * rows

    squares = lax.fori_loop(0, n_chunks, pack_step, jnp.zeros((SLOTS, chunk), F32))
    inv_norm = lax.rsqrt(jnp.sum(squares, axis=1, keepdims=True) * (1.0 / width) + EPSILON)

    def norm_step(i):
        normed[:, at(i)] = (block[:, at(i)] * inv_norm * gain[:, at(i)]).astype(BF16)

    each(n_chunks, norm_step)

    slices[y] = normed[:, at(y)]
    send_slices = along(peer_y, 5, lambda j: normed.at[:, at(lax.rem(y + j, n))], slices.at[y])

    def keys_slab(side, k):
        return wkeys.at[0, k] if side == 0 else wkeys.at[1, :, k]

    def keys_copy(side, block_id, j):
        rows = keys_slab(side, block_id)
        return copy_to(rows, rows, x_send.at[9, j], x_recv.at[9, j], peer_b(j))

    def nearest(t):
        after, odd = lax.div(t, 2), lax.rem(t, 2)
        return (1 - odd) * (1 + after) + odd * (n - 1 - after)

    def keys_sib(slot, block_id):
        for side in (0, 1):

            @pl.when(core == side)
            def _():
                sib_copy(2, slot, keys_slab(side, block_id)).start()

    def keys_arrived(t):
        j = nearest(t)
        keys_copy(0, 0, j).wait_recv()
        keys_sib(t + 1, lax.rem(b + n - j, n))

    arrived(keys_first)
    for side in (0, 1):

        @pl.when(core == side)
        def _():
            others(n, lambda j: keys_copy(side, b, j).start())

    outgoing.append(lambda: others(n, lambda j: keys_copy(0, 0, j).wait_send()))
    keys_sib(0, b)
    arrived(query_first)
    for piece in range(PIECES):
        ring_start(0, piece)
    sib_start(0, b)
    start(out_first)
    start(send_slices)
    pass_on(0)
    arrived(out_first)
    out_second_start()
    each(n - 1, keys_arrived)
    outgoing.append(lambda: each(n, lambda slot: any_sib_copy(2, slot).wait_send()))
    each(n, lambda slot: any_sib_copy(2, slot).wait_recv())

    def project(ref, side):
        def step(i, acc):
            return acc + dot(normed[:, at(i)], ref[side, i].reshape(chunk, -1))

        zero = jnp.zeros((SLOTS, ref.shape[-1]), F32)
        return lax.fori_loop(0, n_chunks, step, zero).astype(BF16)

    lane_id = lax.broadcasted_iota(jnp.int32, (SLOTS, 128), 1)
    own_keys = project(wkeys, 0).astype(F32)
    own_keys = jnp.where((lane_id == 0) & (used < 0.5), KEY_MARK, own_keys)
    kv[b, a, :, :128] = own_keys.astype(BF16)
    kv[b, a, :, 128:] = project(wkeys, 1)
    kv_first = along(peer_a, 0, lambda j: kv.at[b, a], kv.at[b, a])
    kv_second = along(peer_b, 1, lambda j: kv.at[b], kv.at[b])
    start(kv_first)
    for step in (1, 2):
        if step <= last:
            pass_on(step)
    arrived(kv_first)
    start(kv_second)
    others(n, lambda j: out_second(0, j).wait_recv())
    if chips > 1:
        out_start(0)
    out_sib(0, 0)
    for step in range(3, last + 1):
        pass_on(step)
    for slot in range(n):
        any_sib_copy(0, slot).wait_recv()

    low_lane = lax.broadcasted_iota(jnp.int32, (SLOTS, 128), 1) < HEAD

    def pad_heads(ref, rows, group):
        for i in range(group_heads // 2):
            pair = rows[:, i * 128 : (i + 1) * 128]
            for parity in (0, 1):
                moved = pair if parity == group else pltpu.roll(pair, HEAD, 1)
                kept = jnp.where(low_lane, moved, 0.0) if group == 0 else jnp.where(low_lane, 0.0, moved)
                at_row = (group * group_heads + 2 * i + parity) * SLOTS
                ref[at_row : at_row + SLOTS, :] = kept.astype(BF16)

    def join_heads(both):
        tall = jnp.transpose(both)
        groups = []
        for group in (0, 1):
            pairs = []
            for i in range(group_heads // 2):
                at_row = (group * group_heads + 2 * i) * SLOTS
                even = tall[at_row : at_row + SLOTS, :]
                odd = tall[at_row + SLOTS : at_row + 2 * SLOTS, :]
                if group == 0:
                    pairs.append(jnp.where(low_lane, even, pltpu.roll(odd, HEAD, 1)))
                else:
                    pairs.append(jnp.where(low_lane, pltpu.roll(even, HEAD, 1), odd))
            groups.append(jnp.concatenate(pairs, axis=1))
        return groups

    for group in (0, 1):
        pad_heads(qpad, project(wquery, group).astype(F32), group)

    key_row = lax.broadcasted_iota(jnp.int32, (keys, 1), 0)
    query_at = seq * SLOTS + (lax.broadcasted_iota(jnp.int32, (1, lanes), 1) & (SLOTS - 1))
    scale = HEAD**-0.5

    def score_step(i, top):
        rows = kv[i].reshape(keys, 256).astype(F32)
        kvt[i] = jnp.transpose(rows).astype(BF16)
        key_at = seq_of(i, key_row >> 5) * SLOTS + (key_row & (SLOTS - 1))
        key_at = jnp.where(rows[:, 0:1] < KEY_BOUND, key_at, FAR)
        s = dot(rows[:, :128].astype(BF16), qpad[...], 1, 1) * scale
        s = jnp.where(key_at <= query_at, s, NEGATIVE)
        scores[i] = s
        return jnp.maximum(top, jnp.max(s, axis=0, keepdims=True))

    top = score_step(b, jnp.full((1, lanes), NEGATIVE, F32))
    for step in range(last_x):
        out_pass_on(step)

    def next_score_step(t, top):
        j = nearest(t)
        kv_second(j).wait_recv()
        return score_step(lax.rem(b + n - j, n), top)

    top = lax.fori_loop(0, n - 1, next_score_step, top)

    if chips > 1:
        out_pass_on(last_x)
    for slot in range(chips):
        any_sib_copy(1, slot).wait_recv()

    out_rows = n * wout.shape[3]

    def out_at(i):
        return pl.ds(pl.multiple_of(i * out_rows, out_rows), out_rows)

    def head_grad_step(i):
        acc = jnp.zeros((SLOTS, out_rows), F32)
        for d in range(n_dp):
            acc += dot(block_grad[:, cols_of(d)], wout[d, i].reshape(out_rows, out_cols), 1, 1)
        upstream[:, out_at(i)] = acc

    each(n, head_grad_step)
    for group in (0, 1):
        rows = upstream[:, group * half_heads : (group + 1) * half_heads]
        pad_heads(opad, rows, group)

    def exp_step(i, carry):
        total_exp, inner = carry
        e = jnp.exp(scores[i] - top)
        scores[i] = e
        grads = dot(kv[i].reshape(keys, 256)[:, 128:], opad[...], 1, 1)
        dprobs[i] = grads
        total_exp += jnp.sum(e, axis=0, keepdims=True)
        return total_exp, inner + jnp.sum(e * grads, axis=0, keepdims=True)

    zero = jnp.zeros((1, lanes), F32)
    total_exp, inner = lax.fori_loop(0, n, exp_step, (zero, zero))
    inv_sum = 1.0 / total_exp
    inner = inner * inv_sum

    def rs_slab(step, way):
        return lax.rem(b + n + (1 - 2 * way) * (n // 2 - step), n)

    def rs_copy(step, way, kind):
        return copy_to(
            dkv.at[kind, rs_slab(step, way)],
            got_dkv.at[way, kind, step],
            rs_send.at[way, kind, step],
            rs_recv.at[way, kind, step],
            peer_b(1 + way * (n - 2)),
        )

    def rs_start(step, way, kind):
        rs_copy(step, way, kind).start()
        outgoing.append(lambda: rs_copy(step, way, kind).wait_send())

    def grad_step(t, carry):
        mixed_t, query_t = carry
        i = rs_slab(lax.div(t + 1, 2), 1 - lax.rem(t, 2))
        p = scores[i] * inv_sum
        half = p.astype(BF16)
        ds = (p * (dprobs[i] - inner)).astype(BF16)
        dkv[0, i] = dot(ds, qpad[...]) * scale
        dkv[1, i] = dot(half, opad[...])

        @pl.when(t == 0)
        def _():
            rs_copy(0, 0, 0).start()
            rs_copy(0, 1, 1).start()

        return mixed_t + dot(kvt[i, 128:, :], half), query_t + dot(kvt[i, :128, :], ds)

    zero = jnp.zeros((128, lanes), F32)
    mixed_t, query_t = lax.fori_loop(0, n, grad_step, (zero, zero))
    outgoing.append(lambda: rs_copy(0, 0, 0).wait_send())
    outgoing.append(lambda: rs_copy(0, 1, 1).wait_send())

    def rs_step(step):
        for way in (0, 1):
            for kind in (0, 1):
                if step > 1 or kind == way:
                    rs_copy(step - 1, way, kind).wait_recv()
                    dkv[kind, rs_slab(step, way)] += got_dkv[way, kind, step - 1]
                rs_start(step, way, kind)

    rs_step(1)

    heads = jnp.concatenate(join_heads(mixed_t), axis=1).astype(BF16)

    def out_step(d):
        rows = wout[d].reshape(n * out_rows, out_cols)
        block_out[:, cols_of(d)] = dot(heads, rows).astype(BF16)

    each(n_dp, out_step)
    if last > 1:
        rs_step(2)

    def mix_step(i, acc):
        out_tokens = dot(spread, block_out[:, at(i)])
        mixed_out[0, :, at(i)] = (hid[0, :, at(i)].astype(F32) + gate * out_tokens).astype(BF16)
        return acc + cot[0, :, at(i)].astype(F32) * out_tokens

    through = lax.fori_loop(0, n_chunks, mix_step, jnp.zeros((tokens, chunk), F32))
    through = jnp.sum(through, axis=1, keepdims=True)
    grad_logit = through * gate * (1.0 - gate)

    def router_step(i):
        term = hid[0, :, at(i)].astype(F32) * grad_logit
        row_a[a, :, at(i)] = jnp.sum(term, axis=0, keepdims=True)

    each(n_chunks, router_step)
    router_first = along(peer_a, 2, lambda j: row_a.at[a], row_a.at[a])
    router_second = along(peer_b, 3, lambda j: row_b.at[b], row_b.at[b])
    router_third = along_d(0, row_d)
    start(router_first)

    for group, rows in enumerate(join_heads(query_t * scale)):
        dqkv[group, :, :half_heads] = rows.astype(BF16)
    for step in range(3, last + 1):
        rs_step(step)
    arrived(send_slices)
    normed_t[...] = jnp.transpose(slices[...].reshape(keys, chunk).astype(F32)).astype(BF16)

    for kind in (0, 1):
        mine = dkv[kind, b]
        for way in (0, 1):
            rs_copy(last, way, kind).wait_recv()
            mine += got_dkv[way, kind, last]
        part[:, :, kind * 128 : (kind + 1) * 128] = mine.reshape(n, SLOTS, 128)
    send_part = along(peer_a, 4, lambda j: part.at[lax.rem(a + j, n)], got_part.at[a])
    start(send_part)
    arrived(router_first)
    row_b[b] = jnp.sum(row_a[...], axis=0)
    start(router_second)
    arrived(send_part)
    own = part[a]
    own = lax.fori_loop(1, n, lambda j, acc: acc + got_part[lax.rem(a + j, n)], own)
    grad_kv = own.astype(BF16)
    gkv[y] = grad_kv
    gkv_gather = along(peer_y, 6, lambda j: gkv.at[y], gkv.at[y])
    start(gkv_gather)
    dqkv[0, :, half_heads:] = grad_kv[:, :128]
    dqkv[1, :, half_heads:] = grad_kv[:, 128:]

    def back_step(i, acc):
        grads = jnp.zeros((SLOTS, chunk), F32)
        for side in (0, 1):
            grads += dot(dqkv[side, :, :half_heads], wquery[side, i].reshape(chunk, -1), 1, 1)
            grads += dot(dqkv[side, :, half_heads:], wkeys[side, i].reshape(chunk, -1), 1, 1)
        u = grads * gain[:, at(i)]
        upstream[:, at(i)] = u
        return acc + u * block[:, at(i)]

    overlap = lax.fori_loop(0, n_chunks, back_step, jnp.zeros((SLOTS, chunk), F32))
    overlap = jnp.sum(overlap, axis=1, keepdims=True) * (1.0 / width)

    arrived(gkv_gather)
    share[...] = dot(normed_t[...], gkv[...].reshape(keys, 256)).reshape(n, SLOTS, 256)
    half = n // 2
    send_pair = copy_to(
        share.at[pl.ds((1 - core) * half, half)], pair, t_send.at[0], t_recv.at[0], sibling
    )
    send_pair.start()
    arrived(router_second)
    row_d[dp] = jnp.sum(row_b[...], axis=0)
    start(router_third, n_dp)

    cubed = inv_norm * inv_norm * inv_norm * overlap

    send_pair.wait()
    for i in range(half):
        share[core * half + i] += pair[i]

    def share_copy(i):
        to = core * half + i
        rows = share.at[to]
        return copy_to(rows, got_share.at[z], x_send.at[7, i], x_recv.at[7, z], (dp, y * n + to))

    def share_start(i):
        @pl.when(core * half + i != z)
        def _():
            share_copy(i).start()

    def share_sent(i):
        @pl.when(core * half + i != z)
        def _():
            share_copy(i).wait_send()

    each(half, share_start)
    outgoing.append(lambda: each(half, share_sent))

    def input_step(i):
        rows = inv_norm * upstream[:, at(i)] - block[:, at(i)] * cubed
        tokens_grad = dot(spread, rows.astype(BF16))
        grads = cot[0, :, at(i)].astype(F32) + grad_logit * router[:, at(i)] + tokens_grad
        igrad_out[0, :, at(i)] = grads.astype(BF16)

    each(n_chunks, input_step)

    def got_share_copy(j):
        source = lax.rem(z + j, n)
        return copy_to(
            share.at[0], got_share.at[source], x_send.at[7, 0], x_recv.at[7, source], sibling
        )

    x = lax.div(dp, 2)

    def total_copy(j):
        return copy_to(total.at[x], total.at[x], d_send.at[1, j], d_recv.at[1, j], peer_x(j))

    send_final = copy_to(final, final, t_send.at[1], t_recv.at[1], sibling)
    here = lax.div(z, half) == core

    @pl.when(here)
    def _():
        others(n, lambda j: got_share_copy(j).wait_recv())
        mine = share[z]
        total[x] = lax.fori_loop(1, n, lambda j, acc: acc + got_share[lax.rem(z + j, n)], mine)
        others(chips, lambda j: total_copy(j).start())

    arrived(router_third, n_dp)
    row = jnp.sum(row_d[...], axis=0)
    per_tile = 128 // SLOTS
    tile = jnp.zeros((1, SLOTS), F32)
    for i in range(width // SLOTS):
        tile = jnp.where(seq == i, row[:, i * SLOTS : (i + 1) * SLOTS], tile)
    rgrad_out[...] = tile

    @pl.when(here)
    def _():
        others(chips, lambda j: total_copy(j).wait_recv())
        final[...] = jnp.sum(total[...], axis=0)
        send_final.start()
        others(chips, lambda j: total_copy(j).wait_send())
        send_final.wait_send()

    @pl.when(jnp.logical_not(here))
    def _():
        send_final.wait_recv()

    kvgrad_out[...] = final[...]

    for wait in outgoing:
        wait()


def local(hidden, cotangent, picks, gain, router, w_query, w_kv, w_out):
    n_dp, n_seq = lax.axis_size("dp"), lax.axis_size("seq")
    n = math.isqrt(n_seq)
    tokens, width = hidden.shape[1:]
    half_heads = w_query.shape[1] // 2
    group_heads = half_heads // HEAD
    out_slab = w_out.shape[0]
    keys = n * SLOTS
    lanes = 2 * group_heads * SLOTS
    vmem = pl.BlockSpec(memory_space=pltpu.VMEM)
    dma = pltpu.SemaphoreType.DMA
    outs = pl.pallas_call(
        functools.partial(kernel, n, n_dp, width, group_heads),
        out_shape=(
            jax.ShapeDtypeStruct(hidden.shape, BF16),
            jax.ShapeDtypeStruct(hidden.shape, BF16),
            jax.ShapeDtypeStruct((SLOTS, 256), F32),
            jax.ShapeDtypeStruct((1, SLOTS), F32),
        ),
        in_specs=[vmem] * 8,
        out_specs=(vmem,) * 4,
        scratch_shapes=[
            pltpu.VMEM((2, n, n, SLOTS, half_heads), BF16),
            pltpu.VMEM((n_dp, n, n, out_slab, width // n_dp), BF16),
            pltpu.VMEM((2, n, n, SLOTS, 128), BF16),
            pltpu.VMEM((n, n, SLOTS, 256), BF16),
            pltpu.VMEM((n, 256, keys), BF16),
            pltpu.VMEM((n, keys, lanes), F32),
            pltpu.VMEM((n, keys, lanes), F32),
            pltpu.VMEM((lanes, 128), BF16),
            pltpu.VMEM((lanes, 128), BF16),
            pltpu.VMEM((2, n, keys, 128), F32),
            pltpu.VMEM((2, 2, n // 2, keys, 128), F32),
            pltpu.VMEM((n, SLOTS, 256), F32),
            pltpu.VMEM((n, SLOTS, 256), F32),
            pltpu.VMEM((n, SLOTS, 256), BF16),
            pltpu.VMEM((SLOTS, width), BF16),
            pltpu.VMEM((n, SLOTS, keys), BF16),
            pltpu.VMEM((keys, keys), BF16),
            pltpu.VMEM((n, SLOTS, 256), F32),
            pltpu.VMEM((n // 2, SLOTS, 256), F32),
            pltpu.VMEM((n, SLOTS, 256), F32),
            pltpu.VMEM((n_dp // 2, SLOTS, 256), F32),
            pltpu.VMEM((SLOTS, 256), F32),
            pltpu.VMEM((n, 1, width), F32),
            pltpu.VMEM((n, 1, width), F32),
            pltpu.VMEM((n_dp, 1, width), F32),
            pltpu.VMEM((SLOTS, width), F32),
            pltpu.VMEM((SLOTS, width), BF16),
            pltpu.VMEM((SLOTS, width), BF16),
            pltpu.VMEM((2, SLOTS, half_heads + 128), BF16),
            pltpu.VMEM((SLOTS, width), F32),
            dma((3, n)),
            dma((3, n)),
            dma((n // 2, 2, PIECES)),
            dma((n // 2, 2, PIECES)),
            dma((3, max(n, n_dp // 2))),
            dma((3, max(n, n_dp // 2))),
            dma((10, n)),
            dma((10, n)),
            dma((2, 2, n // 2)),
            dma((2, 2, n // 2)),
            dma((2, n_dp)),
            dma((2, n_dp)),
            dma((2, 2)),
            dma((2, 2)),
            dma((2,)),
            dma((2,)),
        ],
        compiler_params=pltpu.CompilerParams(
            collective_id=0, has_side_effects=True, vmem_limit_bytes=58 * 1024 * 1024
        ),
    )(
        hidden, cotangent, picks, gain.reshape(1, -1), router.reshape(1, -1), w_query, w_kv, w_out
    )
    mixed, input_grad, kv_grad, router_grad = outs
    return mixed, input_grad, kv_grad, router_grad.reshape(-1)


def solution(mesh):
    rows = P("dp", "seq", None)
    weight = P("seq", None)
    return jax.shard_map(
        local,
        mesh=mesh,
        in_specs=(rows, rows, P("dp", "seq"), P(), P(), weight, weight, weight),
        out_specs=(rows, rows, weight, P("seq")),
        check_vma=False,
    )
```

```python
import functools
import math

import jax
import jax.numpy as jnp
from jax import lax
from jax.experimental import pallas as pl
from jax.experimental.pallas import tpu as pltpu
from jax.sharding import PartitionSpec as P

MESH = pl.DeviceIdType.MESH
EPSILON = 1e-05
SLOTS = 32
HEAD = 64
F32, BF16 = jnp.float32, jnp.bfloat16
KEY_MARK = 2.0**100
KEY_BOUND = 2.0**64
NEGATIVE = -1e30
FAR = 1 << 30
PIECES = 4


def dot(left, right, left_dim=1, right_dim=0):
    return lax.dot_general(
        left, right, (((left_dim,), (right_dim,)), ((), ())), preferred_element_type=F32
    )


def copy_to(source, target, send_sem, recv_sem, device):
    return pltpu.make_async_remote_copy(
        src_ref=source,
        dst_ref=target,
        send_sem=send_sem,
        recv_sem=recv_sem,
        device_id=device,
        device_id_type=MESH,
    )


def kernel(
    n, n_dp, width, group_heads,
    hid, cot, picks, gain, router, wq, wkv, wo,
    mixed_out, igrad_out, kvgrad_out, rgrad_out,
    wquery, wout, wkeys, kv, kvt, scores, dprobs, qpad, opad, dkv, got_dkv, part, got_part,
    gkv, normed, slices, normed_t, share, pair, got_share, total, final, row_a, row_b, row_d,
    block, block_grad, block_out, dqkv, upstream,
    p1_send, p1_recv, ring_send, ring_recv, sib_send, sib_recv,
    x_send, x_recv, rs_send, rs_recv, d_send, d_recv, o_send, o_recv, t_send, t_recv,
):
    seq, dp = lax.axis_index("seq"), lax.axis_index("dp")
    core = lax.rem(dp, 2)
    y, z = lax.div(seq, n), lax.rem(seq, n)
    a = z + core * (y - z)
    b = y + core * (z - y)
    keys = n * SLOTS
    half_heads = group_heads * HEAD
    lanes = 2 * group_heads * SLOTS
    chips = n_dp // 2
    out_cols = width // n_dp
    chunk = keys

    def seq_of(b_, a_):
        return (1 - core) * (b_ * n + a_) + core * (a_ * n + b_)

    def peer_a(j):
        return (dp, seq_of(b, lax.rem(a + j, n)))

    def peer_b(j):
        return (dp, seq_of(lax.rem(b + j, n), a))

    def peer_y(j):
        return (dp, lax.rem(y + j, n) * n + z)

    def peer_z(j):
        return (dp, y * n + lax.rem(z + j, n))

    def peer_x(j):
        return (lax.rem(dp + 2 * j, n_dp), seq)

    def peer_d(j):
        return (lax.rem(dp + j, n_dp), seq)

    sibling = (dp + 1 - 2 * core, seq)

    def each(count, body):
        def step(j, carry):
            body(j)
            return carry

        lax.fori_loop(0, count, step, 0)

    def others(count, body):
        def step(j, carry):
            body(j)
            return carry

        lax.fori_loop(1, count, step, 0)

    barrier = pltpu.get_barrier_semaphore()

    def greet(device):
        pl.semaphore_signal(barrier, inc=1, device_id=device, device_id_type=MESH)

    others(n, lambda j: greet(peer_a(j)))
    others(n, lambda j: greet(peer_b(j)))
    others(n_dp, lambda j: greet(peer_d(j)))

    for side in (0, 1):

        @pl.when(core == side)
        def _():
            cols = slice(side * half_heads, (side + 1) * half_heads)
            wquery[side, y, z] = wq[:, cols]
            wkeys[side, y, z] = wkv[:, side * 128 : (side + 1) * 128]

    def cols_of(d):
        return pl.ds(pl.multiple_of(d * out_cols, out_cols), out_cols)

    wout[dp, y, z] = wo[:, cols_of(dp)]

    tokens = hid.shape[1]
    row_id = lax.broadcasted_iota(jnp.int32, (tokens, tokens), 0)
    col_id = lax.broadcasted_iota(jnp.int32, (tokens, tokens), 1)
    pick_row = picks[...].astype(F32)
    pick_wide = jnp.broadcast_to(pick_row, (tokens, tokens))
    pick_col = jnp.sum(jnp.where(row_id == col_id, pick_wide, 0.0), axis=1, keepdims=True)
    rank_col = jnp.sum(jnp.where(col_id < row_id, pick_wide, 0.0), axis=1, keepdims=True)
    pick_tall = jnp.broadcast_to(pick_col, (tokens, tokens))
    rank_row = jnp.sum(jnp.where(row_id < col_id, pick_tall, 0.0), axis=0, keepdims=True)
    slot_row = lax.broadcasted_iota(jnp.int32, (SLOTS, tokens), 0).astype(F32)
    slot_col = lax.broadcasted_iota(jnp.int32, (tokens, SLOTS), 1).astype(F32)
    pack = jnp.where((slot_row == rank_row) & (pick_row > 0.5), 1.0, 0.0)
    spread = jnp.where((slot_col == rank_col) & (pick_col > 0.5), 1.0, 0.0).astype(BF16)
    used = jnp.sum(pack, axis=1, keepdims=True)
    pack = pack.astype(BF16)

    n_chunks = width // chunk

    def at(i):
        return pl.ds(pl.multiple_of(i * chunk, chunk), chunk)

    def gate_step(i, acc):
        return acc + hid[0, :, at(i)].astype(F32) * router[:, at(i)]

    logit = lax.fori_loop(0, n_chunks, gate_step, jnp.zeros((tokens, chunk), F32))
    gate = jax.nn.sigmoid(jnp.sum(logit, axis=1, keepdims=True))

    pl.semaphore_wait(barrier, 2 * (n - 1) + n_dp - 1)

    outgoing = []

    def first(which, own):
        def make(j):
            return copy_to(own, own, p1_send.at[which, j], p1_recv.at[which, j], peer_a(j))

        return make

    def along(peer, which, source, target):
        def make(j):
            return copy_to(source(j), target, x_send.at[which, j], x_recv.at[which, j], peer(j))

        return make

    def along_d(which, ref):
        def make(j):
            return copy_to(
                ref.at[dp], ref.at[dp], d_send.at[which, j], d_recv.at[which, j], peer_d(j)
            )

        return make

    def start(make, count=n):
        others(count, lambda j: make(j).start())
        outgoing.append(lambda: sent(make, count))

    def arrived(make, count=n):
        others(count, lambda j: make(j).wait_recv())

    def sent(make, count=n):
        others(count, lambda j: make(j).wait_send())

    last = n // 2 - 1

    def slab(side, k, piece=None):
        size = n // PIECES
        rows = slice(None) if piece is None else pl.ds(piece * size, size)
        return wquery.at[0, k, rows] if side == 0 else wquery.at[1, rows, k]

    def goes(step, way, piece):
        return step < last or (piece < PIECES // 2) == (way == 0)

    def ring_copy(step, way, piece, rows, device):
        return copy_to(
            rows, rows, ring_send.at[step, way, piece], ring_recv.at[step, way, piece], device
        )

    def any_ring_copy(step, way, piece):
        return ring_copy(step, way, piece, slab(0, 0, piece), peer_b(1))

    def ring_start(step, piece):
        for side in (0, 1):

            @pl.when(core == side)
            def _():
                for way, block_id, device in (
                    (0, lax.rem(b + n - step, n), peer_b(1)),
                    (1, lax.rem(b + step, n), peer_b(n - 1)),
                ):
                    if goes(step, way, piece):
                        ring_copy(step, way, piece, slab(side, block_id, piece), device).start()

        for way in (0, 1):
            if goes(step, way, piece):
                outgoing.append(lambda way=way: any_ring_copy(step, way, piece).wait_send())

    def sib_copy(which, slot, rows):
        return copy_to(rows, rows, sib_send.at[which, slot], sib_recv.at[which, slot], sibling)

    def any_sib_copy(which, slot):
        return sib_copy(which, slot, (slab(0, 0), wout.at[0], wkeys.at[0, 0])[which])

    def sib_start(slot, block_id):
        for side in (0, 1):

            @pl.when(core == side)
            def _():
                sib_copy(0, slot, slab(side, block_id)).start()

        outgoing.append(lambda: any_sib_copy(0, slot).wait_send())

    def pass_on(step):
        for piece in range(PIECES):
            for way in (0, 1):
                if goes(step, way, piece):
                    any_ring_copy(step, way, piece).wait_recv()
            if step < last:
                ring_start(step + 1, piece)
        sib_start(1 + 2 * step, lax.rem(b + n - 1 - step, n))
        if step < last:
            sib_start(2 + 2 * step, lax.rem(b + 1 + step, n))

    out_first = first(1, wout.at[dp, y, z])

    def out_second(side, j):
        rows = wout.at[dp, b] if side == 0 else wout.at[dp, :, b]
        return copy_to(rows, rows, x_send.at[8, j], x_recv.at[8, j], peer_b(j))

    def out_second_start():
        for side in (0, 1):

            @pl.when(core == side)
            def _():
                others(n, lambda j: out_second(side, j).start())

        outgoing.append(lambda: others(n, lambda j: out_second(0, j).wait_send()))

    last_x = chips // 2 - 1

    def out_block(distance):
        return lax.rem(dp + 2 * n_dp + 2 * distance, n_dp)

    def out_copy(step, way):
        rows = wout.at[out_block((2 * way - 1) * step)]
        if step == last_x:
            rows = rows.at[pl.ds(way * (n // 2), n // 2)]
        device = peer_x(1 if way == 0 else chips - 1)
        return copy_to(rows, rows, o_send.at[step, way], o_recv.at[step, way], device)

    def out_start(step):
        for way in (0, 1):
            out_copy(step, way).start()
            outgoing.append(lambda way=way: out_copy(step, way).wait_send())

    def out_sib(slot, distance):
        sib_copy(1, slot, wout.at[out_block(distance)]).start()
        outgoing.append(lambda: any_sib_copy(1, slot).wait_send())

    def out_pass_on(step):
        for way in (0, 1):
            out_copy(step, way).wait_recv()
        if step < last_x:
            out_start(step + 1)
        out_sib(1 + 2 * step, -1 - step)
        if step < last_x:
            out_sib(2 + 2 * step, 1 + step)

    query_first = first(0, wquery.at[core, y, z])
    keys_first = first(2, wkeys.at[core, y, z])
    start(keys_first)
    start(out_first)
    start(query_first)

    def pack_step(i, acc):
        rows = dot(pack, hid[0, :, at(i)])
        block[:, at(i)] = rows
        scaled = (gate * cot[0, :, at(i)].astype(F32)).astype(BF16)
        block_grad[:, at(i)] = dot(pack, scaled).astype(BF16)
        return acc + rows * rows

    squares = lax.fori_loop(0, n_chunks, pack_step, jnp.zeros((SLOTS, chunk), F32))
    inv_norm = lax.rsqrt(jnp.sum(squares, axis=1, keepdims=True) * (1.0 / width) + EPSILON)

    def norm_step(i):
        normed[:, at(i)] = (block[:, at(i)] * inv_norm * gain[:, at(i)]).astype(BF16)

    each(n_chunks, norm_step)

    slices[y] = normed[:, at(y)]
    send_slices = along(peer_y, 5, lambda j: normed.at[:, at(lax.rem(y + j, n))], slices.at[y])

    def keys_slab(side, k):
        return wkeys.at[0, k] if side == 0 else wkeys.at[1, :, k]

    def keys_copy(side, block_id, j):
        rows = keys_slab(side, block_id)
        return copy_to(rows, rows, x_send.at[9, j], x_recv.at[9, j], peer_b(j))

    def nearest(t):
        after, odd = lax.div(t, 2), lax.rem(t, 2)
        return (1 - odd) * (1 + after) + odd * (n - 1 - after)

    def keys_sib(slot, block_id):
        for side in (0, 1):

            @pl.when(core == side)
            def _():
                sib_copy(2, slot, keys_slab(side, block_id)).start()

    def keys_arrived(t):
        j = nearest(t)
        keys_copy(0, 0, j).wait_recv()
        keys_sib(t + 1, lax.rem(b + n - j, n))

    arrived(keys_first)
    for side in (0, 1):

        @pl.when(core == side)
        def _():
            others(n, lambda j: keys_copy(side, b, j).start())

    outgoing.append(lambda: others(n, lambda j: keys_copy(0, 0, j).wait_send()))
    keys_sib(0, b)
    arrived(out_first)
    out_second_start()
    arrived(query_first)
    for piece in range(PIECES):
        ring_start(0, piece)
    sib_start(0, b)
    each(n - 1, keys_arrived)
    outgoing.append(lambda: each(n, lambda slot: any_sib_copy(2, slot).wait_send()))
    each(n, lambda slot: any_sib_copy(2, slot).wait_recv())

    def project(ref, side):
        def step(i, acc):
            return acc + dot(normed[:, at(i)], ref[side, i].reshape(chunk, -1))

        zero = jnp.zeros((SLOTS, ref.shape[-1]), F32)
        return lax.fori_loop(0, n_chunks, step, zero).astype(BF16)

    lane_id = lax.broadcasted_iota(jnp.int32, (SLOTS, 128), 1)
    own_keys = project(wkeys, 0).astype(F32)
    own_keys = jnp.where((lane_id == 0) & (used < 0.5), KEY_MARK, own_keys)
    kv[b, a, :, :128] = own_keys.astype(BF16)
    kv[b, a, :, 128:] = project(wkeys, 1)
    kv_first = along(peer_a, 0, lambda j: kv.at[b, a], kv.at[b, a])
    kv_second = along(peer_b, 1, lambda j: kv.at[b], kv.at[b])
    start(kv_first)
    start(send_slices)
    others(n, lambda j: out_second(0, j).wait_recv())
    if chips > 1:
        out_start(0)
    out_sib(0, 0)
    for step in (0, 1):
        if step <= last:
            pass_on(step)
    arrived(kv_first)
    start(kv_second)
    for step in range(2, last):
        pass_on(step)
    for step in range(last_x):
        out_pass_on(step)
    if last > 1:
        pass_on(last)
    for slot in range(n):
        any_sib_copy(0, slot).wait_recv()

    low_lane = lax.broadcasted_iota(jnp.int32, (SLOTS, 128), 1) < HEAD

    def pad_heads(ref, rows, group):
        for i in range(group_heads // 2):
            pair = rows[:, i * 128 : (i + 1) * 128]
            for parity in (0, 1):
                moved = pair if parity == group else pltpu.roll(pair, HEAD, 1)
                kept = jnp.where(low_lane, moved, 0.0) if group == 0 else jnp.where(low_lane, 0.0, moved)
                at_row = (group * group_heads + 2 * i + parity) * SLOTS
                ref[at_row : at_row + SLOTS, :] = kept.astype(BF16)

    def join_heads(both):
        tall = jnp.transpose(both)
        groups = []
        for group in (0, 1):
            pairs = []
            for i in range(group_heads // 2):
                at_row = (group * group_heads + 2 * i) * SLOTS
                even = tall[at_row : at_row + SLOTS, :]
                odd = tall[at_row + SLOTS : at_row + 2 * SLOTS, :]
                if group == 0:
                    pairs.append(jnp.where(low_lane, even, pltpu.roll(odd, HEAD, 1)))
                else:
                    pairs.append(jnp.where(low_lane, pltpu.roll(even, HEAD, 1), odd))
            groups.append(jnp.concatenate(pairs, axis=1))
        return groups

    for group in (0, 1):
        pad_heads(qpad, project(wquery, group).astype(F32), group)

    if chips > 1:
        out_pass_on(last_x)
    for slot in range(chips):
        any_sib_copy(1, slot).wait_recv()

    out_rows = n * wout.shape[3]

    def out_at(i):
        return pl.ds(pl.multiple_of(i * out_rows, out_rows), out_rows)

    def head_grad_step(i):
        acc = jnp.zeros((SLOTS, out_rows), F32)
        for d in range(n_dp):
            acc += dot(block_grad[:, cols_of(d)], wout[d, i].reshape(out_rows, out_cols), 1, 1)
        upstream[:, out_at(i)] = acc

    each(n, head_grad_step)
    for group in (0, 1):
        rows = upstream[:, group * half_heads : (group + 1) * half_heads]
        pad_heads(opad, rows, group)

    key_row = lax.broadcasted_iota(jnp.int32, (keys, 1), 0)
    query_at = seq * SLOTS + (lax.broadcasted_iota(jnp.int32, (1, lanes), 1) & (SLOTS - 1))
    scale = HEAD**-0.5

    def score_step(i, top):
        rows = kv[i].reshape(keys, 256).astype(F32)
        kvt[i] = jnp.transpose(rows).astype(BF16)
        key_at = seq_of(i, key_row >> 5) * SLOTS + (key_row & (SLOTS - 1))
        key_at = jnp.where(rows[:, 0:1] < KEY_BOUND, key_at, FAR)
        s = dot(rows[:, :128].astype(BF16), qpad[...], 1, 1) * scale
        s = jnp.where(key_at <= query_at, s, NEGATIVE)
        scores[i] = s
        return jnp.maximum(top, jnp.max(s, axis=0, keepdims=True))

    top = score_step(b, jnp.full((1, lanes), NEGATIVE, F32))

    def next_score_step(t, top):
        j = nearest(t)
        kv_second(j).wait_recv()
        return score_step(lax.rem(b + n - j, n), top)

    top = lax.fori_loop(0, n - 1, next_score_step, top)

    def exp_step(i, carry):
        total_exp, inner = carry
        e = jnp.exp(scores[i] - top)
        scores[i] = e
        grads = dot(kv[i].reshape(keys, 256)[:, 128:], opad[...], 1, 1)
        dprobs[i] = grads
        total_exp += jnp.sum(e, axis=0, keepdims=True)
        return total_exp, inner + jnp.sum(e * grads, axis=0, keepdims=True)

    zero = jnp.zeros((1, lanes), F32)
    total_exp, inner = lax.fori_loop(0, n, exp_step, (zero, zero))
    inv_sum = 1.0 / total_exp
    inner = inner * inv_sum

    def rs_slab(step, way):
        return lax.rem(b + n + (1 - 2 * way) * (n // 2 - step), n)

    half_keys = keys // 2

    def rs_copy(step, way, kind, piece):
        rows = pl.ds(piece * half_keys, half_keys)
        return copy_to(
            dkv.at[kind, rs_slab(step, way), rows],
            got_dkv.at[way, kind, step, rows],
            rs_send.at[way, kind, step, piece],
            rs_recv.at[way, kind, step, piece],
            peer_b(1 + way * (n - 2)),
        )

    def rs_start(step, way, kind, piece):
        rs_copy(step, way, kind, piece).start()
        outgoing.append(lambda: rs_copy(step, way, kind, piece).wait_send())

    def grad_step(t, carry):
        mixed_t, query_t = carry
        i = rs_slab(lax.div(t + 1, 2), 1 - lax.rem(t, 2))
        p = scores[i] * inv_sum
        half = p.astype(BF16)
        ds = (p * (dprobs[i] - inner)).astype(BF16)
        dkv[0, i] = dot(ds, qpad[...]) * scale
        dkv[1, i] = dot(half, opad[...])

        @pl.when(t == 0)
        def _():
            for way in (0, 1):
                for piece in (0, 1):
                    rs_copy(0, way, way, piece).start()

        return mixed_t + dot(kvt[i, 128:, :], half), query_t + dot(kvt[i, :128, :], ds)

    zero = jnp.zeros((128, lanes), F32)
    mixed_t, query_t = lax.fori_loop(0, n, grad_step, (zero, zero))
    for way in (0, 1):
        for piece in (0, 1):
            outgoing.append(
                lambda way=way, piece=piece: rs_copy(0, way, way, piece).wait_send()
            )

    def rs_step(step):
        for kind, piece, way in [(k, p, w) for k in (0, 1) for p in (0, 1) for w in (0, 1)]:
            if step > 1 or kind == way:
                rs_copy(step - 1, way, kind, piece).wait_recv()
                rows = slice(piece * half_keys, (piece + 1) * half_keys)
                dkv[kind, rs_slab(step, way), rows] += got_dkv[way, kind, step - 1, rows]
            rs_start(step, way, kind, piece)

    rs_step(1)

    heads = jnp.concatenate(join_heads(mixed_t), axis=1).astype(BF16)

    def out_step(d):
        rows = wout[d].reshape(n * out_rows, out_cols)
        block_out[:, cols_of(d)] = dot(heads, rows).astype(BF16)

    each(n_dp, out_step)
    if last > 1:
        rs_step(2)

    def mix_step(i, acc):
        out_tokens = dot(spread, block_out[:, at(i)])
        mixed_out[0, :, at(i)] = (hid[0, :, at(i)].astype(F32) + gate * out_tokens).astype(BF16)
        return acc + cot[0, :, at(i)].astype(F32) * out_tokens

    through = lax.fori_loop(0, n_chunks, mix_step, jnp.zeros((tokens, chunk), F32))
    through = jnp.sum(through, axis=1, keepdims=True)
    grad_logit = through * gate * (1.0 - gate)

    def router_step(i):
        term = hid[0, :, at(i)].astype(F32) * grad_logit
        row_a[a, :, at(i)] = jnp.sum(term, axis=0, keepdims=True)

    each(n_chunks, router_step)
    router_first = along(peer_a, 2, lambda j: row_a.at[a], row_a.at[a])
    router_second = along(peer_b, 3, lambda j: row_b.at[b], row_b.at[b])
    router_third = along_d(0, row_d)
    start(router_first)

    for group, rows in enumerate(join_heads(query_t * scale)):
        dqkv[group, :, :half_heads] = rows.astype(BF16)
    for step in range(3, last + 1):
        rs_step(step)
    arrived(send_slices)
    normed_t[...] = jnp.transpose(slices[...].reshape(keys, chunk).astype(F32)).astype(BF16)

    for kind in (0, 1):
        mine = dkv[kind, b]
        for way in (0, 1):
            for piece in (0, 1):
                rs_copy(last, way, kind, piece).wait_recv()
            mine += got_dkv[way, kind, last]
        part[:, :, kind * 128 : (kind + 1) * 128] = mine.reshape(n, SLOTS, 128)
    send_part = along(peer_a, 4, lambda j: part.at[lax.rem(a + j, n)], got_part.at[a])
    start(send_part)
    arrived(router_first)
    row_b[b] = jnp.sum(row_a[...], axis=0)
    start(router_second)
    arrived(send_part)
    own = part[a]
    own = lax.fori_loop(1, n, lambda j, acc: acc + got_part[lax.rem(a + j, n)], own)
    grad_kv = own.astype(BF16)
    gkv[y] = grad_kv
    gkv_gather = along(peer_y, 6, lambda j: gkv.at[y], gkv.at[y])
    start(gkv_gather)
    dqkv[0, :, half_heads:] = grad_kv[:, :128]
    dqkv[1, :, half_heads:] = grad_kv[:, 128:]

    def back_step(i, acc):
        grads = jnp.zeros((SLOTS, chunk), F32)
        for side in (0, 1):
            grads += dot(dqkv[side, :, :half_heads], wquery[side, i].reshape(chunk, -1), 1, 1)
            grads += dot(dqkv[side, :, half_heads:], wkeys[side, i].reshape(chunk, -1), 1, 1)
        u = grads * gain[:, at(i)]
        upstream[:, at(i)] = u
        return acc + u * block[:, at(i)]

    overlap = lax.fori_loop(0, n_chunks, back_step, jnp.zeros((SLOTS, chunk), F32))
    overlap = jnp.sum(overlap, axis=1, keepdims=True) * (1.0 / width)

    arrived(gkv_gather)
    share[...] = dot(normed_t[...], gkv[...].reshape(keys, 256)).reshape(n, SLOTS, 256)
    half = n // 2
    send_pair = copy_to(
        share.at[pl.ds((1 - core) * half, half)], pair, t_send.at[0], t_recv.at[0], sibling
    )
    send_pair.start()
    arrived(router_second)
    row_d[dp] = jnp.sum(row_b[...], axis=0)
    start(router_third, n_dp)

    cubed = inv_norm * inv_norm * inv_norm * overlap

    send_pair.wait()
    for i in range(half):
        share[core * half + i] += pair[i]

    def share_copy(i):
        to = core * half + i
        rows = share.at[to]
        return copy_to(rows, got_share.at[z], x_send.at[7, i], x_recv.at[7, z], (dp, y * n + to))

    def share_start(i):
        @pl.when(core * half + i != z)
        def _():
            share_copy(i).start()

    def share_sent(i):
        @pl.when(core * half + i != z)
        def _():
            share_copy(i).wait_send()

    each(half, share_start)
    outgoing.append(lambda: each(half, share_sent))

    def input_step(i):
        rows = inv_norm * upstream[:, at(i)] - block[:, at(i)] * cubed
        tokens_grad = dot(spread, rows.astype(BF16))
        grads = cot[0, :, at(i)].astype(F32) + grad_logit * router[:, at(i)] + tokens_grad
        igrad_out[0, :, at(i)] = grads.astype(BF16)

    each(n_chunks, input_step)

    def got_share_copy(j):
        source = lax.rem(z + j, n)
        return copy_to(
            share.at[0], got_share.at[source], x_send.at[7, 0], x_recv.at[7, source], sibling
        )

    x = lax.div(dp, 2)

    def total_copy(j):
        return copy_to(total.at[x], total.at[x], d_send.at[1, j], d_recv.at[1, j], peer_x(j))

    send_final = copy_to(final, final, t_send.at[1], t_recv.at[1], sibling)
    here = lax.div(z, half) == core

    @pl.when(here)
    def _():
        others(n, lambda j: got_share_copy(j).wait_recv())
        mine = share[z]
        total[x] = lax.fori_loop(1, n, lambda j, acc: acc + got_share[lax.rem(z + j, n)], mine)
        others(chips, lambda j: total_copy(j).start())

    arrived(router_third, n_dp)
    row = jnp.sum(row_d[...], axis=0)
    per_tile = 128 // SLOTS
    tile = jnp.zeros((1, SLOTS), F32)
    for i in range(width // SLOTS):
        tile = jnp.where(seq == i, row[:, i * SLOTS : (i + 1) * SLOTS], tile)
    rgrad_out[...] = tile

    @pl.when(here)
    def _():
        others(chips, lambda j: total_copy(j).wait_recv())
        final[...] = jnp.sum(total[...], axis=0)
        send_final.start()
        others(chips, lambda j: total_copy(j).wait_send())
        send_final.wait_send()

    @pl.when(jnp.logical_not(here))
    def _():
        send_final.wait_recv()

    kvgrad_out[...] = final[...]

    for wait in outgoing:
        wait()


def local(hidden, cotangent, picks, gain, router, w_query, w_kv, w_out):
    n_dp, n_seq = lax.axis_size("dp"), lax.axis_size("seq")
    n = math.isqrt(n_seq)
    tokens, width = hidden.shape[1:]
    half_heads = w_query.shape[1] // 2
    group_heads = half_heads // HEAD
    out_slab = w_out.shape[0]
    keys = n * SLOTS
    lanes = 2 * group_heads * SLOTS
    vmem = pl.BlockSpec(memory_space=pltpu.VMEM)
    dma = pltpu.SemaphoreType.DMA
    outs = pl.pallas_call(
        functools.partial(kernel, n, n_dp, width, group_heads),
        out_shape=(
            jax.ShapeDtypeStruct(hidden.shape, BF16),
            jax.ShapeDtypeStruct(hidden.shape, BF16),
            jax.ShapeDtypeStruct((SLOTS, 256), F32),
            jax.ShapeDtypeStruct((1, SLOTS), F32),
        ),
        in_specs=[vmem] * 8,
        out_specs=(vmem,) * 4,
        scratch_shapes=[
            pltpu.VMEM((2, n, n, SLOTS, half_heads), BF16),
            pltpu.VMEM((n_dp, n, n, out_slab, width // n_dp), BF16),
            pltpu.VMEM((2, n, n, SLOTS, 128), BF16),
            pltpu.VMEM((n, n, SLOTS, 256), BF16),
            pltpu.VMEM((n, 256, keys), BF16),
            pltpu.VMEM((n, keys, lanes), F32),
            pltpu.VMEM((n, keys, lanes), F32),
            pltpu.VMEM((lanes, 128), BF16),
            pltpu.VMEM((lanes, 128), BF16),
            pltpu.VMEM((2, n, keys, 128), F32),
            pltpu.VMEM((2, 2, n // 2, keys, 128), F32),
            pltpu.VMEM((n, SLOTS, 256), F32),
            pltpu.VMEM((n, SLOTS, 256), F32),
            pltpu.VMEM((n, SLOTS, 256), BF16),
            pltpu.VMEM((SLOTS, width), BF16),
            pltpu.VMEM((n, SLOTS, keys), BF16),
            pltpu.VMEM((keys, keys), BF16),
            pltpu.VMEM((n, SLOTS, 256), F32),
            pltpu.VMEM((n // 2, SLOTS, 256), F32),
            pltpu.VMEM((n, SLOTS, 256), F32),
            pltpu.VMEM((n_dp // 2, SLOTS, 256), F32),
            pltpu.VMEM((SLOTS, 256), F32),
            pltpu.VMEM((n, 1, width), F32),
            pltpu.VMEM((n, 1, width), F32),
            pltpu.VMEM((n_dp, 1, width), F32),
            pltpu.VMEM((SLOTS, width), F32),
            pltpu.VMEM((SLOTS, width), BF16),
            pltpu.VMEM((SLOTS, width), BF16),
            pltpu.VMEM((2, SLOTS, half_heads + 128), BF16),
            pltpu.VMEM((SLOTS, width), F32),
            dma((3, n)),
            dma((3, n)),
            dma((n // 2, 2, PIECES)),
            dma((n // 2, 2, PIECES)),
            dma((3, max(n, n_dp // 2))),
            dma((3, max(n, n_dp // 2))),
            dma((10, n)),
            dma((10, n)),
            dma((2, 2, n // 2, 2)),
            dma((2, 2, n // 2, 2)),
            dma((2, n_dp)),
            dma((2, n_dp)),
            dma((2, 2)),
            dma((2, 2)),
            dma((2,)),
            dma((2,)),
        ],
        compiler_params=pltpu.CompilerParams(
            collective_id=0, has_side_effects=True, vmem_limit_bytes=58 * 1024 * 1024
        ),
    )(
        hidden, cotangent, picks, gain.reshape(1, -1), router.reshape(1, -1), w_query, w_kv, w_out
    )
    mixed, input_grad, kv_grad, router_grad = outs
    return mixed, input_grad, kv_grad, router_grad.reshape(-1)


def solution(mesh):
    rows = P("dp", "seq", None)
    weight = P("seq", None)
    return jax.shard_map(
        local,
        mesh=mesh,
        in_specs=(rows, rows, P("dp", "seq"), P(), P(), weight, weight, weight),
        out_specs=(rows, rows, weight, P("seq")),
        check_vma=False,
    )
```

```python
import functools
import math

import jax
import jax.numpy as jnp
from jax import lax
from jax.experimental import pallas as pl
from jax.experimental.pallas import tpu as pltpu
from jax.sharding import PartitionSpec as P

MESH = pl.DeviceIdType.MESH
EPSILON = 1e-05
SLOTS = 32
HEAD = 64
F32, BF16 = jnp.float32, jnp.bfloat16
KEY_MARK = 2.0**100
KEY_BOUND = 2.0**64
NEGATIVE = -1e30
FAR = 1 << 30
PIECES = 4


def dot(left, right, left_dim=1, right_dim=0):
    return lax.dot_general(
        left, right, (((left_dim,), (right_dim,)), ((), ())), preferred_element_type=F32
    )


def copy_to(source, target, send_sem, recv_sem, device):
    return pltpu.make_async_remote_copy(
        src_ref=source,
        dst_ref=target,
        send_sem=send_sem,
        recv_sem=recv_sem,
        device_id=device,
        device_id_type=MESH,
    )


def kernel(
    n, n_dp, width, group_heads,
    hid, cot, picks, gain, router, wq, wkv, wo,
    mixed_out, igrad_out, kvgrad_out, rgrad_out,
    wquery, wout, wkeys, kv, kvt, scores, dprobs, qpad, opad, dkv, got_dkv, part, got_part,
    gkv, normed, slices, normed_t, share, pair, got_share, total, final, row_a, row_b, row_d,
    block, block_grad, block_out, dqkv, upstream,
    p1_send, p1_recv, ring_send, ring_recv, sib_send, sib_recv,
    x_send, x_recv, rs_send, rs_recv, d_send, d_recv, o_send, o_recv, t_send, t_recv,
):
    seq, dp = lax.axis_index("seq"), lax.axis_index("dp")
    core = lax.rem(dp, 2)
    y, z = lax.div(seq, n), lax.rem(seq, n)
    a = z + core * (y - z)
    b = y + core * (z - y)
    keys = n * SLOTS
    half_heads = group_heads * HEAD
    lanes = 2 * group_heads * SLOTS
    chips = n_dp // 2
    out_cols = width // n_dp
    chunk = keys

    def seq_of(b_, a_):
        return (1 - core) * (b_ * n + a_) + core * (a_ * n + b_)

    def peer_a(j):
        return (dp, seq_of(b, lax.rem(a + j, n)))

    def peer_b(j):
        return (dp, seq_of(lax.rem(b + j, n), a))

    def peer_y(j):
        return (dp, lax.rem(y + j, n) * n + z)

    def peer_z(j):
        return (dp, y * n + lax.rem(z + j, n))

    def peer_x(j):
        return (lax.rem(dp + 2 * j, n_dp), seq)

    def peer_d(j):
        return (lax.rem(dp + j, n_dp), seq)

    sibling = (dp + 1 - 2 * core, seq)

    def each(count, body):
        def step(j, carry):
            body(j)
            return carry

        lax.fori_loop(0, count, step, 0)

    def others(count, body):
        def step(j, carry):
            body(j)
            return carry

        lax.fori_loop(1, count, step, 0)

    barrier = pltpu.get_barrier_semaphore()

    def greet(device):
        pl.semaphore_signal(barrier, inc=1, device_id=device, device_id_type=MESH)

    others(n, lambda j: greet(peer_a(j)))
    others(n, lambda j: greet(peer_b(j)))
    others(n_dp, lambda j: greet(peer_d(j)))

    for side in (0, 1):

        @pl.when(core == side)
        def _():
            cols = slice(side * half_heads, (side + 1) * half_heads)
            wquery[side, y, z] = wq[:, cols]
            wkeys[side, y, z] = wkv[:, side * 128 : (side + 1) * 128]

    def cols_of(d):
        return pl.ds(pl.multiple_of(d * out_cols, out_cols), out_cols)

    wout[dp, y, z] = wo[:, cols_of(dp)]

    tokens = hid.shape[1]
    row_id = lax.broadcasted_iota(jnp.int32, (tokens, tokens), 0)
    col_id = lax.broadcasted_iota(jnp.int32, (tokens, tokens), 1)
    pick_row = picks[...].astype(F32)
    pick_wide = jnp.broadcast_to(pick_row, (tokens, tokens))
    pick_col = jnp.sum(jnp.where(row_id == col_id, pick_wide, 0.0), axis=1, keepdims=True)
    rank_col = jnp.sum(jnp.where(col_id < row_id, pick_wide, 0.0), axis=1, keepdims=True)
    pick_tall = jnp.broadcast_to(pick_col, (tokens, tokens))
    rank_row = jnp.sum(jnp.where(row_id < col_id, pick_tall, 0.0), axis=0, keepdims=True)
    slot_row = lax.broadcasted_iota(jnp.int32, (SLOTS, tokens), 0).astype(F32)
    slot_col = lax.broadcasted_iota(jnp.int32, (tokens, SLOTS), 1).astype(F32)
    pack = jnp.where((slot_row == rank_row) & (pick_row > 0.5), 1.0, 0.0)
    spread = jnp.where((slot_col == rank_col) & (pick_col > 0.5), 1.0, 0.0).astype(BF16)
    used = jnp.sum(pack, axis=1, keepdims=True)
    pack = pack.astype(BF16)

    n_chunks = width // chunk

    def at(i):
        return pl.ds(pl.multiple_of(i * chunk, chunk), chunk)

    def gate_step(i, acc):
        return acc + hid[0, :, at(i)].astype(F32) * router[:, at(i)]

    logit = lax.fori_loop(0, n_chunks, gate_step, jnp.zeros((tokens, chunk), F32))
    gate = jax.nn.sigmoid(jnp.sum(logit, axis=1, keepdims=True))

    pl.semaphore_wait(barrier, 2 * (n - 1) + n_dp - 1)

    outgoing = []

    def first(which, own):
        def make(j):
            return copy_to(own, own, p1_send.at[which, j], p1_recv.at[which, j], peer_a(j))

        return make

    def along(peer, which, source, target):
        def make(j):
            return copy_to(source(j), target, x_send.at[which, j], x_recv.at[which, j], peer(j))

        return make

    def along_d(which, ref):
        def make(j):
            return copy_to(
                ref.at[dp], ref.at[dp], d_send.at[which, j], d_recv.at[which, j], peer_d(j)
            )

        return make

    def start(make, count=n):
        others(count, lambda j: make(j).start())
        outgoing.append(lambda: sent(make, count))

    def arrived(make, count=n):
        others(count, lambda j: make(j).wait_recv())

    def sent(make, count=n):
        others(count, lambda j: make(j).wait_send())

    last = n // 2 - 1

    def slab(side, k, piece=None):
        size = n // PIECES
        rows = slice(None) if piece is None else pl.ds(piece * size, size)
        return wquery.at[0, k, rows] if side == 0 else wquery.at[1, rows, k]

    def goes(step, way, piece):
        return step < last or (piece < PIECES // 2) == (way == 0)

    def ring_copy(step, way, piece, rows, device):
        return copy_to(
            rows, rows, ring_send.at[step, way, piece], ring_recv.at[step, way, piece], device
        )

    def any_ring_copy(step, way, piece):
        return ring_copy(step, way, piece, slab(0, 0, piece), peer_b(1))

    def ring_start(step, piece):
        for side in (0, 1):

            @pl.when(core == side)
            def _():
                for way, block_id, device in (
                    (0, lax.rem(b + n - step, n), peer_b(1)),
                    (1, lax.rem(b + step, n), peer_b(n - 1)),
                ):
                    if goes(step, way, piece):
                        ring_copy(step, way, piece, slab(side, block_id, piece), device).start()

        for way in (0, 1):
            if goes(step, way, piece):
                outgoing.append(lambda way=way: any_ring_copy(step, way, piece).wait_send())

    def sib_copy(which, slot, rows):
        return copy_to(rows, rows, sib_send.at[which, slot], sib_recv.at[which, slot], sibling)

    def any_sib_copy(which, slot):
        return sib_copy(which, slot, (slab(0, 0), wout.at[0], wkeys.at[0, 0])[which])

    def sib_start(slot, block_id):
        for side in (0, 1):

            @pl.when(core == side)
            def _():
                sib_copy(0, slot, slab(side, block_id)).start()

        outgoing.append(lambda: any_sib_copy(0, slot).wait_send())

    def pass_on(step):
        for piece in range(PIECES):
            for way in (0, 1):
                if goes(step, way, piece):
                    any_ring_copy(step, way, piece).wait_recv()
            if step < last:
                ring_start(step + 1, piece)
        sib_start(1 + 2 * step, lax.rem(b + n - 1 - step, n))
        if step < last:
            sib_start(2 + 2 * step, lax.rem(b + 1 + step, n))

    out_first = first(1, wout.at[dp, y, z])

    def out_second(side, j):
        rows = wout.at[dp, b] if side == 0 else wout.at[dp, :, b]
        return copy_to(rows, rows, x_send.at[8, j], x_recv.at[8, j], peer_b(j))

    def out_second_start():
        for side in (0, 1):

            @pl.when(core == side)
            def _():
                others(n, lambda j: out_second(side, j).start())

        outgoing.append(lambda: others(n, lambda j: out_second(0, j).wait_send()))

    last_x = chips // 2 - 1

    def out_block(distance):
        return lax.rem(dp + 2 * n_dp + 2 * distance, n_dp)

    def out_copy(step, way):
        rows = wout.at[out_block((2 * way - 1) * step)]
        if step == last_x:
            rows = rows.at[pl.ds(way * (n // 2), n // 2)]
        device = peer_x(1 if way == 0 else chips - 1)
        return copy_to(rows, rows, o_send.at[step, way], o_recv.at[step, way], device)

    def out_start(step):
        for way in (0, 1):
            out_copy(step, way).start()
            outgoing.append(lambda way=way: out_copy(step, way).wait_send())

    def out_sib(slot, distance):
        sib_copy(1, slot, wout.at[out_block(distance)]).start()
        outgoing.append(lambda: any_sib_copy(1, slot).wait_send())

    def out_pass_on(step):
        for way in (0, 1):
            out_copy(step, way).wait_recv()
        if step < last_x:
            out_start(step + 1)
        out_sib(1 + 2 * step, -1 - step)
        if step < last_x:
            out_sib(2 + 2 * step, 1 + step)

    query_first = first(0, wquery.at[core, y, z])
    keys_first = first(2, wkeys.at[core, y, z])
    start(keys_first)
    start(out_first)
    start(query_first)

    def pack_step(i, acc):
        rows = dot(pack, hid[0, :, at(i)])
        block[:, at(i)] = rows
        scaled = (gate * cot[0, :, at(i)].astype(F32)).astype(BF16)
        block_grad[:, at(i)] = dot(pack, scaled).astype(BF16)
        return acc + rows * rows

    squares = lax.fori_loop(0, n_chunks, pack_step, jnp.zeros((SLOTS, chunk), F32))
    inv_norm = lax.rsqrt(jnp.sum(squares, axis=1, keepdims=True) * (1.0 / width) + EPSILON)

    def norm_step(i):
        normed[:, at(i)] = (block[:, at(i)] * inv_norm * gain[:, at(i)]).astype(BF16)

    each(n_chunks, norm_step)

    slices[y] = normed[:, at(y)]
    send_slices = along(peer_y, 5, lambda j: normed.at[:, at(lax.rem(y + j, n))], slices.at[y])

    def keys_slab(side, k):
        return wkeys.at[0, k] if side == 0 else wkeys.at[1, :, k]

    def keys_copy(side, block_id, j):
        rows = keys_slab(side, block_id)
        return copy_to(rows, rows, x_send.at[9, j], x_recv.at[9, j], peer_b(j))

    def nearest(t):
        after, odd = lax.div(t, 2), lax.rem(t, 2)
        return (1 - odd) * (1 + after) + odd * (n - 1 - after)

    def keys_sib(slot, block_id):
        for side in (0, 1):

            @pl.when(core == side)
            def _():
                sib_copy(2, slot, keys_slab(side, block_id)).start()

    def keys_arrived(t):
        j = nearest(t)
        keys_copy(0, 0, j).wait_recv()
        keys_sib(t + 1, lax.rem(b + n - j, n))

    arrived(keys_first)
    for side in (0, 1):

        @pl.when(core == side)
        def _():
            others(n, lambda j: keys_copy(side, b, j).start())

    outgoing.append(lambda: others(n, lambda j: keys_copy(0, 0, j).wait_send()))
    keys_sib(0, b)
    arrived(out_first)
    out_second_start()
    arrived(query_first)
    for piece in range(PIECES):
        ring_start(0, piece)
    sib_start(0, b)
    each(n - 1, keys_arrived)
    outgoing.append(lambda: each(n, lambda slot: any_sib_copy(2, slot).wait_send()))
    each(n, lambda slot: any_sib_copy(2, slot).wait_recv())

    def project(ref, side):
        def step(i, acc):
            return acc + dot(normed[:, at(i)], ref[side, i].reshape(chunk, -1))

        zero = jnp.zeros((SLOTS, ref.shape[-1]), F32)
        return lax.fori_loop(0, n_chunks, step, zero).astype(BF16)

    lane_id = lax.broadcasted_iota(jnp.int32, (SLOTS, 128), 1)
    own_keys = project(wkeys, 0).astype(F32)
    own_keys = jnp.where((lane_id == 0) & (used < 0.5), KEY_MARK, own_keys)
    kv[b, a, :, :128] = own_keys.astype(BF16)
    kv[b, a, :, 128:] = project(wkeys, 1)
    kv_first = along(peer_a, 0, lambda j: kv.at[b, a], kv.at[b, a])
    kv_second = along(peer_b, 1, lambda j: kv.at[b], kv.at[b])
    start(kv_first)
    start(send_slices)
    others(n, lambda j: out_second(0, j).wait_recv())
    if chips > 1:
        out_start(0)
    out_sib(0, 0)
    for step in (0, 1):
        if step <= last:
            pass_on(step)
    arrived(kv_first)
    start(kv_second)
    for step in range(2, last):
        pass_on(step)
    for step in range(last_x):
        out_pass_on(step)
    if last > 1:
        pass_on(last)
    for slot in range(n):
        any_sib_copy(0, slot).wait_recv()

    low_lane = lax.broadcasted_iota(jnp.int32, (SLOTS, 128), 1) < HEAD

    def pad_heads(ref, rows, group):
        for i in range(group_heads // 2):
            pair = rows[:, i * 128 : (i + 1) * 128]
            for parity in (0, 1):
                moved = pair if parity == group else pltpu.roll(pair, HEAD, 1)
                kept = jnp.where(low_lane, moved, 0.0) if group == 0 else jnp.where(low_lane, 0.0, moved)
                at_row = (group * group_heads + 2 * i + parity) * SLOTS
                ref[at_row : at_row + SLOTS, :] = kept.astype(BF16)

    def join_heads(both):
        tall = jnp.transpose(both)
        groups = []
        for group in (0, 1):
            pairs = []
            for i in range(group_heads // 2):
                at_row = (group * group_heads + 2 * i) * SLOTS
                even = tall[at_row : at_row + SLOTS, :]
                odd = tall[at_row + SLOTS : at_row + 2 * SLOTS, :]
                if group == 0:
                    pairs.append(jnp.where(low_lane, even, pltpu.roll(odd, HEAD, 1)))
                else:
                    pairs.append(jnp.where(low_lane, pltpu.roll(even, HEAD, 1), odd))
            groups.append(jnp.concatenate(pairs, axis=1))
        return groups

    for group in (0, 1):
        pad_heads(qpad, project(wquery, group).astype(F32), group)

    key_row = lax.broadcasted_iota(jnp.int32, (keys, 1), 0)
    query_at = seq * SLOTS + (lax.broadcasted_iota(jnp.int32, (1, lanes), 1) & (SLOTS - 1))
    scale = HEAD**-0.5

    def score_step(i, top):
        rows = kv[i].reshape(keys, 256).astype(F32)
        kvt[i] = jnp.transpose(rows).astype(BF16)
        key_at = seq_of(i, key_row >> 5) * SLOTS + (key_row & (SLOTS - 1))
        key_at = jnp.where(rows[:, 0:1] < KEY_BOUND, key_at, FAR)
        s = dot(rows[:, :128].astype(BF16), qpad[...], 1, 1) * scale
        s = jnp.where(key_at <= query_at, s, NEGATIVE)
        scores[i] = s
        return jnp.maximum(top, jnp.max(s, axis=0, keepdims=True))

    top = score_step(b, jnp.full((1, lanes), NEGATIVE, F32))

    def next_score_step(t, top):
        j = nearest(t)
        kv_second(j).wait_recv()
        return score_step(lax.rem(b + n - j, n), top)

    top = lax.fori_loop(0, n // 2, next_score_step, top)
    if chips > 1:
        out_pass_on(last_x)
    for slot in range(chips):
        any_sib_copy(1, slot).wait_recv()

    out_rows = n * wout.shape[3]

    def out_at(i):
        return pl.ds(pl.multiple_of(i * out_rows, out_rows), out_rows)

    def head_grad_step(i):
        acc = jnp.zeros((SLOTS, out_rows), F32)
        for d in range(n_dp):
            acc += dot(block_grad[:, cols_of(d)], wout[d, i].reshape(out_rows, out_cols), 1, 1)
        upstream[:, out_at(i)] = acc

    each(n, head_grad_step)
    for group in (0, 1):
        rows = upstream[:, group * half_heads : (group + 1) * half_heads]
        pad_heads(opad, rows, group)

    top = lax.fori_loop(n // 2, n - 1, next_score_step, top)

    def exp_step(i, carry):
        total_exp, inner = carry
        e = jnp.exp(scores[i] - top)
        scores[i] = e
        grads = dot(kv[i].reshape(keys, 256)[:, 128:], opad[...], 1, 1)
        dprobs[i] = grads
        total_exp += jnp.sum(e, axis=0, keepdims=True)
        return total_exp, inner + jnp.sum(e * grads, axis=0, keepdims=True)

    zero = jnp.zeros((1, lanes), F32)
    total_exp, inner = lax.fori_loop(0, n, exp_step, (zero, zero))
    inv_sum = 1.0 / total_exp
    inner = inner * inv_sum

    def rs_slab(step, way):
        return lax.rem(b + n + (1 - 2 * way) * (n // 2 - step), n)

    half_keys = keys // 2

    def rs_copy(step, way, kind, piece):
        rows = pl.ds(piece * half_keys, half_keys)
        return copy_to(
            dkv.at[kind, rs_slab(step, way), rows],
            got_dkv.at[way, kind, step, rows],
            rs_send.at[way, kind, step, piece],
            rs_recv.at[way, kind, step, piece],
            peer_b(1 + way * (n - 2)),
        )

    def rs_start(step, way, kind, piece):
        rs_copy(step, way, kind, piece).start()
        outgoing.append(lambda: rs_copy(step, way, kind, piece).wait_send())

    def grad_step(t, carry):
        mixed_t, query_t = carry
        i = rs_slab(lax.div(t + 1, 2), 1 - lax.rem(t, 2))
        p = scores[i] * inv_sum
        half = p.astype(BF16)
        ds = (p * (dprobs[i] - inner)).astype(BF16)
        dkv[0, i] = dot(ds, qpad[...]) * scale
        dkv[1, i] = dot(half, opad[...])

        @pl.when(t == 0)
        def _():
            for way in (0, 1):
                for piece in (0, 1):
                    rs_copy(0, way, way, piece).start()

        return mixed_t + dot(kvt[i, 128:, :], half), query_t + dot(kvt[i, :128, :], ds)

    zero = jnp.zeros((128, lanes), F32)
    mixed_t, query_t = lax.fori_loop(0, n, grad_step, (zero, zero))
    for way in (0, 1):
        for piece in (0, 1):
            outgoing.append(
                lambda way=way, piece=piece: rs_copy(0, way, way, piece).wait_send()
            )

    def rs_step(step):
        for kind, piece, way in [(k, p, w) for k in (0, 1) for p in (0, 1) for w in (0, 1)]:
            if step > 1 or kind == way:
                rs_copy(step - 1, way, kind, piece).wait_recv()
                rows = slice(piece * half_keys, (piece + 1) * half_keys)
                dkv[kind, rs_slab(step, way), rows] += got_dkv[way, kind, step - 1, rows]
            rs_start(step, way, kind, piece)

    rs_step(1)

    heads = jnp.concatenate(join_heads(mixed_t), axis=1).astype(BF16)

    def out_step(d):
        rows = wout[d].reshape(n * out_rows, out_cols)
        block_out[:, cols_of(d)] = dot(heads, rows).astype(BF16)

    each(n_dp, out_step)
    if last > 1:
        rs_step(2)

    def mix_step(i, acc):
        out_tokens = dot(spread, block_out[:, at(i)])
        mixed_out[0, :, at(i)] = (hid[0, :, at(i)].astype(F32) + gate * out_tokens).astype(BF16)
        return acc + cot[0, :, at(i)].astype(F32) * out_tokens

    through = lax.fori_loop(0, n_chunks, mix_step, jnp.zeros((tokens, chunk), F32))
    through = jnp.sum(through, axis=1, keepdims=True)
    grad_logit = through * gate * (1.0 - gate)

    def router_step(i):
        term = hid[0, :, at(i)].astype(F32) * grad_logit
        row_a[a, :, at(i)] = jnp.sum(term, axis=0, keepdims=True)

    each(n_chunks, router_step)
    router_first = along(peer_a, 2, lambda j: row_a.at[a], row_a.at[a])
    router_second = along(peer_b, 3, lambda j: row_b.at[b], row_b.at[b])
    router_third = along_d(0, row_d)
    start(router_first)

    for group, rows in enumerate(join_heads(query_t * scale)):
        dqkv[group, :, :half_heads] = rows.astype(BF16)
    for step in range(3, last + 1):
        rs_step(step)
    arrived(send_slices)
    normed_t[...] = jnp.transpose(slices[...].reshape(keys, chunk).astype(F32)).astype(BF16)

    for kind in (0, 1):
        mine = dkv[kind, b]
        for way in (0, 1):
            for piece in (0, 1):
                rs_copy(last, way, kind, piece).wait_recv()
            mine += got_dkv[way, kind, last]
        part[:, :, kind * 128 : (kind + 1) * 128] = mine.reshape(n, SLOTS, 128)
    send_part = along(peer_a, 4, lambda j: part.at[lax.rem(a + j, n)], got_part.at[a])
    start(send_part)
    arrived(router_first)
    row_b[b] = jnp.sum(row_a[...], axis=0)
    start(router_second)
    arrived(send_part)
    own = part[a]
    own = lax.fori_loop(1, n, lambda j, acc: acc + got_part[lax.rem(a + j, n)], own)
    grad_kv = own.astype(BF16)
    gkv[y] = grad_kv
    gkv_gather = along(peer_y, 6, lambda j: gkv.at[y], gkv.at[y])
    start(gkv_gather)
    dqkv[0, :, half_heads:] = grad_kv[:, :128]
    dqkv[1, :, half_heads:] = grad_kv[:, 128:]

    def back_step(i, acc):
        grads = jnp.zeros((SLOTS, chunk), F32)
        for side in (0, 1):
            grads += dot(dqkv[side, :, :half_heads], wquery[side, i].reshape(chunk, -1), 1, 1)
            grads += dot(dqkv[side, :, half_heads:], wkeys[side, i].reshape(chunk, -1), 1, 1)
        u = grads * gain[:, at(i)]
        upstream[:, at(i)] = u
        return acc + u * block[:, at(i)]

    overlap = lax.fori_loop(0, n_chunks, back_step, jnp.zeros((SLOTS, chunk), F32))
    overlap = jnp.sum(overlap, axis=1, keepdims=True) * (1.0 / width)

    arrived(gkv_gather)
    share[...] = dot(normed_t[...], gkv[...].reshape(keys, 256)).reshape(n, SLOTS, 256)
    half = n // 2
    send_pair = copy_to(
        share.at[pl.ds((1 - core) * half, half)], pair, t_send.at[0], t_recv.at[0], sibling
    )
    send_pair.start()
    arrived(router_second)
    row_d[dp] = jnp.sum(row_b[...], axis=0)
    start(router_third, n_dp)

    cubed = inv_norm * inv_norm * inv_norm * overlap

    send_pair.wait()
    for i in range(half):
        share[core * half + i] += pair[i]

    def share_copy(i):
        to = core * half + i
        rows = share.at[to]
        return copy_to(rows, got_share.at[z], x_send.at[7, i], x_recv.at[7, z], (dp, y * n + to))

    def share_start(i):
        @pl.when(core * half + i != z)
        def _():
            share_copy(i).start()

    def share_sent(i):
        @pl.when(core * half + i != z)
        def _():
            share_copy(i).wait_send()

    each(half, share_start)
    outgoing.append(lambda: each(half, share_sent))

    def input_step(i):
        rows = inv_norm * upstream[:, at(i)] - block[:, at(i)] * cubed
        tokens_grad = dot(spread, rows.astype(BF16))
        grads = cot[0, :, at(i)].astype(F32) + grad_logit * router[:, at(i)] + tokens_grad
        igrad_out[0, :, at(i)] = grads.astype(BF16)

    each(n_chunks, input_step)

    def got_share_copy(j):
        source = lax.rem(z + j, n)
        return copy_to(
            share.at[0], got_share.at[source], x_send.at[7, 0], x_recv.at[7, source], sibling
        )

    x = lax.div(dp, 2)

    def total_copy(j):
        return copy_to(total.at[x], total.at[x], d_send.at[1, j], d_recv.at[1, j], peer_x(j))

    send_final = copy_to(final, final, t_send.at[1], t_recv.at[1], sibling)
    here = lax.div(z, half) == core

    @pl.when(here)
    def _():
        others(n, lambda j: got_share_copy(j).wait_recv())
        mine = share[z]
        total[x] = lax.fori_loop(1, n, lambda j, acc: acc + got_share[lax.rem(z + j, n)], mine)
        others(chips, lambda j: total_copy(j).start())

    arrived(router_third, n_dp)
    row = jnp.sum(row_d[...], axis=0)
    per_tile = 128 // SLOTS
    tile = jnp.zeros((1, SLOTS), F32)
    for i in range(width // SLOTS):
        tile = jnp.where(seq == i, row[:, i * SLOTS : (i + 1) * SLOTS], tile)
    rgrad_out[...] = tile

    @pl.when(here)
    def _():
        others(chips, lambda j: total_copy(j).wait_recv())
        final[...] = jnp.sum(total[...], axis=0)
        send_final.start()
        others(chips, lambda j: total_copy(j).wait_send())
        send_final.wait_send()

    @pl.when(jnp.logical_not(here))
    def _():
        send_final.wait_recv()

    kvgrad_out[...] = final[...]

    for wait in outgoing:
        wait()


def local(hidden, cotangent, picks, gain, router, w_query, w_kv, w_out):
    n_dp, n_seq = lax.axis_size("dp"), lax.axis_size("seq")
    n = math.isqrt(n_seq)
    tokens, width = hidden.shape[1:]
    half_heads = w_query.shape[1] // 2
    group_heads = half_heads // HEAD
    out_slab = w_out.shape[0]
    keys = n * SLOTS
    lanes = 2 * group_heads * SLOTS
    vmem = pl.BlockSpec(memory_space=pltpu.VMEM)
    dma = pltpu.SemaphoreType.DMA
    outs = pl.pallas_call(
        functools.partial(kernel, n, n_dp, width, group_heads),
        out_shape=(
            jax.ShapeDtypeStruct(hidden.shape, BF16),
            jax.ShapeDtypeStruct(hidden.shape, BF16),
            jax.ShapeDtypeStruct((SLOTS, 256), F32),
            jax.ShapeDtypeStruct((1, SLOTS), F32),
        ),
        in_specs=[vmem] * 8,
        out_specs=(vmem,) * 4,
        scratch_shapes=[
            pltpu.VMEM((2, n, n, SLOTS, half_heads), BF16),
            pltpu.VMEM((n_dp, n, n, out_slab, width // n_dp), BF16),
            pltpu.VMEM((2, n, n, SLOTS, 128), BF16),
            pltpu.VMEM((n, n, SLOTS, 256), BF16),
            pltpu.VMEM((n, 256, keys), BF16),
            pltpu.VMEM((n, keys, lanes), F32),
            pltpu.VMEM((n, keys, lanes), F32),
            pltpu.VMEM((lanes, 128), BF16),
            pltpu.VMEM((lanes, 128), BF16),
            pltpu.VMEM((2, n, keys, 128), F32),
            pltpu.VMEM((2, 2, n // 2, keys, 128), F32),
            pltpu.VMEM((n, SLOTS, 256), F32),
            pltpu.VMEM((n, SLOTS, 256), F32),
            pltpu.VMEM((n, SLOTS, 256), BF16),
            pltpu.VMEM((SLOTS, width), BF16),
            pltpu.VMEM((n, SLOTS, keys), BF16),
            pltpu.VMEM((keys, keys), BF16),
            pltpu.VMEM((n, SLOTS, 256), F32),
            pltpu.VMEM((n // 2, SLOTS, 256), F32),
            pltpu.VMEM((n, SLOTS, 256), F32),
            pltpu.VMEM((n_dp // 2, SLOTS, 256), F32),
            pltpu.VMEM((SLOTS, 256), F32),
            pltpu.VMEM((n, 1, width), F32),
            pltpu.VMEM((n, 1, width), F32),
            pltpu.VMEM((n_dp, 1, width), F32),
            pltpu.VMEM((SLOTS, width), F32),
            pltpu.VMEM((SLOTS, width), BF16),
            pltpu.VMEM((SLOTS, width), BF16),
            pltpu.VMEM((2, SLOTS, half_heads + 128), BF16),
            pltpu.VMEM((SLOTS, width), F32),
            dma((3, n)),
            dma((3, n)),
            dma((n // 2, 2, PIECES)),
            dma((n // 2, 2, PIECES)),
            dma((3, max(n, n_dp // 2))),
            dma((3, max(n, n_dp // 2))),
            dma((10, n)),
            dma((10, n)),
            dma((2, 2, n // 2, 2)),
            dma((2, 2, n // 2, 2)),
            dma((2, n_dp)),
            dma((2, n_dp)),
            dma((2, 2)),
            dma((2, 2)),
            dma((2,)),
            dma((2,)),
        ],
        compiler_params=pltpu.CompilerParams(
            collective_id=0, has_side_effects=True, vmem_limit_bytes=58 * 1024 * 1024
        ),
    )(
        hidden, cotangent, picks, gain.reshape(1, -1), router.reshape(1, -1), w_query, w_kv, w_out
    )
    mixed, input_grad, kv_grad, router_grad = outs
    return mixed, input_grad, kv_grad, router_grad.reshape(-1)


def solution(mesh):
    rows = P("dp", "seq", None)
    weight = P("seq", None)
    return jax.shard_map(
        local,
        mesh=mesh,
        in_specs=(rows, rows, P("dp", "seq"), P(), P(), weight, weight, weight),
        out_specs=(rows, rows, weight, P("seq")),
        check_vma=False,
    )
```
